32 devices in a mesh: dp: 8 (over z, y), head: 4 (over x, core).
Axes of the slice: x: 2, y: 2, z: 4, core: 2. Of those that a mesh axis runs over, the one named last changes fastest.
Arguments:
- tokens: bfloat16 [192, 136, 768], P(('dp', 'head')), may hold values from -6 to 6
- cotangent: bfloat16 [192, 136, 768], P(('dp', 'head')), may hold values from -6 to 6
- ratios: int32 [192], P('dp'), may hold values from 40 to 90, as said below
- patch_index: int32 [192, 136], P('dp'), may hold values from 0 to 224, as said below
- encoder_gains: float32 [2, 2, 768], replicated, may hold values from 0.25 to 1.75
- encoder_attend_in: bfloat16 [2, 768, 3, 768], P(None, None, None, 'head'), may hold values from -0.21875 to 0.21875
- encoder_attend_out: bfloat16 [2, 768, 768], P(None, 'head'), may hold values from -0.625 to 0.625
- encoder_expand: bfloat16 [2, 768, 3072], P(None, None, 'head'), may hold values from -0.21875 to 0.21875
- encoder_reduce: bfloat16 [2, 3072, 768], P(None, 'head'), may hold values from -0.109375 to 0.109375
- uniting_gains: float32 [3, 768], replicated, may hold values from 0.25 to 1.75
- uniting_query: bfloat16 [768, 768], P(None, 'head'), may hold values from -0.21875 to 0.21875
- uniting_pair: bfloat16 [768, 2, 768], P(None, None, 'head'), may hold values from -0.21875 to 0.21875
- uniting_attend_out: bfloat16 [768, 768], P('head'), may hold values from -0.625 to 0.625
- uniting_expand: bfloat16 [768, 3072], P(None, 'head'), may hold values from -0.21875 to 0.21875
- uniting_reduce: bfloat16 [3072, 768], P('head'), may hold values from -0.109375 to 0.109375
Outputs:
- layer_output: bfloat16 [192, 136, 768], P(('dp', 'head'))
- tokens_delta: float32 [192, 136, 768], P(('dp', 'head'))
- encoder_gains_delta: float32 [2, 2, 768], replicated
- encoder_attend_in_delta: float32 [2, 768, 3, 768], P(None, None, None, 'head')
- encoder_attend_out_delta: float32 [2, 768, 768], P(None, 'head')
- encoder_expand_delta: float32 [2, 768, 3072], P(None, None, 'head')
- encoder_reduce_delta: float32 [2, 3072, 768], P(None, 'head')
- uniting_gains_delta: float32 [3, 768], replicated
- uniting_query_delta: float32 [768, 768], P(None, 'head')
- uniting_pair_delta: float32 [768, 2, 768], P(None, None, 'head')
- uniting_attend_out_delta: float32 [768, 768], P('head')
- uniting_expand_delta: float32 [768, 3072], P(None, 'head')
- uniting_reduce_delta: float32 [3072, 768], P('head')
The draws below stay inside these ranges and needn't reach their ends.
Inputs may be any that keep to these rules, and one draw needn't show every extreme that they name: `ratios`: image i and image i + 96 (its radar partner) have the same ratio; some image has 40 and some 90 in every draw. `patch_index`: patch numbers are distinct within an image and equal for an image and its partner 96 later; only the first 225 * (100 - ratio) // 100 slots of an image are visible, the others are ignored.
All inputs are finite; a program needn't handle non-finite values.
Results may differ from the reference program's by a relative error of at most 0.035.
Values may be sent and summed in bfloat16 or wider, within the bound.
No kernel may reach another device: no remote copies, remote signals or barrier semaphores. Data moves between devices by JAX's collectives and lax.ppermute only.
A program may use at most 320 MiB of HBM per device.

```python
import jax
import jax.numpy as jnp
from jax import lax

D = 768
HEADS = 12
HEAD_DIM = 64
FF = 3072
GRID = 15
PATCHES = 225
SLOTS = 136
IMG_DEV = 24
IMAGES = 96


def draw_ratios(key, part):
    key = jax.random.fold_in(key, 3)
    first_key, second_key = jax.random.split(key)
    drawn = jax.random.randint(first_key, (IMAGES,), 40, 91)
    anchor = jax.random.randint(second_key, (), 0, IMAGES)
    drawn = drawn.at[anchor].set(40)
    drawn = drawn.at[(anchor + 1) % IMAGES].set(90)
    return jnp.concatenate([drawn, drawn]).astype(jnp.int32)


def draw_patch_index(key, part):
    key = jax.random.fold_in(key, 5)
    image_keys = jax.random.split(key, IMAGES)

    def one_image(image_key):
        return jax.random.permutation(image_key, PATCHES)[:SLOTS]
    chosen = jax.vmap(one_image)(image_keys)
    return jnp.concatenate([chosen, chosen]).astype(jnp.int32)


def level_of(rng, extent, pieces, least, top_value):
    level, own = 1.0, jax.random.fold_in(rng, 6)
    for dim, blocks in pieces:
        steps = jnp.exp(jax.random.uniform(jax.random.fold_in(own, dim), (blocks,), jnp.float32, least / len(pieces), top_value / len(pieces)))
        level = level * jnp.repeat(steps, extent[dim] // blocks).reshape([-1 if axis == dim else 1 for axis in range(len(extent))])
    return level


def normal_values(own_key, dims, scale, bound, cuts=(), kind=jnp.bfloat16):
    values = jax.random.normal(own_key, dims, jnp.float32) * scale
    if len(cuts) > 0:
        values = level_of(own_key, dims, cuts, -0.22, 0.18) * values
    return jnp.clip(values, min=-bound, max=bound).astype(kind)


def setup_inputs(seed: int = 0) -> dict:
    splits = jax.random.split(jax.random.key(seed), 16)
    tokens = normal_values(splits[0], (2 * IMAGES, SLOTS, D), 1.0, 6.0, ((0, 32),))
    cotangent = normal_values(splits[1], (2 * IMAGES, SLOTS, D), 1.0, 6.0, ((0, 32),))
    ratios = draw_ratios(jax.random.fold_in(splits[15], 71), 0)
    patch_index = draw_patch_index(jax.random.fold_in(splits[15], 71), 0)
    encoder_gains = jnp.clip(1.0 + 0.15 * jax.random.normal(splits[4], (2, 2, D), jnp.float32), 0.25, 1.75)
    encoder_attend_in = normal_values(splits[5], (2, D, 3, D), D ** -0.5, 0.21875, ((3, 4),))
    encoder_attend_out = normal_values(splits[6], (2, D, D), (D // 8) ** -0.5, 0.625, ((1, 4),))
    encoder_expand = normal_values(splits[7], (2, D, FF), D ** -0.5, 0.21875, ((2, 4),))
    encoder_reduce = normal_values(splits[8], (2, FF, D), FF ** -0.5, 0.109375, ((1, 4),))
    uniting_gains = jnp.clip(1.0 + 0.15 * jax.random.normal(splits[9], (3, D), jnp.float32), 0.25, 1.75)
    uniting_query = normal_values(splits[10], (D, D), D ** -0.5, 0.21875, ((1, 4),))
    uniting_pair = normal_values(splits[11], (D, 2, D), D ** -0.5, 0.21875, ((2, 4),))
    uniting_attend_out = normal_values(splits[12], (D, D), (D // 8) ** -0.5, 0.625, ((0, 4),))
    uniting_expand = normal_values(splits[13], (D, FF), D ** -0.5, 0.21875, ((1, 4),))
    uniting_reduce = normal_values(splits[14], (FF, D), FF ** -0.5, 0.109375, ((0, 4),))
    return dict(tokens=tokens, cotangent=cotangent, ratios=ratios, patch_index=patch_index, encoder_gains=encoder_gains, encoder_attend_in=encoder_attend_in, encoder_attend_out=encoder_attend_out, encoder_expand=encoder_expand, encoder_reduce=encoder_reduce, uniting_gains=uniting_gains, uniting_query=uniting_query, uniting_pair=uniting_pair, uniting_attend_out=uniting_attend_out, uniting_expand=uniting_expand, uniting_reduce=uniting_reduce)


EPSILON = 1e-06
NEGATIVE = -1e+30
HIGHEST_PRECISION = lax.Precision.HIGHEST

@jax.custom_vjp
def low(v):
    return lax.optimization_barrier(v.astype(jnp.bfloat16)).astype(jnp.float32)

@jax.custom_vjp
def low_back(v):
    return v

def low_keep(v):
    return (low(v), None)

def low_pass(kept, grad):
    return (grad,)

def back_keep(v):
    return (v, None)

def back_low(kept, grad):
    return (low(grad),)
low.defvjp(low_keep, low_pass)
low_back.defvjp(back_keep, back_low)

def product(pattern, left_side, right_side):
    return jnp.einsum(pattern, left_side, right_side, precision=HIGHEST_PRECISION)

def layer_norm(values, gain_vector):
    centered = values - lax.optimization_barrier(jnp.mean(values, -1, keepdims=True))
    spread = lax.optimization_barrier(jnp.mean(centered * centered, -1, keepdims=True))
    return centered * lax.rsqrt(spread + EPSILON) * gain_vector

def geometry(ratios, patch_index):
    counts = PATCHES * (100 - ratios) // 100
    visible = (jnp.arange(SLOTS)[None, :] < counts[:, None]).astype(jnp.float32)
    grid_row = (patch_index // GRID).astype(jnp.float32)
    grid_col = (patch_index % GRID).astype(jnp.float32)
    row_gap = grid_row[:, :, None] - grid_row[:, None, :]
    col_gap = grid_col[:, :, None] - grid_col[:, None, :]
    return (visible, jnp.sqrt(row_gap * row_gap + col_gap * col_gap))

def slope_table():
    return 2.0 ** (-8.0 * (jnp.arange(HEADS).astype(jnp.float32) + 1.0) / HEADS)

def attend_group(operands):
    queries, key_rows, value_rows, visible, distance = operands
    raw_scores = product('bqhd,bkhd->bhqk', queries, key_rows) * HEAD_DIM ** (-0.5)
    raw_scores = raw_scores - slope_table()[None, :, None, None] * distance[:, None]
    scores = jnp.where(visible[:, None, None, :] > 0.5, low_back(raw_scores), NEGATIVE)
    row_max = lax.optimization_barrier(jnp.max(scores, -1, keepdims=True))
    exponent = jnp.exp(scores - row_max)
    weights = low(exponent / lax.optimization_barrier(jnp.sum(exponent, -1, keepdims=True)))
    return low_back(low(product('bhqk,bkhd->bqhd', weights, value_rows)))

def attention(queries, key_rows, value_rows, visible, distance):
    images = queries.shape[0]
    groups = images // IMG_DEV

    def grouped(tensor):
        return tensor.reshape((groups, IMG_DEV) + tensor.shape[1:])
    mixed_rows = lax.map(jax.checkpoint(attend_group), (grouped(queries), grouped(key_rows), grouped(value_rows), grouped(visible), grouped(distance)))
    return mixed_rows.reshape((images, SLOTS, HEADS * HEAD_DIM))

def split_heads(tensor):
    return tensor.reshape(tensor.shape[:-1] + (HEADS, HEAD_DIM))

def attention_branch(normed, context, query_weight, pair_weight, output_weight, visible, distance):
    queries = low_back(low(product('bsd,de->bse', normed, query_weight)))
    pair_rows = low_back(low(product('bsd,dke->bske', context, pair_weight)))
    mixed_rows = attention(split_heads(queries), split_heads(pair_rows[:, :, 0]), split_heads(pair_rows[:, :, 1]), visible, distance)
    return low_back(product('bse,ed->bsd', mixed_rows, output_weight))

def feed_forward(inputs, gain_vector, expand_weight, reduce_weight):
    normed = low(layer_norm(inputs, gain_vector))
    hidden_pre = low_back(product('bsd,df->bsf', normed, expand_weight))
    hidden = low(jax.nn.gelu(hidden_pre, approximate=False))
    return inputs + low_back(product('bsf,fd->bsd', hidden, reduce_weight))

def encoder_block(inputs, gains, attend_in, attend_out, expand_weight, reduce_weight, visible, distance):
    normed = low(layer_norm(inputs, gains[0]))
    middle = inputs + attention_branch(normed, normed, attend_in[:, 0], attend_in[:, 1:], attend_out, visible, distance)
    return feed_forward(middle, gains[1], expand_weight, reduce_weight)

def uniting_block(radar, optical, gains, query_weight, pair_weight, attend_out, expand_weight, reduce_weight, visible, distance):
    context = low_back(low(layer_norm(optical, gains[0])))
    normed = low(layer_norm(radar, gains[1]))
    middle = radar + attention_branch(normed, context, query_weight, pair_weight, attend_out, visible, distance)
    return feed_forward(middle, gains[2], expand_weight, reduce_weight)

def stack_forward(tokens, encoder_gains, attend_in, attend_out, expand_weight, reduce_weight, uniting_gains, uniting_query, uniting_pair, uniting_out, uniting_expand, uniting_reduce, visible, distance):
    optical = encoder_block(tokens[:IMAGES], encoder_gains[0], attend_in[0], attend_out[0], expand_weight[0], reduce_weight[0], visible[:IMAGES], distance[:IMAGES])
    radar = encoder_block(tokens[IMAGES:], encoder_gains[1], attend_in[1], attend_out[1], expand_weight[1], reduce_weight[1], visible[IMAGES:], distance[IMAGES:])
    joined = uniting_block(radar, optical, uniting_gains, uniting_query, uniting_pair, uniting_out, uniting_expand, uniting_reduce, visible[IMAGES:], distance[IMAGES:])
    return jnp.concatenate([optical, joined], 0) * visible[:, :, None]

def reference(tokens, cotangent, ratios, patch_index, encoder_gains, encoder_attend_in, encoder_attend_out, encoder_expand, encoder_reduce, uniting_gains, uniting_query, uniting_pair, uniting_attend_out, uniting_expand, uniting_reduce):
    visible, distance = geometry(ratios, patch_index)
    floats = tuple((operand.astype(jnp.float32) for operand in (tokens, encoder_gains, encoder_attend_in, encoder_attend_out, encoder_expand, encoder_reduce, uniting_gains, uniting_query, uniting_pair, uniting_attend_out, uniting_expand, uniting_reduce)))

    def forward(*params):
        return stack_forward(*params, visible, distance)
    result, pullback = jax.vjp(forward, *floats)
    tokens_delta, egain_delta, ain_delta, aout_delta, eexp_delta, ered_delta, fgain_delta, fquery_delta, fpair_delta, fout_delta, fexp_delta, fred_delta = pullback(cotangent.astype(jnp.float32))
    return (result.astype(jnp.bfloat16), tokens_delta, egain_delta, ain_delta, aout_delta, eexp_delta, ered_delta, fgain_delta, fquery_delta, fpair_delta, fout_delta, fexp_delta, fred_delta)
```

```python
import jax
import jax.numpy as jnp
from jax import lax
from jax.experimental import pallas as pl
from jax.experimental.pallas import tpu as pltpu
from jax.sharding import PartitionSpec as P

D = 768
HEADS = 12
HEAD_DIM = 64
GRID = 15
PATCHES = 225
SLOTS = 136
PARTS = 4
CORE, ACROSS = 1, 2

EPSILON = 1e-06
NEGATIVE = -1e30
F32, BF16 = jnp.float32, jnp.bfloat16


def swap(array, dp_mask=0, head_mask=0):
    groups, lanes = lax.axis_size("dp"), lax.axis_size("head")
    pairs = [
        (g * lanes + h, (g ^ dp_mask) * lanes + (h ^ head_mask))
        for g in range(groups)
        for h in range(lanes)
    ]
    return lax.ppermute(array, ("dp", "head"), pairs)


def rows_nt(left, right):
    return lax.dot_general(left, right, (((1,), (1,)), ((), ())), preferred_element_type=F32)


def rows_nn(left, right):
    return lax.dot_general(left, right, (((1,), (0,)), ((), ())), preferred_element_type=F32)


def rows_tn(left, right):
    return lax.dot_general(left, right, (((0,), (0,)), ((), ())), preferred_element_type=F32)


def normalize(values):
    centered = values - jnp.mean(values, -1, keepdims=True)
    spread = lax.rsqrt(jnp.mean(centered * centered, -1, keepdims=True) + EPSILON)
    return centered * spread, spread


def layer_norm(values, gain):
    return normalize(values)[0] * gain


def norm_back(values, gain, incoming):
    unit, spread = normalize(values)
    scaled = incoming * gain
    delta = spread * (
        scaled
        - jnp.mean(scaled, -1, keepdims=True)
        - unit * jnp.mean(scaled * unit, -1, keepdims=True)
    )
    return delta, jnp.sum(incoming * unit, 0)


def gelu_pair(values):
    bell = jnp.exp(-0.5 * values * values) * 0.3989422804014327
    share = 0.5 * (1.0 + lax.erf(values * 0.7071067811865476))
    return (values * share).astype(BF16), (share + values * bell).astype(BF16)


def head_masks(rows):
    lanes = lax.broadcasted_iota(jnp.int32, (rows, 2 * HEAD_DIM), 1)
    return lanes < HEAD_DIM


def two_heads(block, first):
    zero = jnp.zeros_like(block)
    return jnp.concatenate([jnp.where(first, block, zero), jnp.where(first, zero, block)], 0)


def pick_heads(stacked, first):
    rows = stacked.shape[0] // 2
    return jnp.where(first, stacked[:rows], stacked[rows:])


def score_setup(count, key_place, query_place):
    rows = key_place.shape[0]
    row_gap = key_place[:, 0:1] - query_place[0:1, :]
    col_gap = key_place[:, 1:2] - query_place[1:2, :]
    distance = jnp.sqrt(row_gap * row_gap + col_gap * col_gap)
    seen = lax.broadcasted_iota(jnp.int32, (rows, 1), 0) < count
    return distance, seen


def scores_of(queries_two, keys, distance, slope, seen):
    raw = rows_nt(keys, queries_two) - distance * slope
    return jnp.where(seen, raw, NEGATIVE)


def attend_kernel(count, q_ref, k_ref, v_ref, key_place, query_place, slopes, o_ref, lse_ref):
    distance, seen = score_setup(count[pl.program_id(0)], key_place[0], query_place[0])
    first = head_masks(SLOTS)
    for pair in range(q_ref.shape[2] // (2 * HEAD_DIM)):
        span = slice(pair * 2 * HEAD_DIM, (pair + 1) * 2 * HEAD_DIM)
        queries = two_heads(q_ref[0, :, span].astype(F32) * HEAD_DIM**-0.5, first).astype(BF16)
        scores = scores_of(queries, k_ref[0, :, span], distance, slopes[pair : pair + 1, :], seen)
        top = jnp.max(scores, 0, keepdims=True)
        exponent = jnp.exp(scores - top)
        total = jnp.sum(exponent, 0, keepdims=True)
        weights = (exponent * (1.0 / total)).astype(BF16)
        mixed = rows_tn(weights, v_ref[0, :, span])
        o_ref[0, :, span] = pick_heads(mixed, first).astype(BF16)
        lse_ref[0, pair : pair + 1, :] = top + jnp.log(total)


def attend_back_kernel(
    count, q_ref, k_ref, v_ref, e_ref, lse_ref, key_place, query_place, slopes, dq_ref, dkv_ref
):
    distance, seen = score_setup(count[pl.program_id(0)], key_place[0], query_place[0])
    first = head_masks(SLOTS)
    width = q_ref.shape[2]
    scale = HEAD_DIM**-0.5
    for pair in range(width // (2 * HEAD_DIM)):
        low, high = pair * 2 * HEAD_DIM, (pair + 1) * 2 * HEAD_DIM
        queries = two_heads(q_ref[0, :, low:high].astype(F32) * scale, first).astype(BF16)
        incoming = two_heads(e_ref[0, :, low:high].astype(F32), first).astype(BF16)
        keys, values = k_ref[0, :, low:high], v_ref[0, :, low:high]
        scores = scores_of(queries, keys, distance, slopes[pair : pair + 1, :], seen)
        probable = jnp.exp(scores - lse_ref[0, pair : pair + 1, :])
        delta_p = rows_nt(values, incoming)
        inner = jnp.sum(delta_p * probable, 0, keepdims=True)
        delta_s = (probable * (delta_p - inner)).astype(BF16)
        dkv_ref[0, :, low:high] = rows_nn(delta_s, queries).astype(BF16)
        dkv_ref[0, :, width + low : width + high] = rows_nn(
            probable.astype(BF16), incoming
        ).astype(BF16)
        dq_ref[0, :, low:high] = (pick_heads(rows_tn(delta_s, keys), first) * scale).astype(BF16)


def lane_block(width, index):
    return pl.BlockSpec((1, SLOTS, width), lambda i, c, index=index: (i, 0, index))


def place_blocks(pairs):
    return [
        pl.BlockSpec((1, SLOTS, 2), lambda i, c: (i, 0, 0)),
        pl.BlockSpec((1, 2, 2 * SLOTS), lambda i, c: (i, 0, 0)),
        pl.BlockSpec((pairs, 2 * SLOTS), lambda i, c: (0, 0)),
    ]


def attend(q_from, k_from, v_from, width, geometry, slopes):
    counts, key_place, query_place = geometry
    images, pairs = counts.shape[0], width // (2 * HEAD_DIM)
    return pl.pallas_call(
        attend_kernel,
        grid_spec=pltpu.PrefetchScalarGridSpec(
            num_scalar_prefetch=1,
            grid=(images,),
            in_specs=[lane_block(width, part[1]) for part in (q_from, k_from, v_from)]
            + place_blocks(pairs),
            out_specs=[
                pl.BlockSpec((1, SLOTS, width), lambda i, c: (i, 0, 0)),
                pl.BlockSpec((1, pairs, 2 * SLOTS), lambda i, c: (i, 0, 0)),
            ],
        ),
        out_shape=[
            jax.ShapeDtypeStruct((images, SLOTS, width), BF16),
            jax.ShapeDtypeStruct((images, pairs, 2 * SLOTS), F32),
        ],
        cost_estimate=pl.CostEstimate(
            flops=images * pairs * 4 * 2 * SLOTS * SLOTS * 256 * 2,
            bytes_accessed=images * SLOTS * width * 8,
            transcendentals=images * pairs * 2 * SLOTS * SLOTS,
        ),
        name="attend",
    )(counts, q_from[0], k_from[0], v_from[0], key_place, query_place, slopes)


def attend_back(q_from, k_from, v_from, e_from, lse, width, geometry, slopes):
    counts, key_place, query_place = geometry
    images, pairs = counts.shape[0], width // (2 * HEAD_DIM)
    return pl.pallas_call(
        attend_back_kernel,
        grid_spec=pltpu.PrefetchScalarGridSpec(
            num_scalar_prefetch=1,
            grid=(images,),
            in_specs=[lane_block(width, part[1]) for part in (q_from, k_from, v_from, e_from)]
            + [pl.BlockSpec((1, pairs, 2 * SLOTS), lambda i, c: (i, 0, 0))]
            + place_blocks(pairs),
            out_specs=[
                pl.BlockSpec((1, SLOTS, width), lambda i, c: (i, 0, 0)),
                pl.BlockSpec((1, SLOTS, 2 * width), lambda i, c: (i, 0, 0)),
            ],
        ),
        out_shape=[
            jax.ShapeDtypeStruct((images, SLOTS, width), BF16),
            jax.ShapeDtypeStruct((images, SLOTS, 2 * width), BF16),
        ],
        cost_estimate=pl.CostEstimate(
            flops=images * pairs * 10 * 2 * SLOTS * SLOTS * 256 * 2,
            bytes_accessed=images * SLOTS * width * 16,
            transcendentals=images * pairs * 2 * SLOTS * SLOTS,
        ),
        name="attend_back",
    )(
        counts, q_from[0], k_from[0], v_from[0], e_from[0], lse, key_place, query_place, slopes
    )


def relative_parts(parts, own):
    return jnp.stack(
        [lax.dynamic_index_in_dim(parts, r ^ own, 0, keepdims=False) for r in range(PARTS)]
    )


def pack_attend(triple, out_weight, own):
    rows = jnp.concatenate([triple.transpose(1, 2, 0), out_weight[None]], 0)
    kinds = rows.shape[0]
    rows = rows.reshape(kinds, -1, PARTS, HEAD_DIM // PARTS, rows.shape[2])
    return relative_parts(rows.transpose(2, 0, 1, 3, 4), own)


def unpack_attend(parts, own):
    rows = relative_parts(parts, own).transpose(1, 2, 0, 3, 4)
    rows = rows.reshape(rows.shape[0], -1, rows.shape[4])
    return rows[:-1].transpose(2, 0, 1).astype(F32), rows[-1].astype(F32)


def pack_feed(expand, reduce, own):
    rows = jnp.stack([expand.T, reduce])
    rows = rows.reshape(2, PARTS, -1, rows.shape[2])
    return relative_parts(rows.transpose(1, 0, 2, 3), own)


def unpack_feed(parts, own):
    rows = relative_parts(parts, own).transpose(1, 0, 2, 3)
    rows = rows.reshape(2, -1, rows.shape[3])
    return rows[0].T.astype(F32), rows[1].astype(F32)


def fetch(quarter):
    beside = swap(quarter, head_mask=CORE)
    direct = swap(jnp.stack([quarter[0], quarter[3]]), head_mask=ACROSS)
    second = swap(direct[0], dp_mask=1)
    third = swap(direct[0], dp_mask=2)
    across = jnp.stack([direct[0], second, third, direct[1]])
    return (quarter, beside), (across, swap(across, head_mask=CORE))


def attend_rows(half):
    rows = jnp.stack(half).transpose(2, 0, 3, 1, 4, 5)
    return rows.reshape(rows.shape[0], -1, rows.shape[5])


def attend_parts(rows):
    split = rows.reshape(rows.shape[0], 2, -1, PARTS, HEAD_DIM // PARTS, rows.shape[2])
    return split.transpose(1, 3, 0, 2, 4, 5)


def feed_rows(half):
    rows = jnp.stack(half).transpose(2, 0, 1, 3, 4)
    return rows.reshape(2, -1, rows.shape[4])


def feed_parts(rows):
    split = rows.reshape(2, 2, PARTS, -1, rows.shape[2])
    return split.transpose(1, 2, 0, 3, 4)


def reduce_parts(near, far, order):
    received = swap(jnp.stack([near[1], far[1]]), head_mask=CORE)
    kept = jnp.stack([near[0], far[0]]) + received
    for step in order:
        if step == "x":
            kept = kept[:1] + swap(kept[1:], head_mask=ACROSS)
        elif step == "y":
            take = kept.reshape((kept.shape[0], -1, 2) + kept.shape[2:])
            kept = take[:, :, 0] + swap(take[:, :, 1], dp_mask=1)
        else:
            take = kept.reshape((kept.shape[0], 2, -1) + kept.shape[2:])
            kept = take[:, 0] + swap(take[:, 1], dp_mask=2)
    return kept[0, 0]


def gather_parts(part, order):
    if order == "yz":
        pair = jnp.stack([part, swap(part, dp_mask=1)])
        return jnp.concatenate([pair, swap(pair, dp_mask=2)], 0)
    pair = jnp.stack([part, swap(part, dp_mask=2)])
    other = swap(pair, dp_mask=1)
    return jnp.stack([pair[0], other[0], pair[1], other[1]])


def as_images(rows):
    return rows.reshape(-1, SLOTS, rows.shape[-1])


def as_rows(images):
    return images.reshape(-1, images.shape[-1])


def mix_forward(own_rows, side_rows, halves, geometry, slopes):
    total, stored = 0.0, []
    for weights, slope in zip(halves, slopes, strict=True):
        width = weights.shape[1]
        if side_rows is None:
            qkv = rows_nt(own_rows, weights[:3].reshape(-1, D)).astype(BF16)
            qkv = as_images(qkv)
            places = ((qkv, 0), (qkv, 1), (qkv, 2))
        else:
            q = as_images(rows_nt(own_rows, weights[0]).astype(BF16))
            kv = as_images(rows_nt(side_rows, weights[1:3].reshape(-1, D)).astype(BF16))
            places = ((q, 0), (kv, 0), (kv, 1))
        mixed, lse = attend(*places, width, geometry, slope)
        total = total + rows_nn(as_rows(mixed), weights[3])
        stored.append((places, mixed, lse))
    return total, stored


def mix_back(delta, own_rows, side_rows, halves, geometry, slopes, stored):
    delta = delta.astype(BF16)
    delta_own, delta_side, grads = 0.0, 0.0, []
    for weights, slope, (places, mixed, lse) in zip(halves, slopes, stored, strict=True):
        width = weights.shape[1]
        delta_out = rows_tn(as_rows(mixed), delta).astype(BF16)
        delta_mixed = as_images(rows_nt(delta, weights[3]).astype(BF16))
        dq, dkv = attend_back(*places, (delta_mixed, 0), lse, width, geometry, slope)
        dq, dkv = as_rows(dq), as_rows(dkv)
        source = own_rows if side_rows is None else side_rows
        grad_q = rows_tn(dq, own_rows).astype(BF16)
        grad_kv = rows_tn(dkv, source).astype(BF16)
        grads.append(
            attend_parts(
                jnp.concatenate([grad_q[None], grad_kv.reshape(2, width, D), delta_out[None]], 0)
            )
        )
        delta_own = delta_own + rows_nn(dq, weights[0])
        delta_side = delta_side + rows_nn(dkv, weights[1:3].reshape(-1, D))
    return delta_own, delta_side, grads


def feed_forward(normed, halves):
    total, stored = 0.0, []
    for weights in halves:
        hidden, slope = gelu_pair(rows_nt(normed, weights[0]))
        total = total + rows_nn(hidden, weights[1])
        stored.append((hidden, slope))
    return total, stored


def feed_back(delta, normed, halves, stored):
    delta = delta.astype(BF16)
    total, grads = 0.0, []
    for weights, (hidden, slope) in zip(halves, stored, strict=True):
        delta_pre = (rows_nt(delta, weights[1]) * slope.astype(F32)).astype(BF16)
        delta_reduce = rows_tn(hidden, delta).astype(BF16)
        delta_expand = rows_tn(delta_pre, normed).astype(BF16)
        grads.append(feed_parts(jnp.stack([delta_expand, delta_reduce])))
        total = total + rows_nn(delta_pre, weights[0])
    return total, grads


def on_device(
    tokens,
    cotangent,
    ratios,
    patch_index,
    encoder_gains,
    encoder_attend_in,
    encoder_attend_out,
    encoder_expand,
    encoder_reduce,
    uniting_gains,
    uniting_query,
    uniting_pair,
    uniting_attend_out,
    uniting_expand,
    uniting_reduce,
):
    groups = lax.axis_size("dp")
    side = groups // 2
    group, lane = lax.axis_index("dp"), lax.axis_index("head")
    radar = group >= side
    modality = radar.astype(jnp.int32)
    own = group % PARTS
    images = tokens.shape[0]
    some = images // 2

    def select_slot(stacked):
        return lax.dynamic_index_in_dim(stacked, modality, 0, keepdims=False)

    gains = select_slot(encoder_gains)

    enc_attend = fetch(
        pack_attend(select_slot(encoder_attend_in), select_slot(encoder_attend_out), own)
    )
    enc_feed = fetch(pack_feed(select_slot(encoder_expand), select_slot(encoder_reduce), own))
    uni_attend = fetch(
        pack_attend(
            jnp.concatenate([uniting_query[:, None], uniting_pair], 1), uniting_attend_out, own
        )
    )
    uni_feed = fetch(pack_feed(uniting_expand, uniting_reduce, own))
    enc_attend = [attend_rows(half) for half in enc_attend]
    enc_feed = [feed_rows(half) for half in enc_feed]
    uni_attend = [attend_rows(half) for half in uni_attend]
    uni_feed = [feed_rows(half) for half in uni_feed]

    own_ratios = lax.dynamic_slice_in_dim(ratios, lane * images, images, 0)
    own_patches = lax.dynamic_slice_in_dim(patch_index, lane * images, images, 0)
    counts = PATCHES * (100 - own_ratios) // 100
    place = jnp.stack([own_patches // GRID, own_patches % GRID], 1).astype(F32)
    geometry = (counts, place.transpose(0, 2, 1), jnp.concatenate([place, place], 2))

    def own_pairs(array):
        return lax.dynamic_slice_in_dim(array, modality * some, some, 0)

    pair_geometry = tuple(own_pairs(part) for part in geometry)
    visible = (jnp.arange(SLOTS)[None, :] < counts[:, None]).astype(F32)[:, :, None]

    table = 2.0 ** (-8.0 * (jnp.arange(HEADS).astype(F32) + 1.0) / HEADS)
    table = table.reshape(lax.axis_size("head"), -1)

    def slopes_of(*masks):
        heads = jnp.concatenate(
            [lax.dynamic_index_in_dim(table, lane ^ mask, 0, keepdims=False) for mask in masks]
        )
        return jnp.repeat(heads.reshape(-1, 2), SLOTS, 1)

    slopes = (slopes_of(0, CORE), slopes_of(ACROSS, ACROSS | CORE))

    inputs = as_rows(tokens).astype(F32)
    normed_one = layer_norm(inputs, gains[0]).astype(BF16)
    mixed, mix_stored = mix_forward(normed_one, None, enc_attend, geometry, slopes)
    middle = inputs + mixed
    normed_two = layer_norm(middle, gains[1]).astype(BF16)
    fed, feed_stored = feed_forward(normed_two, enc_feed)
    encoded = middle + fed

    context = layer_norm(encoded, uniting_gains[0]).astype(BF16)
    cut = some * SLOTS
    received = swap(
        jnp.where(radar, encoded[:cut].astype(BF16), context[cut:]), dp_mask=side
    )
    radar_rows = jnp.where(radar, encoded[cut:], received.astype(F32))
    context_rows = jnp.where(radar, received, context[:cut])
    sent_cotangent = swap(cotangent[:some], dp_mask=side)
    pair_cotangent = jnp.where(radar, cotangent[some:], sent_cotangent)

    normed_query = layer_norm(radar_rows, uniting_gains[1]).astype(BF16)
    mixed, unite_stored = mix_forward(
        normed_query, context_rows, uni_attend, pair_geometry, slopes
    )
    unite_middle = radar_rows + mixed
    normed_three = layer_norm(unite_middle, uniting_gains[2]).astype(BF16)
    fed, unite_feed_stored = feed_forward(normed_three, uni_feed)
    joined = unite_middle + fed

    joined_half = as_images(joined).astype(BF16)
    other_half = swap(joined_half, dp_mask=side)
    encoded_images = as_images(encoded).astype(BF16)
    layer_output = visible.astype(BF16) * jnp.where(
        radar, jnp.concatenate([other_half, joined_half], 0), encoded_images
    )

    delta_joined = as_rows(own_pairs(visible) * pair_cotangent.astype(F32))
    delta_normed, uni_feed_grads = feed_back(
        delta_joined, normed_three, uni_feed, unite_feed_stored
    )
    delta_part, gain_three = norm_back(unite_middle, uniting_gains[2], delta_normed)
    delta_middle = delta_joined + delta_part
    delta_query, delta_context, uni_attend_grads = mix_back(
        delta_middle,
        normed_query,
        context_rows,
        uni_attend,
        pair_geometry,
        slopes,
        unite_stored,
    )
    delta_part, gain_two = norm_back(radar_rows, uniting_gains[1], delta_query)
    delta_radar = delta_middle + delta_part
    delta_context = delta_context.astype(BF16)
    returned = swap(
        jnp.where(radar, delta_context, delta_radar.astype(BF16)), dp_mask=side
    )
    nothing = jnp.zeros_like(returned)
    into_context = jnp.where(
        radar, 0, jnp.concatenate([delta_context, returned], 0)
    ).astype(F32)
    delta_part, gain_one = norm_back(encoded, uniting_gains[0], into_context)
    direct = jnp.where(
        radar,
        jnp.concatenate([returned.astype(F32), delta_radar], 0),
        as_rows(visible * cotangent.astype(F32)),
    )
    delta_encoded = direct + delta_part

    delta_normed, enc_feed_grads = feed_back(delta_encoded, normed_two, enc_feed, feed_stored)
    delta_part, gain_b = norm_back(middle, gains[1], delta_normed)
    delta_middle = delta_encoded + delta_part
    delta_own, delta_side, enc_attend_grads = mix_back(
        delta_middle, normed_one, None, enc_attend, geometry, slopes, mix_stored
    )
    delta_part, gain_a = norm_back(inputs, gains[0], delta_own + delta_side)
    tokens_delta = as_images(delta_middle + delta_part)

    def over_rest(array, stop):
        mask = PARTS
        while mask < stop:
            array = array + swap(array, dp_mask=mask)
            mask *= 2
        return array

    def united(grads, order, spread):
        return gather_parts(over_rest(reduce_parts(*grads, order), groups), spread)

    def of_encoders(grads, order, spread):
        part = over_rest(reduce_parts(*grads, order), side)
        other = swap(part, dp_mask=side)
        both = jnp.stack([jnp.where(radar, other, part), jnp.where(radar, part, other)])
        gathered = gather_parts(both, spread)
        return gathered[:, 0], gathered[:, 1]

    fexpand, freduce = unpack_feed(united(uni_feed_grads, "xyz", "yz"), own)
    ftriple, fout = unpack_attend(united(uni_attend_grads, "yzx", "zy"), own)
    feeds = [unpack_feed(g, own) for g in of_encoders(enc_feed_grads, "zyx", "yz")]
    attends = [unpack_attend(g, own) for g in of_encoders(enc_attend_grads, "xzy", "zy")]

    slot_mask = (jnp.arange(2) == modality).astype(F32)[:, None, None]
    gain_totals = lax.psum(
        (
            slot_mask * jnp.stack([gain_a, gain_b])[None],
            jnp.stack([gain_one, gain_two, gain_three]),
        ),
        ("dp", "head"),
    )
    return (
        layer_output,
        tokens_delta,
        gain_totals[0],
        jnp.stack([attends[0][0], attends[1][0]]),
        jnp.stack([attends[0][1], attends[1][1]]),
        jnp.stack([feeds[0][0], feeds[1][0]]),
        jnp.stack([feeds[0][1], feeds[1][1]]),
        gain_totals[1],
        ftriple[:, 0],
        ftriple[:, 1:],
        fout,
        fexpand,
        freduce,
    )


def solution(mesh):
    return jax.shard_map(
        on_device,
        mesh=mesh,
        in_specs=(
            P(("dp", "head"), None, None),
            P(("dp", "head"), None, None),
            P("dp"),
            P("dp", None),
            P(),
            P(None, None, None, "head"),
            P(None, "head", None),
            P(None, None, "head"),
            P(None, "head", None),
            P(),
            P(None, "head"),
            P(None, None, "head"),
            P("head", None),
            P(None, "head"),
            P("head", None),
        ),
        out_specs=(
            P(("dp", "head"), None, None),
            P(("dp", "head"), None, None),
            P(),
            P(None, None, None, "head"),
            P(None, "head", None),
            P(None, None, "head"),
            P(None, "head", None),
            P(),
            P(None, "head"),
            P(None, None, "head"),
            P("head", None),
            P(None, "head"),
            P("head", None),
        ),
        check_vma=False,
    )
```

```python
import functools

import jax
import jax.numpy as jnp
from jax import lax
from jax.experimental import pallas as pl
from jax.experimental.pallas import tpu as pltpu
from jax.sharding import PartitionSpec as P

D = 768
HEADS = 12
HEAD_DIM = 64
GRID = 15
PATCHES = 225
SLOTS = 136
PARTS = 4
PIECE = D // PARTS
CORE, ACROSS = 1, 2
SCALE = HEAD_DIM**-0.5

EPSILON = 1e-06
NEGATIVE = -1e30
F32, BF16 = jnp.float32, jnp.bfloat16
WHOLE = pl.BlockSpec(memory_space=pltpu.VMEM)
ANYWHERE = pl.BlockSpec(memory_space=pl.ANY)
SCALARS = pl.BlockSpec(memory_space=pltpu.SMEM)
ROOM = 56 << 20


def cost(rows, fixed, each):
    return pl.CostEstimate(
        flops=int((fixed + each * rows / 816) * 1e7), bytes_accessed=1, transcendentals=0
    )


def swap(array, dp_mask=0, head_mask=0, senders=None):
    groups, lanes = lax.axis_size("dp"), lax.axis_size("head")
    pairs = [
        (g * lanes + h, (g ^ dp_mask) * lanes + (h ^ head_mask))
        for g in (range(groups) if senders is None else senders)
        for h in range(lanes)
    ]
    return lax.ppermute(array, ("dp", "head"), pairs)


def tie(*arrays):
    return lax.optimization_barrier(arrays)


def rows_nt(left, right):
    return lax.dot_general(left, right, (((1,), (1,)), ((), ())), preferred_element_type=F32)


def rows_nn(left, right):
    return lax.dot_general(left, right, (((1,), (0,)), ((), ())), preferred_element_type=F32)


def rows_tn(left, right):
    return lax.dot_general(left, right, (((0,), (0,)), ((), ())), preferred_element_type=F32)


def normalize(values):
    centered = values - jnp.mean(values, -1, keepdims=True)
    spread = lax.rsqrt(jnp.mean(centered * centered, -1, keepdims=True) + EPSILON)
    return centered * spread, spread


def layer_norm(values, gain):
    return normalize(values)[0] * gain


def norm_back(values, gain, incoming):
    unit, spread = normalize(values)
    scaled = incoming * gain
    delta = spread * (
        scaled
        - jnp.mean(scaled, -1, keepdims=True)
        - unit * jnp.mean(scaled * unit, -1, keepdims=True)
    )
    return delta, jnp.sum(incoming * unit, 0, keepdims=True)


def glue(function, *arrays):
    leaves, tree = jax.tree.flatten(arrays)
    results, result_tree = jax.tree.flatten(jax.eval_shape(function, *arrays))

    def kernel(*refs):
        values = tree.unflatten([ref[...] for ref in refs[: len(leaves)]])
        for ref, value in zip(refs[len(leaves) :], jax.tree.leaves(function(*values))):
            ref[...] = value

    out = pl.pallas_call(
        kernel,
        in_specs=[WHOLE] * len(leaves),
        out_specs=[WHOLE] * len(results),
        out_shape=results,
        compiler_params=pltpu.CompilerParams(vmem_limit_bytes=ROOM),
        cost_estimate=cost(816, 1, 0),
        name="glue",
    )(*leaves)
    return result_tree.unflatten(out)


def chunks_of(rows):
    step = 2 * SLOTS if rows % (2 * SLOTS) == 0 else rows
    return [slice(start, start + step) for start in range(0, rows, step)]


QUARTERS_IN = {1: 4, 2: 2, 8: 2, 10: 4}


def feed_copies(pieces, meta, room, sems):
    if len(pieces) == 1:
        return [
            [pltpu.make_async_copy(pieces[0].at[meta[1] ^ q], room.at[q], sems.at[q])]
            for q in range(4)
        ]
    near = len(pieces) % 8
    copies = [
        [pltpu.make_async_copy(pieces[q], room.at[q], sems.at[q])] for q in range(near)
    ]
    for q in range(near, near + (len(pieces) - near) // PARTS):
        group = []
        for r in range(PARTS):
            at = near + (q - near) * PARTS + r
            rows = pl.ds(pl.multiple_of((meta[0] ^ r) * PIECE, PIECE), PIECE)
            group.append(
                pltpu.make_async_copy(pieces[at], room.at[q, :, rows, :], sems.at[at])
            )
        copies.append(group)
    return copies


def mix_copies(pieces, meta, room, sems):
    near = len(pieces) % 8
    copies = [
        pltpu.make_async_copy(
            pieces[q], room.at[:, pl.ds(q * PIECE, PIECE), :], sems.at[q]
        )
        for q in range(near)
    ]
    for at in range(near, len(pieces)):
        q, r = divmod(at - near, PARTS)
        rows = pl.ds((near + q) * PIECE, PIECE)
        copies.append(
            pltpu.make_async_copy(pieces[at], room.at[meta[0] ^ r, rows, :], sems.at[at])
        )
    return copies


SIZES = (64, 96, 128, SLOTS)


def by_size(count, branch):
    which = sum((count > size).astype(jnp.int32) for size in SIZES[:-1])
    lax.switch(which, [functools.partial(branch, size) for size in SIZES])


def two_heads(block, first):
    zero = jnp.zeros_like(block)
    return jnp.concatenate(
        [jnp.where(first, block, zero), jnp.where(first, zero, block)], 0
    ).astype(BF16)


def pick_heads(stacked, first):
    size = stacked.shape[0] // 2
    return jnp.where(first, stacked[:size], stacked[size:])


def image_setup(size, distance_ref, image, count):
    first = lax.broadcasted_iota(jnp.int32, (size, 2 * HEAD_DIM), 1) < HEAD_DIM
    distance = distance_ref[image, :size, :size]
    distance = jnp.concatenate([distance, distance], 1)
    seen = lax.broadcasted_iota(jnp.int32, (size, 1), 0) < count
    lanes = lax.broadcasted_iota(jnp.int32, (1, 2 * size), 1) < size

    def scores_of(keys, queries, slopes, head):
        slope = jnp.where(lanes, slopes[head], slopes[head + 1])
        return jnp.where(seen, rows_nt(keys, queries) - distance * slope, NEGATIVE)

    return first, scores_of


def mix_forward_kernel(local, cross, images, head, n_pieces, *refs):
    meta, slopes, x_ref = refs[:3]
    refs = refs[3:]
    if cross:
        c_ref, refs = refs[0], refs[1:]
    if local:
        gain_ref, refs = refs[0], refs[1:]
    else:
        a_ref, refs = refs[0], refs[1:]
    pieces, refs = refs[:n_pieces], refs[n_pieces:]
    distance_ref, refs = refs[0], refs[1:]
    if local:
        a_ref, refs = refs[0], refs[1:]
    out_ref, qkv_ref, o_ref, lse_ref, room, wide, sems = refs
    copies = mix_copies(pieces, meta, room, sems)
    for copy in copies:
        copy.start()
    chunks = chunks_of(images * SLOTS)
    if local:
        for rows in chunks:
            a_ref[rows, :] = layer_norm(x_ref[rows, :].astype(F32), gain_ref[...]).astype(BF16)
    for copy in copies:
        copy.wait()
    width = o_ref.shape[1]
    if cross:
        wide[:, :width] = rows_nt(a_ref[...], room[0])
        wide[:, width:] = rows_nt(c_ref[...], room[1:3].reshape(2 * width, D))
    else:
        wide[...] = rows_nt(a_ref[...], room[:3].reshape(3 * width, D))

    def one_image(i, carry):
        image = meta[2] + i
        start = pl.multiple_of(i * SLOTS, 8)
        qkv_ref[i] = wide[pl.ds(start, SLOTS), :].astype(BF16)

        def work(size):
            first, scores_of = image_setup(size, distance_ref, image, meta[3 + image])
            rows = pl.ds(start, size)
            for pair in range(width // (2 * HEAD_DIM)):
                low, high = pair * 2 * HEAD_DIM, (pair + 1) * 2 * HEAD_DIM
                k = wide[rows, width + low : width + high].astype(BF16)
                v = wide[rows, 2 * width + low : 2 * width + high].astype(BF16)
                queries = two_heads(
                    wide[rows, low:high].astype(BF16).astype(F32) * SCALE, first
                )
                scores = scores_of(k, queries, slopes, head + 2 * pair)
                top = jnp.max(scores, 0, keepdims=True)
                exponent = jnp.exp(scores - top)
                total = jnp.sum(exponent, 0, keepdims=True)
                weights = (exponent * (1.0 / total)).astype(BF16)
                wide[rows, low:high] = pick_heads(rows_tn(weights, v), first)
                lse_ref[i, pair : pair + 1, : 2 * size] = top + jnp.log(total)
            if size < SLOTS:
                rest = pl.ds(pl.multiple_of(start + size, 8), SLOTS - size)
                wide[rest, :width] = jnp.zeros((SLOTS - size, width), F32)

        by_size(meta[3 + image], work)
        return carry

    lax.fori_loop(0, images, one_image, 0)
    for rows in chunks:
        o_ref[rows, :] = wide[rows, :width].astype(BF16)
    out_ref[...] = x_ref[...].astype(F32) + rows_nn(o_ref[...], room[3])


def mix_forward(meta, slopes, x, context, gain, normed, pieces, distance, head=0):
    images = x.shape[0] // SLOTS
    rows = images * SLOTS
    cross, local = context is not None, normed is None
    width = PIECE * QUARTERS_IN[len(pieces)]
    operands = [meta, slopes, x] + ([context] if cross else [])
    operands += [gain if local else normed, *pieces, distance]
    specs = [SCALARS] * 2 + [WHOLE] * (3 if cross else 2) + [ANYWHERE] * len(pieces) + [WHOLE]
    narrow = jax.ShapeDtypeStruct((rows, D), BF16)
    return pl.pallas_call(
        functools.partial(mix_forward_kernel, local, cross, images, head, len(pieces)),
        in_specs=specs,
        out_specs=[WHOLE] * (5 if local else 4),
        out_shape=([narrow] if local else [])
        + [
            jax.ShapeDtypeStruct((rows, D), F32),
            jax.ShapeDtypeStruct((images, SLOTS, 3 * width), BF16),
            jax.ShapeDtypeStruct((rows, width), BF16),
            jax.ShapeDtypeStruct((images, width // (2 * HEAD_DIM), 2 * SLOTS), F32),
        ],
        scratch_shapes=[
            pltpu.VMEM((4, width, D), BF16),
            pltpu.VMEM((rows, 3 * width), F32),
            pltpu.SemaphoreType.DMA((16,)),
        ],
        compiler_params=pltpu.CompilerParams(vmem_limit_bytes=ROOM),
        cost_estimate=cost(rows, 4, 8 * width / 384),
        name="mix_forward",
    )(*operands)


def mix_back_kernel(cross, images, spans, *refs):
    meta, slopes, e_ref, x_ref, gain_ref = refs[:5]
    refs = refs[5:]
    qkv_refs, lse_refs, refs = refs[:spans], refs[spans : 2 * spans], refs[2 * spans :]
    pieces, refs = refs[:10], refs[10:]
    distance_ref, dx_ref, dgain_ref, dqkv_ref, eb_ref = refs[:5]
    refs = refs[5:]
    if cross:
        dc_ref, refs = refs[0], refs[1:]
    room, inner_ref, wide, sems = refs
    copies = mix_copies(pieces, meta, room, sems)
    for copy in copies:
        copy.start()
    chunks = chunks_of(images * SLOTS)
    for rows in chunks:
        eb_ref[rows, :] = e_ref[rows, :].astype(BF16)
    for copy in copies:
        copy.wait()
    inner_ref[...] = rows_nt(eb_ref[...], room[3])

    width = D // spans

    def one_image(i, carry):
        image = meta[2] + i
        start = pl.multiple_of(i * SLOTS, 8)

        def work(size):
            first, scores_of = image_setup(size, distance_ref, image, meta[3 + image])
            rows = pl.ds(start, size)
            for pair in range(HEADS // 2):
                low, high = pair * 2 * HEAD_DIM, (pair + 1) * 2 * HEAD_DIM
                half, inside = divmod(pair, HEADS // 2 // spans)
                qkv_ref, lse_ref = qkv_refs[half], lse_refs[half]
                at, to = inside * 2 * HEAD_DIM, (inside + 1) * 2 * HEAD_DIM
                queries = two_heads(qkv_ref[i, :size, at:to].astype(F32) * SCALE, first)
                incoming = two_heads(inner_ref[rows, low:high], first)
                k = qkv_ref[i, :size, width + at : width + to]
                v = qkv_ref[i, :size, 2 * width + at : 2 * width + to]
                scores = scores_of(k, queries, slopes, 2 * pair)
                probable = jnp.exp(scores - lse_ref[i, inside : inside + 1, : 2 * size])
                delta_p = rows_nt(v, incoming)
                shared = jnp.sum(delta_p * probable, 0, keepdims=True)
                delta_s = (probable * (delta_p - shared)).astype(BF16)
                wide[rows, low:high] = pick_heads(rows_tn(delta_s, k), first) * SCALE
                wide[rows, D + low : D + high] = rows_nn(delta_s, queries)
                wide[rows, 2 * D + low : 2 * D + high] = rows_nn(
                    probable.astype(BF16), incoming
                )
            if size < SLOTS:
                rest = pl.ds(pl.multiple_of(start + size, 8), SLOTS - size)
                wide[rest, :] = jnp.zeros((SLOTS - size, 3 * D), F32)

        by_size(meta[3 + image], work)
        return carry

    lax.fori_loop(0, images, one_image, 0)
    for rows in chunks:
        dqkv_ref[rows, :] = wide[rows, :].astype(BF16)
    delta = rows_nn(dqkv_ref[:, :D], room[0])
    side = rows_nn(dqkv_ref[:, D : 2 * D], room[1]) + rows_nn(dqkv_ref[:, 2 * D :], room[2])
    if cross:
        dc_ref[...] = side.astype(BF16)
        inner_ref[...] = delta
    else:
        inner_ref[...] = delta + side
    gain_total = jnp.zeros((1, D), F32)
    for rows in chunks:
        part, gain_part = norm_back(x_ref[rows, :].astype(F32), gain_ref[...], inner_ref[rows, :])
        dx_ref[rows, :] = e_ref[rows, :] + part
        gain_total = gain_total + gain_part
    dgain_ref[...] = gain_total


def mix_back(meta, slopes, delta, x, gain, qkv, lse, pieces, distance, cross):
    images = qkv[0].shape[0]
    rows = images * SLOTS
    wide_rows = jax.ShapeDtypeStruct((rows, D), BF16)
    return pl.pallas_call(
        functools.partial(mix_back_kernel, cross, images, len(qkv)),
        in_specs=[SCALARS] * 2
        + [WHOLE] * (3 + 2 * len(qkv))
        + [ANYWHERE] * len(pieces)
        + [WHOLE],
        out_specs=[WHOLE] * (5 if cross else 4),
        out_shape=[
            jax.ShapeDtypeStruct((rows, D), F32),
            jax.ShapeDtypeStruct((1, D), F32),
            jax.ShapeDtypeStruct((rows, 3 * D), BF16),
            wide_rows,
        ]
        + ([wide_rows] if cross else []),
        scratch_shapes=[
            pltpu.VMEM((4, D, D), BF16),
            pltpu.VMEM((rows, D), F32),
            pltpu.VMEM((rows, 3 * D), F32),
            pltpu.SemaphoreType.DMA((16,)),
        ],
        compiler_params=pltpu.CompilerParams(vmem_limit_bytes=ROOM),
        cost_estimate=cost(rows, 5, 23),
        name="mix_back",
    )(meta, slopes, delta, x, gain, *qkv, *lse, *pieces, distance)


def mix_weights_kernel(more, place, dqkv_ref, *refs):
    if more:
        *refs, scratch = refs
        refs, outs = refs[:-2], refs[-2:]
        refs = (*refs, scratch)
    else:
        refs, outs = refs[:-2], refs[-2:]
    if more:
        gain_refs, refs, gains_ref = refs[:5], refs[5:-1], refs[-1]
    o_refs, (a_ref, c_ref, eb_ref) = refs[:-3], refs[-3:]
    kind = pl.program_id(0)

    def put(first, delta):
        for q in range(delta.shape[0] // PIECE):
            part = delta[q * PIECE : (q + 1) * PIECE].astype(BF16)
            outs[(first + q) % 2][(first + q) // 2, 0, :PIECE] = part

    @pl.when(kind == 0)
    def _():
        put(0, rows_tn(dqkv_ref[...], a_ref[...]))

    @pl.when(jnp.logical_or(kind == 1, kind == 2))
    def _():
        put(0, rows_tn(dqkv_ref[...], c_ref[...]))

    @pl.when(kind == 3)
    def _():
        for span, o_ref in enumerate(o_refs):
            put(span * 4 // len(o_refs), rows_tn(o_ref[...], eb_ref[...]))

    if more:
        gains_ref[...] = jnp.zeros_like(gains_ref)
        for i in range(2):
            gains_ref[pl.ds(2 * place[2] + i, 1), :] = gain_refs[i][...]
        for i in range(2, 5):
            gains_ref[2 + i : 3 + i, :] = gain_refs[i][...]
        for out in outs:
            for half in range(2):
                out[half, 0, PIECE:] = gains_ref[...].astype(BF16)


def mix_weights(place, dqkv, o, a, c, eb, gains=None):
    rows = a.shape[0]
    more = gains is not None
    fixed = pl.BlockSpec((rows, D), lambda kind, place: (0, 0))
    narrow = pl.BlockSpec((rows, D // len(o)), lambda kind, place: (0, 0))
    tall = PIECE + (16 if more else 0)
    out = pl.BlockSpec((2, 1, tall, D), lambda kind, place: (0, kind ^ place[0], 0, 0))
    shape = jax.ShapeDtypeStruct((2, PARTS, tall, D), BF16)
    return pl.pallas_call(
        functools.partial(mix_weights_kernel, more),
        grid_spec=pltpu.PrefetchScalarGridSpec(
            num_scalar_prefetch=1,
            grid=(4,),
            in_specs=[pl.BlockSpec((rows, D), lambda kind, place: (0, jnp.minimum(kind, 2)))]
            + [pl.BlockSpec((1, D), lambda kind, place: (0, 0))] * (5 if more else 0)
            + [narrow] * len(o)
            + [fixed] * 3,
            out_specs=[out, out],
            scratch_shapes=[pltpu.VMEM((16, D), F32)] if more else [],
        ),
        out_shape=[shape, shape],
        compiler_params=pltpu.CompilerParams(vmem_limit_bytes=ROOM),
        cost_estimate=cost(rows, 3.5, 7),
        name="mix_weights",
    )(place, dqkv, *(gains if more else []), *o, a, c, eb)


def fetch_quarter(step, copies):
    @pl.when(step == 0)
    def _():
        for group in copies:
            for copy in group:
                copy.start()

    for q, group in enumerate(copies):

        @pl.when(step == q)
        def _(group=group):
            for copy in group:
                copy.wait()


def feed_forward_kernel(local, n_pieces, meta, x_ref, norm_ref, *refs):
    pieces, refs = refs[:n_pieces], refs[n_pieces:]
    if local:
        b_ref, refs = refs[0], refs[1:]
    else:
        b_ref = norm_ref
    y_ref, h_ref, g_ref, room, sems = refs
    step = pl.program_id(0)
    fetch_quarter(step, feed_copies(pieces, meta, room, sems))

    @pl.when(step == 0)
    def _():
        for rows in chunks_of(x_ref.shape[0]):
            values = x_ref[rows, :]
            y_ref[rows, :] = values
            if local:
                b_ref[rows, :] = layer_norm(values, norm_ref[...]).astype(BF16)

    before = rows_nn(b_ref[...], room[step, 0])
    bell = jnp.exp(-0.5 * before * before) * 0.3989422804014327
    share = 0.5 * (1.0 + lax.erf(before * 0.7071067811865476))
    h_ref[...] = (before * share).astype(BF16)
    g_ref[...] = (share + before * bell).astype(BF16)
    y_ref[...] += rows_nn(h_ref[...], room[step, 1])


def feed_forward(meta, x, gain, normed, pieces):
    rows = x.shape[0]
    local = normed is None
    quarters = QUARTERS_IN[len(pieces)]
    fixed = pl.BlockSpec((rows, D), lambda q: (0, 0))
    moving = pl.BlockSpec((rows, D), lambda q: (0, q))
    hidden = jax.ShapeDtypeStruct((rows, quarters * D), BF16)
    return pl.pallas_call(
        functools.partial(feed_forward_kernel, local, len(pieces)),
        grid=(quarters,),
        in_specs=[SCALARS, fixed, pl.BlockSpec((1, D), lambda q: (0, 0)) if local else fixed]
        + [ANYWHERE] * len(pieces),
        out_specs=([fixed] if local else []) + [fixed, moving, moving],
        out_shape=([jax.ShapeDtypeStruct((rows, D), BF16)] if local else [])
        + [jax.ShapeDtypeStruct((rows, D), F32), hidden, hidden],
        scratch_shapes=[pltpu.VMEM((quarters, 2, D, D), BF16), pltpu.SemaphoreType.DMA((16,))],
        compiler_params=pltpu.CompilerParams(vmem_limit_bytes=ROOM),
        cost_estimate=cost(rows, 3.6, 4 * quarters),
        name="feed_forward",
    )(meta, x, gain if local else normed, *pieces)


def feed_rows_kernel(leaving, meta, x_ref, gain_ref, next_gain_ref, *refs):
    pieces, refs = refs[:10], refs[10:]
    if not leaving:
        refs = refs[4:]
    y_ref, b_ref, h_ref, g_ref, out_ref, room, sems = refs
    step = pl.program_id(0)
    fetch_quarter(step, feed_copies(pieces, meta, room, sems))

    @pl.when(step == 0)
    def _():
        values = x_ref[...]
        y_ref[...] = values
        b_ref[...] = layer_norm(values, gain_ref[...]).astype(BF16)

    before = rows_nn(b_ref[...], room[step, 0])
    bell = jnp.exp(-0.5 * before * before) * 0.3989422804014327
    share = 0.5 * (1.0 + lax.erf(before * 0.7071067811865476))
    h_ref[...] = (before * share).astype(BF16)
    g_ref[...] = (share + before * bell).astype(BF16)
    y_ref[...] += rows_nn(h_ref[...], room[step, 1])

    @pl.when(jnp.logical_and(step == 3, jnp.logical_or(not leaving, meta[2] == 0)))
    def _():
        out_ref[...] = layer_norm(y_ref[...], next_gain_ref[...]).astype(BF16)

    if leaving:

        @pl.when(jnp.logical_and(step == 3, meta[2] == 1))
        def _():
            out_ref[...] = y_ref[...].astype(BF16)


def feed_rows(place, x, gain, next_gain, pieces, first=None):
    rows = x.shape[0] // 2
    leaving = first is None

    def block(place):
        return 1 - place[2] if leaving else place[2]

    fixed = pl.BlockSpec((rows, D), lambda q, place: (block(place), 0))
    moving = pl.BlockSpec((rows, D), lambda q, place: (block(place), q))
    narrow = pl.BlockSpec((1, D), lambda q, place: (0, 0))
    hidden = jax.ShapeDtypeStruct((2 * rows, 4 * D), BF16)
    return pl.pallas_call(
        functools.partial(feed_rows_kernel, leaving),
        grid_spec=pltpu.PrefetchScalarGridSpec(
            num_scalar_prefetch=1,
            grid=(4,),
            in_specs=[fixed, narrow, narrow] + [ANYWHERE] * (10 if leaving else 14),
            out_specs=[fixed, fixed, moving, moving]
            + [pl.BlockSpec((rows, D), lambda q, place: (0, 0))],
            scratch_shapes=[pltpu.VMEM((4, 2, D, D), BF16), pltpu.SemaphoreType.DMA((16,))],
        ),
        out_shape=[
            jax.ShapeDtypeStruct((2 * rows, D), F32),
            jax.ShapeDtypeStruct((2 * rows, D), BF16),
            hidden,
            hidden,
            jax.ShapeDtypeStruct((rows, D), BF16),
        ],
        input_output_aliases={} if leaving else {14 + i: i for i in range(4)},
        compiler_params=pltpu.CompilerParams(vmem_limit_bytes=ROOM),
        cost_estimate=cost(rows, 3.6, 16),
        name="feed_rows",
    )(place, x, gain, next_gain, *pieces, *([] if leaving else first))


def feed_back_kernel(spans, n_pieces, meta, e_ref, x_ref, gain_ref, *refs):
    slopes, refs = refs[:spans], refs[spans:]
    pieces, refs = refs[:n_pieces], refs[n_pieces:]
    dx_ref, dgain_ref, eb_ref, eu_ref, room, sems = refs
    step = pl.program_id(0)
    fetch_quarter(step, feed_copies(pieces, meta, room, sems))
    chunks = chunks_of(x_ref.shape[0])

    @pl.when(step == 0)
    def _():
        for rows in chunks:
            eb_ref[rows, :] = e_ref[rows, :].astype(BF16)
            dx_ref[rows, :] = jnp.zeros_like(dx_ref[rows, :])

    slope = slopes[0][...]
    if spans == 2:
        slope = jnp.where(step < 2, slope, slopes[1][...])
    slope = slope.astype(F32)
    eu_ref[...] = (rows_nt(eb_ref[...], room[step, 1]) * slope).astype(BF16)
    dx_ref[...] += rows_nt(eu_ref[...], room[step, 0])

    @pl.when(step == 3)
    def _():
        gain_total = jnp.zeros((1, D), F32)
        for rows in chunks:
            part, gain_part = norm_back(x_ref[rows, :], gain_ref[...], dx_ref[rows, :])
            dx_ref[rows, :] = e_ref[rows, :] + part
            gain_total = gain_total + gain_part
        dgain_ref[...] = gain_total


def feed_back(meta, delta, x, gain, slope, pieces):
    rows = x.shape[0]
    fixed = pl.BlockSpec((rows, D), lambda q: (0, 0))
    moving = pl.BlockSpec((rows, D), lambda q: (0, q))
    narrow = pl.BlockSpec((1, D), lambda q: (0, 0))
    slopes = [moving]
    if len(slope) == 2:
        slopes = [
            pl.BlockSpec((rows, D), lambda q: (0, jnp.minimum(q, 1))),
            pl.BlockSpec((rows, D), lambda q: (0, jnp.maximum(q - 2, 0))),
        ]
    return pl.pallas_call(
        functools.partial(feed_back_kernel, len(slope), len(pieces)),
        grid=(4,),
        in_specs=[SCALARS, fixed, fixed, narrow] + slopes + [ANYWHERE] * len(pieces),
        out_specs=[fixed, narrow, fixed, moving],
        out_shape=[
            jax.ShapeDtypeStruct((rows, D), F32),
            jax.ShapeDtypeStruct((1, D), F32),
            jax.ShapeDtypeStruct((rows, D), BF16),
            jax.ShapeDtypeStruct((rows, 4 * D), BF16),
        ],
        scratch_shapes=[pltpu.VMEM((4, 2, D, D), BF16), pltpu.SemaphoreType.DMA((16,))],
        compiler_params=pltpu.CompilerParams(vmem_limit_bytes=ROOM),
        cost_estimate=cost(rows, 5, 13.5),
        name="feed_back",
    )(meta, delta, x, gain, *slope, *pieces)


def feed_weights_kernel(place, eu_ref, *refs):
    h_refs, (b_ref, eb_ref, out_ref) = refs[:-3], refs[-3:]
    j, kind = pl.program_id(0), pl.program_id(1)

    def put(delta):
        for p in range(PARTS):
            rows = pl.ds(pl.multiple_of((place[0] ^ p) * PIECE, PIECE), PIECE)
            out_ref[0, 0, rows, :] = delta[p * PIECE : (p + 1) * PIECE].astype(BF16)

    @pl.when(kind == 0)
    def _():
        put(rows_tn(b_ref[...], eu_ref[...]))

    for span, h_ref in enumerate(h_refs):

        @pl.when(jnp.logical_and(kind == 1, jnp.logical_or(len(h_refs) == 1, j == span)))
        def _(h_ref=h_ref):
            put(rows_tn(h_ref[...], eb_ref[...]))


def feed_weights(place, eu, h, b, eb, first):
    rows = b.shape[0]
    fixed = pl.BlockSpec((rows, D), lambda j, kind, place: (0, 0))
    moving = pl.BlockSpec((rows, D), lambda j, kind, place: (0, 2 * j + first))
    hidden = [moving]
    if len(h) == 2:
        hidden = [pl.BlockSpec((rows, D), lambda j, kind, place: (0, first))] * 2
    return pl.pallas_call(
        feed_weights_kernel,
        grid_spec=pltpu.PrefetchScalarGridSpec(
            num_scalar_prefetch=1,
            grid=(2, 2),
            in_specs=[moving] + hidden + [fixed, fixed],
            out_specs=pl.BlockSpec((1, 1, D, D), lambda j, kind, place: (j, kind, 0, 0)),
        ),
        out_shape=jax.ShapeDtypeStruct((2, 2, D, D), BF16),
        compiler_params=pltpu.CompilerParams(vmem_limit_bytes=ROOM),
        cost_estimate=cost(rows, 4, 6),
        name="feed_weights",
    )(place, eu, *h, b, eb)


def turn_back_kernel(
    meta, side, encoded, gain, context, returned, radar_part, cotangent, out, gain_out
):
    cut = context.shape[0]

    @pl.when(side[0] == 1)
    def _():
        out[:cut] = returned[...].astype(F32)
        out[cut:] = radar_part[...]
        gain_out[...] = jnp.zeros_like(gain_out)

    @pl.when(side[0] == 0)
    def _():
        total = jnp.zeros_like(gain_out)
        for part, incoming in enumerate((context, returned)):
            rows = slice(part * cut, (part + 1) * cut)
            delta, gain_part = norm_back(encoded[rows], gain[...], incoming[...].astype(F32))
            total = total + gain_part
            out[rows] = delta
        gain_out[...] = total

        def one_image(i, carry):
            rows = pl.ds(pl.multiple_of(i * SLOTS, 8), SLOTS)
            seen = lax.broadcasted_iota(jnp.int32, (SLOTS, 1), 0) < meta[3 + i]
            out[rows] += jnp.where(seen, cotangent[i].astype(F32), 0.0)
            return carry

        lax.fori_loop(0, cotangent.shape[0], one_image, 0)


def turn_back(meta, modality, encoded, gain, context, returned, radar_part, cotangent):
    return pl.pallas_call(
        turn_back_kernel,
        in_specs=[SCALARS] * 2 + [WHOLE] * 6,
        out_specs=[WHOLE] * 2,
        out_shape=[
            jax.ShapeDtypeStruct(encoded.shape, F32),
            jax.ShapeDtypeStruct((1, D), F32),
        ],
        compiler_params=pltpu.CompilerParams(vmem_limit_bytes=ROOM),
        cost_estimate=cost(816, 5, 0),
        name="turn_back",
    )(meta, modality[None], encoded, gain, context, returned, radar_part, cotangent)


def relative_parts(parts, own):
    return jnp.stack(
        [lax.dynamic_index_in_dim(parts, r ^ own, 0, keepdims=False) for r in range(PARTS)]
    )


def pack_mix(triple, out_weight):
    return jnp.concatenate([triple.transpose(1, 2, 0), out_weight[None]], 0)


def piece_of(quarter, part):
    if quarter.shape[1] == PIECE:
        return lax.dynamic_index_in_dim(quarter, part, 0, keepdims=False)
    return lax.dynamic_slice_in_dim(quarter, part * PIECE, PIECE, 1)


def unpack_mix(parts):
    return parts[:3].transpose(2, 0, 1).astype(F32), parts[3].astype(F32)


def unpack_feed_kernel(place, *refs):
    refs, (expand_ref, reduce_ref) = refs[:-2], refs[-2:]
    step = PIECE // 2
    for n in range(len(refs) // 5):

        @pl.when(pl.program_id(0) == n)
        def _(n=n):
            part, low, high, low_far, high_far = refs[5 * n : 5 * n + 5]
            for kind, out in enumerate((expand_ref, reduce_ref)):
                lows = [part[kind, :step], low[kind], low_far[0, kind], low_far[1, kind]]
                highs = [part[kind, step:], high_far[0, kind], high[kind], high_far[1, kind]]
                for p in range(PARTS):
                    start = pl.multiple_of((place[0] ^ p) * PIECE, PIECE)
                    out[0, pl.ds(start, step), :] = lows[p].astype(F32)
                    out[0, pl.ds(start + step, step), :] = highs[p].astype(F32)


def unpack_feed(place, *gathered):
    count = len(gathered)
    operands = [piece for pieces in gathered for piece in pieces]
    if count == 1:
        out = pl.BlockSpec((1, D, D), lambda n, place: (n, 0, 0))
    else:
        out = pl.BlockSpec((1, D, D), lambda n, place: (n ^ place[2], 0, 0))
    shape = jax.ShapeDtypeStruct((count, D, D), F32)
    return pl.pallas_call(
        unpack_feed_kernel,
        grid_spec=pltpu.PrefetchScalarGridSpec(
            num_scalar_prefetch=1,
            grid=(count,),
            in_specs=[WHOLE] * len(operands),
            out_specs=[out, out],
        ),
        out_shape=[shape, shape],
        compiler_params=pltpu.CompilerParams(vmem_limit_bytes=ROOM),
        cost_estimate=cost(816, 1, 2 * count),
        name="unpack_feed",
    )(place, *operands)


def fetch_relayed(zero, three):
    return (zero, swap(zero, dp_mask=1), swap(zero, dp_mask=2), three)


def fetch_beside(pieces):
    return pieces + tuple(swap(piece, head_mask=CORE) for piece in pieces)


AXES = {"x": (0, 0, ACROSS), "y": (3, 1, 0), "z": (2, 2, 0)}
THIRDS = ("xyz", "yxz", "zxy")
HALVES = ("xyz", "yzx")
LAST = ("xyz", "yxz")


def halves(array, axis):
    return lax.slice_in_dim(array, 0, 1, axis=axis), lax.slice_in_dim(array, 1, 2, axis=axis)


def add_split(keep, beside, orders=THIRDS):
    kinds, rows = keep.shape[1:3]
    kinds, rows = (1, rows) if kinds == PARTS else (kinds, rows // PARTS)
    total = (keep + beside).reshape(2, kinds, 2, 2, rows, D)
    step = PIECE // len(orders)
    cuts = [i * step for i in range(len(orders))] + [rows]
    return [total[:, :, :, :, low:high] for low, high in zip(cuts[:-1], cuts[1:])]


def link_send(shares, stage, orders=THIRDS):
    out = []
    for array, order in zip(shares, orders, strict=True):
        axis, dp_mask, head_mask = AXES[order[stage]]
        keep, sent = halves(array, axis)
        out.append((keep, swap(sent, dp_mask, head_mask)))
    return out


def link_next(pairs, stage, orders=THIRDS):
    def split(pairs):
        return [
            halves(keep + received, AXES[order[stage]][0])
            for (keep, received), order in zip(pairs, orders, strict=True)
        ]

    return [
        (keep, swap(sent, *AXES[order[stage]][1:]))
        for (keep, sent), order in zip(glue(split, pairs), orders, strict=True)
    ]


def link_add(pairs):
    return [keep + received for keep, received in pairs]


def join(shares):
    return jnp.concatenate([share[0, :, 0, 0] for share in shares], 1)


def rest_send(array, stop):
    mask = PARTS
    while 2 * mask < stop:
        array = array + swap(array, dp_mask=mask)
        mask *= 2
    return array, swap(array, dp_mask=mask)


def rest_add(pair):
    return pair[0] + pair[1]


def over_rest(array, stop):
    mask = PARTS
    while mask < stop:
        array = array + swap(array, dp_mask=mask)
        mask *= 2
    return array


def gather_first(part):
    step = PIECE // 2
    return part, swap(part[:, :step], dp_mask=1), swap(part[:, step:PIECE], dp_mask=2)


def gather_second(first):
    part, low, high = first
    step = PIECE // 2
    return (
        part,
        low,
        high,
        swap(jnp.stack([part[:, :step], low]), dp_mask=2),
        swap(jnp.stack([part[:, step:PIECE], high]), dp_mask=1),
    )


def gather_join(pieces):
    part, low, high, low_far, high_far = pieces
    step = PIECE // 2
    lows = [part[:, :step], low, low_far[0], low_far[1]]
    highs = [part[:, step:PIECE], high_far[0], high, high_far[1]]
    return jnp.stack([jnp.concatenate(pair, 1) for pair in zip(lows, highs, strict=True)])


def on_device(
    tokens,
    cotangent,
    ratios,
    patch_index,
    encoder_gains,
    encoder_attend_in,
    encoder_attend_out,
    encoder_expand,
    encoder_reduce,
    uniting_gains,
    uniting_query,
    uniting_pair,
    uniting_attend_out,
    uniting_expand,
    uniting_reduce,
):
    groups = lax.axis_size("dp")
    side = groups // 2
    group, lane = lax.axis_index("dp"), lax.axis_index("head")
    radar = group >= side
    modality = radar.astype(jnp.int32)
    own = group % PARTS
    images = tokens.shape[0]
    some = images // 2
    cut = some * SLOTS

    def select_slot(stacked):
        return lax.dynamic_index_in_dim(stacked, modality, 0, keepdims=False)

    gains = select_slot(encoder_gains)[:, None]
    uni_gains = uniting_gains[:, None]

    own_ratios = lax.dynamic_slice_in_dim(ratios, lane * images, images, 0)
    patches = lax.dynamic_slice_in_dim(patch_index, lane * images, images, 0)
    counts = PATCHES * (100 - own_ratios) // 100
    first = modality * some
    meta = jnp.concatenate([jnp.stack([own, lane, 0 * first]), counts])
    pair_meta = jnp.concatenate([jnp.stack([own, lane, first]), counts])
    place = jnp.stack([own, lane, modality])
    visible = (jnp.arange(SLOTS)[None, :] < counts[:, None])[:, :, None]
    queries = patches[:, None, :]
    row_gap = (patches // GRID)[:, :, None] - queries // GRID
    col_gap = (patches % GRID)[:, :, None] - queries % GRID
    distance = jnp.sqrt((row_gap * row_gap + col_gap * col_gap).astype(F32))
    per_lane = HEADS // lax.axis_size("head")
    heads = jnp.concatenate(
        [(lane ^ mask) * per_lane + jnp.arange(per_lane) for mask in range(4)]
    )
    slopes = 2.0 ** (-8.0 * (heads.astype(F32) + 1.0) / HEADS)

    mix_quarter = pack_mix(select_slot(encoder_attend_in), select_slot(encoder_attend_out))
    mix_zero = swap(piece_of(mix_quarter, own), head_mask=ACROSS)
    mix_near = (mix_quarter, swap(mix_quarter, head_mask=CORE))
    mix_quarter, encoder_expand, encoder_reduce = tie(
        mix_quarter, encoder_expand, encoder_reduce
    )
    feed_quarter = jnp.stack([select_slot(encoder_expand), select_slot(encoder_reduce)])
    feed_quarter, mix_quarter, mix_zero, flat, uni_feed_quarter = tie(
        feed_quarter,
        mix_quarter,
        mix_zero,
        tokens.reshape(-1, D),
        jnp.stack([uniting_expand, uniting_reduce]),
    )
    mix_pieces = fetch_relayed(
        mix_zero, swap(piece_of(mix_quarter, own ^ 3), head_mask=ACROSS)
    )
    feed_zero = swap(piece_of(feed_quarter, own), head_mask=ACROSS)
    feed_near = (feed_quarter, swap(feed_quarter, head_mask=CORE))

    normed_one, middle, *near = mix_forward(
        meta, slopes, flat, None, gains[0], None, mix_near, distance
    )
    middle, mix_pieces, feed_zero, feed_near = tie(middle, mix_pieces, feed_zero, feed_near)
    feed_quarter = feed_near[0]
    mix_far = fetch_beside(mix_pieces)
    feed_pieces = fetch_relayed(
        feed_zero, swap(piece_of(feed_quarter, own ^ 3), head_mask=ACROSS)
    )
    feed_zero, uniting_query, uniting_pair, uniting_attend_out = tie(
        feed_zero, uniting_query, uniting_pair, uniting_attend_out
    )
    uni_quarter = pack_mix(
        jnp.concatenate([uniting_query[:, None], uniting_pair], 1), uniting_attend_out
    )
    middle, mix_far, uni_feed_quarter = tie(middle, mix_far, uni_feed_quarter)
    uni_feed = (lax.all_gather(uni_feed_quarter, "head"),)
    middle, *far = mix_forward(
        meta, slopes, middle, None, None, normed_one, mix_far, distance, HEADS // 2
    )
    qkv, mixed, lse = zip(near, far)
    middle, feed_pieces, uni_quarter = tie(middle, feed_pieces, uni_quarter)
    feed_far = fetch_beside(feed_pieces)
    uni_zero = swap(piece_of(uni_quarter, own), head_mask=ACROSS)
    uni_three = swap(piece_of(uni_quarter, own ^ 3), head_mask=ACROSS)
    enc_mix, enc_feed = mix_near + mix_far, feed_near + feed_far

    *half_fed, leaving = feed_rows(place, middle, gains[1], uni_gains[0], enc_feed)
    leaving, half_fed, uni_zero = tie(leaving, half_fed, uni_zero)
    received = swap(leaving, dp_mask=side)
    uni_mix_pieces = fetch_relayed(uni_zero, uni_three)
    uni_mix_near = (uni_quarter, swap(uni_quarter, head_mask=CORE))
    encoded, normed_two, *stored, context = feed_rows(
        place, middle, gains[1], uni_gains[0], enc_feed, half_fed
    )
    hidden, bend = ([part] for part in stored)
    encoded, received, uni_mix_pieces = tie(encoded, received, uni_mix_pieces)
    uni_mix = uni_mix_near + fetch_beside(uni_mix_pieces)
    received, cotangent = tie(received, cotangent)
    sent_cotangent = swap(cotangent[:some], dp_mask=side)
    radar_rows = jnp.where(radar, encoded[cut:], received.astype(F32))
    context_rows = jnp.where(radar, received, context)

    uni_normed, uni_middle, *stored = mix_forward(
        pair_meta, slopes, radar_rows, context_rows, uni_gains[1], None, uni_mix, distance
    )
    uni_qkv, uni_mixed, uni_lse = ([part] for part in stored)
    uni_normed_two, joined, *stored = feed_forward(
        meta, uni_middle, uni_gains[2], None, uni_feed
    )
    uni_hidden, uni_bend = ([part] for part in stored)

    joined, sent_cotangent = tie(joined, sent_cotangent)
    joined_half = joined.astype(BF16).reshape(some, SLOTS, D)
    other_half = [swap(joined_half[i : i + 1], dp_mask=side) for i in range(some)]
    pair_cotangent = jnp.where(radar, cotangent[some:], sent_cotangent)
    pair_visible = lax.dynamic_slice_in_dim(visible, first, some, 0)
    delta_joined = jnp.where(pair_visible, pair_cotangent, 0).astype(F32).reshape(-1, D)
    delta_middle, gain_three, eb, eu = feed_back(
        meta, delta_joined, uni_middle, uni_gains[2], uni_bend, uni_feed
    )
    eu, other_half[0] = tie(eu, other_half[0])
    sent = feed_weights(place, eu, uni_hidden, uni_normed_two, eb, 1)
    sent, eu, other_half[1] = tie(sent, eu, other_half[1])
    beside = swap(sent, head_mask=CORE)
    keep = feed_weights(place, eu, uni_hidden, uni_normed_two, eb, 0)
    keep, beside = tie(keep, beside)
    uni_feed_sum, delta_middle = tie(add_split(keep, beside), delta_middle)
    uni_feed_pairs = link_send(uni_feed_sum, 0)
    delta_radar, gain_two, dqkv, mix_eb, delta_context = mix_back(
        pair_meta,
        slopes,
        delta_middle,
        radar_rows,
        uni_gains[1],
        uni_qkv,
        uni_lse,
        uni_mix,
        distance,
        True,
    )
    leaving = jnp.where(radar, delta_context, delta_radar.astype(BF16))
    leaving, dqkv, uni_feed_pairs, other_half = tie(leaving, dqkv, uni_feed_pairs, other_half)
    other_half = jnp.concatenate(other_half, 0)
    returned = swap(leaving, dp_mask=side)
    uni_feed_pairs = link_next(uni_feed_pairs, 1)
    keep, sent = mix_weights(place, dqkv, uni_mixed, uni_normed, context_rows, mix_eb)
    layer_output = jnp.where(
        visible,
        jnp.where(
            radar,
            jnp.concatenate([other_half, joined_half], 0),
            encoded.astype(BF16).reshape(images, SLOTS, D),
        ),
        0,
    )
    sent, returned, uni_feed_pairs, layer_output = tie(
        sent, returned, uni_feed_pairs, layer_output
    )
    beside = swap(sent, head_mask=CORE)
    uni_feed_pairs = link_send(link_add(uni_feed_pairs), 2)
    delta_encoded, gain_one = turn_back(
        meta, modality, encoded, uni_gains[0], delta_context, returned, delta_radar, cotangent
    )
    delta_encoded, beside, uni_feed_pairs = tie(delta_encoded, beside, uni_feed_pairs)
    uni_mix_sum, uni_feed_part = add_split(keep, beside, HALVES), join(link_add(uni_feed_pairs))
    delta_encoded, uni_mix_sum, uni_feed_part = tie(delta_encoded, uni_mix_sum, uni_feed_part)
    uni_feed_rest = rest_send(uni_feed_part, groups)
    uni_mix_pairs = link_send(uni_mix_sum, 0, HALVES)

    delta_middle, gain_b, eb, eu = feed_back(
        meta, delta_encoded, middle, gains[1], bend, enc_feed
    )
    eu, uni_mix_pairs = tie(eu, uni_mix_pairs)
    uni_mix_sum, eu = tie(link_add(uni_mix_pairs), eu)
    uni_mix_pairs = link_send(uni_mix_sum, 1, HALVES)
    sent = feed_weights(place, eu, hidden, normed_two, eb, 1)
    sent, eu, uni_feed_rest, uni_mix_pairs = tie(sent, eu, uni_feed_rest, uni_mix_pairs)
    uni_feed_part, uni_mix_sum = rest_add(uni_feed_rest), link_add(uni_mix_pairs)
    eu, uni_feed_part, uni_mix_sum = tie(eu, uni_feed_part, uni_mix_sum)
    beside = swap(sent, head_mask=CORE)
    uni_feed_near = swap(uni_feed_part, dp_mask=1)
    uni_mix_pairs = link_send(uni_mix_sum, 2, HALVES)
    keep = feed_weights(place, eu, hidden, normed_two, eb, 0)
    keep, beside, uni_feed_near, uni_mix_pairs = tie(keep, beside, uni_feed_near, uni_mix_pairs)
    uni_feed_near = jnp.stack([uni_feed_part, uni_feed_near])
    enc_feed_sum, uni_mix_part = add_split(keep, beside, HALVES), join(link_add(uni_mix_pairs))
    delta_middle, enc_feed_sum, uni_mix_part, uni_feed_near = tie(
        delta_middle, enc_feed_sum, uni_mix_part, uni_feed_near
    )
    enc_feed_pairs = link_send(enc_feed_sum, 0, HALVES)
    uni_mix_rest = rest_send(uni_mix_part, groups)
    uni_feed_far = swap(uni_feed_near, dp_mask=2)
    delta_inputs, gain_a, dqkv, eb = mix_back(
        meta, slopes, delta_middle, flat, gains[0], qkv, lse, enc_mix, distance, False
    )
    dqkv, enc_feed_pairs, uni_mix_rest, uni_feed_far = tie(
        dqkv, enc_feed_pairs, uni_mix_rest, uni_feed_far
    )
    enc_feed_sum, uni_mix_part = link_add(enc_feed_pairs), rest_add(uni_mix_rest)
    dqkv, enc_feed_sum, uni_mix_part = tie(dqkv, enc_feed_sum, uni_mix_part)
    enc_feed_pairs = link_send(enc_feed_sum, 1, HALVES)
    uni_mix_gather = gather_first(uni_mix_part)

    totals = (gain_a, gain_b, gain_one, gain_two, gain_three)
    keep, sent = mix_weights(place, dqkv, mixed, normed_one, normed_one, eb, totals)
    sent, enc_feed_pairs, uni_mix_gather = tie(sent, enc_feed_pairs, uni_mix_gather)
    beside = swap(sent, head_mask=CORE)
    enc_feed_pairs = link_send(link_add(enc_feed_pairs), 2, HALVES)
    enc_mix_pairs = link_send(add_split(keep, beside, LAST), 0, LAST)
    feed_part = over_rest(join(link_add(enc_feed_pairs)), side)
    feed_other = swap(feed_part, dp_mask=side)
    enc_mix_pairs, feed_part = tie(enc_mix_pairs, feed_part)
    enc_mix_pairs = link_send(link_add(enc_mix_pairs), 1, LAST)
    feed_gather = gather_first(feed_part)
    enc_mix_pairs = link_send(link_add(enc_mix_pairs), 2, LAST)
    enc_mix_pairs, feed_gather = tie(enc_mix_pairs, feed_gather)
    feed_gather = gather_second(feed_gather)
    enc_mix_pairs, feed_other = tie(enc_mix_pairs, feed_other)
    mix_part = over_rest(join(link_add(enc_mix_pairs)), side)
    mix_part, feed_other = tie(mix_part, feed_other)
    mix_other = swap(mix_part, dp_mask=side)
    feed_other_gather = gather_first(feed_other)
    feed_gather, uni_feed_near = tie(feed_gather, uni_feed_near)
    uni_feed_all = relative_parts(jnp.concatenate([uni_feed_near, uni_feed_far], 0), own)
    fexpand, freduce = (uni_feed_all[:, i].reshape(D, D).astype(F32) for i in range(2))
    mix_other, feed_other_gather, feed_gather, uni_mix_gather, fexpand, freduce = tie(
        mix_other, feed_other_gather, feed_gather, uni_mix_gather, fexpand, freduce
    )
    mix_gather = gather_first(jnp.concatenate([mix_part, mix_other], 0))
    feed_other_gather = gather_second(feed_other_gather)
    mix_gather, uni_mix_gather = tie(mix_gather, uni_mix_gather)
    mix_gather, uni_mix_gather = gather_second(mix_gather), gather_second(uni_mix_gather)
    totals = (mix_part + mix_other)[0, PIECE:].astype(F32)

    ftriple, fout = unpack_mix(relative_parts(gather_join(uni_mix_gather)[:, 0], own))
    expands, reduces = unpack_feed(place, feed_gather, feed_other_gather)
    mix_all = gather_join(mix_gather)
    mine, theirs = mix_all[:, 0], mix_all[:, 1]
    mixes = [
        unpack_mix(relative_parts(part, own))
        for part in (jnp.where(radar, theirs, mine), jnp.where(radar, mine, theirs))
    ]

    return (
        layer_output,
        delta_inputs.reshape(images, SLOTS, D),
        totals[:4].reshape(2, 2, D),
        jnp.stack([mixes[0][0], mixes[1][0]]),
        jnp.stack([mixes[0][1], mixes[1][1]]),
        expands,
        reduces,
        totals[4:7],
        ftriple[:, 0],
        ftriple[:, 1:],
        fout,
        fexpand,
        freduce,
    )


def solution(mesh):
    return jax.shard_map(
        on_device,
        mesh=mesh,
        in_specs=(
            P(("dp", "head"), None, None),
            P(("dp", "head"), None, None),
            P("dp"),
            P("dp", None),
            P(),
            P(None, None, None, "head"),
            P(None, "head", None),
            P(None, None, "head"),
            P(None, "head", None),
            P(),
            P(None, "head"),
            P(None, None, "head"),
            P("head", None),
            P(None, "head"),
            P("head", None),
        ),
        out_specs=(
            P(("dp", "head"), None, None),
            P(("dp", "head"), None, None),
            P(),
            P(None, None, None, "head"),
            P(None, "head", None),
            P(None, None, "head"),
            P(None, "head", None),
            P(),
            P(None, "head"),
            P(None, None, "head"),
            P("head", None),
            P(None, "head"),
            P("head", None),
        ),
        check_vma=False,
    )
```

```python
import functools

import jax
import jax.numpy as jnp
from jax import lax
from jax.experimental import pallas as pl
from jax.experimental.pallas import tpu as pltpu
from jax.sharding import PartitionSpec as P

D = 768
HEADS = 12
HEAD_DIM = 64
GRID = 15
PATCHES = 225
SLOTS = 136
PARTS = 4
PIECE = D // PARTS
CORE, ACROSS = 1, 2
SCALE = HEAD_DIM**-0.5

EPSILON = 1e-06
NEGATIVE = -1e30
F32, BF16 = jnp.float32, jnp.bfloat16
WHOLE = pl.BlockSpec(memory_space=pltpu.VMEM)
ANYWHERE = pl.BlockSpec(memory_space=pl.ANY)
SCALARS = pl.BlockSpec(memory_space=pltpu.SMEM)
ROOM = 56 << 20


def cost(rows, fixed, each):
    return pl.CostEstimate(
        flops=int((fixed + each * rows / 816) * 1e7), bytes_accessed=1, transcendentals=0
    )


def swap(array, dp_mask=0, head_mask=0, senders=None):
    groups, lanes = lax.axis_size("dp"), lax.axis_size("head")
    pairs = [
        (g * lanes + h, (g ^ dp_mask) * lanes + (h ^ head_mask))
        for g in (range(groups) if senders is None else senders)
        for h in range(lanes)
    ]
    return lax.ppermute(array, ("dp", "head"), pairs)


def tie(*arrays):
    return lax.optimization_barrier(arrays)


def rows_nt(left, right):
    return lax.dot_general(left, right, (((1,), (1,)), ((), ())), preferred_element_type=F32)


def rows_nn(left, right):
    return lax.dot_general(left, right, (((1,), (0,)), ((), ())), preferred_element_type=F32)


def rows_tn(left, right):
    return lax.dot_general(left, right, (((0,), (0,)), ((), ())), preferred_element_type=F32)


def normalize(values):
    centered = values - jnp.mean(values, -1, keepdims=True)
    spread = lax.rsqrt(jnp.mean(centered * centered, -1, keepdims=True) + EPSILON)
    return centered * spread, spread


def layer_norm(values, gain):
    return normalize(values)[0] * gain


def norm_back(values, gain, incoming):
    unit, spread = normalize(values)
    scaled = incoming * gain
    delta = spread * (
        scaled
        - jnp.mean(scaled, -1, keepdims=True)
        - unit * jnp.mean(scaled * unit, -1, keepdims=True)
    )
    return delta, jnp.sum(incoming * unit, 0, keepdims=True)


def glue(function, *arrays):
    leaves, tree = jax.tree.flatten(arrays)
    results, result_tree = jax.tree.flatten(jax.eval_shape(function, *arrays))

    def kernel(*refs):
        values = tree.unflatten([ref[...] for ref in refs[: len(leaves)]])
        for ref, value in zip(refs[len(leaves) :], jax.tree.leaves(function(*values))):
            ref[...] = value

    out = pl.pallas_call(
        kernel,
        in_specs=[WHOLE] * len(leaves),
        out_specs=[WHOLE] * len(results),
        out_shape=results,
        compiler_params=pltpu.CompilerParams(vmem_limit_bytes=ROOM),
        cost_estimate=cost(816, 1, 0),
        name="glue",
    )(*leaves)
    return result_tree.unflatten(out)


def chunks_of(rows):
    step = 2 * SLOTS if rows % (2 * SLOTS) == 0 else rows
    return [slice(start, start + step) for start in range(0, rows, step)]


QUARTERS_IN = {1: 4, 2: 2, 8: 2, 10: 4}


def feed_copies(pieces, meta, room, sems):
    if len(pieces) == 1:
        return [
            [pltpu.make_async_copy(pieces[0].at[meta[1] ^ q], room.at[q], sems.at[q])]
            for q in range(4)
        ]
    near = len(pieces) % 8
    copies = [
        [pltpu.make_async_copy(pieces[q], room.at[q], sems.at[q])] for q in range(near)
    ]
    for q in range(near, near + (len(pieces) - near) // PARTS):
        group = []
        for r in range(PARTS):
            at = near + (q - near) * PARTS + r
            rows = pl.ds(pl.multiple_of((meta[0] ^ r) * PIECE, PIECE), PIECE)
            group.append(
                pltpu.make_async_copy(pieces[at], room.at[q, :, rows, :], sems.at[at])
            )
        copies.append(group)
    return copies


def mix_copies(pieces, meta, room, sems):
    near = len(pieces) % 8
    copies = [
        pltpu.make_async_copy(
            pieces[q], room.at[:, pl.ds(q * PIECE, PIECE), :], sems.at[q]
        )
        for q in range(near)
    ]
    for at in range(near, len(pieces)):
        q, r = divmod(at - near, PARTS)
        rows = pl.ds((near + q) * PIECE, PIECE)
        copies.append(
            pltpu.make_async_copy(pieces[at], room.at[meta[0] ^ r, rows, :], sems.at[at])
        )
    return copies


SIZES = (64, 96, 128, SLOTS)


def by_size(count, branch):
    which = sum((count > size).astype(jnp.int32) for size in SIZES[:-1])
    lax.switch(which, [functools.partial(branch, size) for size in SIZES])


def two_heads(block, first):
    zero = jnp.zeros_like(block)
    return jnp.concatenate(
        [jnp.where(first, block, zero), jnp.where(first, zero, block)], 0
    ).astype(BF16)


def pick_heads(stacked, first):
    size = stacked.shape[0] // 2
    return jnp.where(first, stacked[:size], stacked[size:])


def image_setup(size, distance_ref, image, count):
    first = lax.broadcasted_iota(jnp.int32, (size, 2 * HEAD_DIM), 1) < HEAD_DIM
    distance = distance_ref[image, :size, :size]
    distance = jnp.concatenate([distance, distance], 1)
    seen = lax.broadcasted_iota(jnp.int32, (size, 1), 0) < count
    lanes = lax.broadcasted_iota(jnp.int32, (1, 2 * size), 1) < size

    def scores_of(keys, queries, slopes, head):
        slope = jnp.where(lanes, slopes[head], slopes[head + 1])
        return jnp.where(seen, rows_nt(keys, queries) - distance * slope, NEGATIVE)

    return first, scores_of


def mix_forward_kernel(local, cross, images, head, n_pieces, *refs):
    meta, slopes, x_ref = refs[:3]
    refs = refs[3:]
    if cross:
        c_ref, refs = refs[0], refs[1:]
    if local:
        gain_ref, refs = refs[0], refs[1:]
    else:
        a_ref, refs = refs[0], refs[1:]
    pieces, refs = refs[:n_pieces], refs[n_pieces:]
    distance_ref, refs = refs[0], refs[1:]
    if local:
        a_ref, refs = refs[0], refs[1:]
    out_ref, qkv_ref, o_ref, lse_ref, room, wide, sems = refs
    copies = mix_copies(pieces, meta, room, sems)
    for copy in copies:
        copy.start()
    chunks = chunks_of(images * SLOTS)
    if local:
        for rows in chunks:
            a_ref[rows, :] = layer_norm(x_ref[rows, :].astype(F32), gain_ref[...]).astype(BF16)
    for copy in copies:
        copy.wait()
    width = o_ref.shape[1]
    if cross:
        wide[:, :width] = rows_nt(a_ref[...], room[0])
        wide[:, width:] = rows_nt(c_ref[...], room[1:3].reshape(2 * width, D))
    else:
        wide[...] = rows_nt(a_ref[...], room[:3].reshape(3 * width, D))

    def one_image(i, carry):
        image = meta[2] + i
        start = pl.multiple_of(i * SLOTS, 8)
        qkv_ref[i] = wide[pl.ds(start, SLOTS), :].astype(BF16)

        def work(size):
            first, scores_of = image_setup(size, distance_ref, image, meta[3 + image])
            rows = pl.ds(start, size)
            for pair in range(width // (2 * HEAD_DIM)):
                low, high = pair * 2 * HEAD_DIM, (pair + 1) * 2 * HEAD_DIM
                k = wide[rows, width + low : width + high].astype(BF16)
                v = wide[rows, 2 * width + low : 2 * width + high].astype(BF16)
                queries = two_heads(
                    wide[rows, low:high].astype(BF16).astype(F32) * SCALE, first
                )
                scores = scores_of(k, queries, slopes, head + 2 * pair)
                top = jnp.max(scores, 0, keepdims=True)
                exponent = jnp.exp(scores - top)
                total = jnp.sum(exponent, 0, keepdims=True)
                weights = (exponent * (1.0 / total)).astype(BF16)
                wide[rows, low:high] = pick_heads(rows_tn(weights, v), first)
                lse_ref[i, pair : pair + 1, : 2 * size] = top + jnp.log(total)
            if size < SLOTS:
                rest = pl.ds(pl.multiple_of(start + size, 8), SLOTS - size)
                wide[rest, :width] = jnp.zeros((SLOTS - size, width), F32)

        by_size(meta[3 + image], work)
        return carry

    lax.fori_loop(0, images, one_image, 0)
    for rows in chunks:
        o_ref[rows, :] = wide[rows, :width].astype(BF16)
    out_ref[...] = x_ref[...].astype(F32) + rows_nn(o_ref[...], room[3])


def mix_forward(meta, slopes, x, context, gain, normed, pieces, distance, head=0):
    images = x.shape[0] // SLOTS
    rows = images * SLOTS
    cross, local = context is not None, normed is None
    width = PIECE * QUARTERS_IN[len(pieces)]
    operands = [meta, slopes, x] + ([context] if cross else [])
    operands += [gain if local else normed, *pieces, distance]
    specs = [SCALARS] * 2 + [WHOLE] * (3 if cross else 2) + [ANYWHERE] * len(pieces) + [WHOLE]
    narrow = jax.ShapeDtypeStruct((rows, D), BF16)
    return pl.pallas_call(
        functools.partial(mix_forward_kernel, local, cross, images, head, len(pieces)),
        in_specs=specs,
        out_specs=[WHOLE] * (5 if local else 4),
        out_shape=([narrow] if local else [])
        + [
            jax.ShapeDtypeStruct((rows, D), F32),
            jax.ShapeDtypeStruct((images, SLOTS, 3 * width), BF16),
            jax.ShapeDtypeStruct((rows, width), BF16),
            jax.ShapeDtypeStruct((images, width // (2 * HEAD_DIM), 2 * SLOTS), F32),
        ],
        scratch_shapes=[
            pltpu.VMEM((4, width, D), BF16),
            pltpu.VMEM((rows, 3 * width), F32),
            pltpu.SemaphoreType.DMA((16,)),
        ],
        compiler_params=pltpu.CompilerParams(vmem_limit_bytes=ROOM),
        cost_estimate=cost(rows, 4, 8 * width / 384),
        name="mix_forward",
    )(*operands)


def mix_back_kernel(cross, images, spans, *refs):
    meta, slopes, e_ref, x_ref, gain_ref = refs[:5]
    refs = refs[5:]
    qkv_refs, lse_refs, refs = refs[:spans], refs[spans : 2 * spans], refs[2 * spans :]
    pieces, refs = refs[:10], refs[10:]
    distance_ref, dx_ref, dgain_ref, dqkv_ref, eb_ref = refs[:5]
    refs = refs[5:]
    if cross:
        dc_ref, leaving_ref, refs = refs[0], refs[1], refs[2:]
    room, inner_ref, wide, sems = refs
    copies = mix_copies(pieces, meta, room, sems)
    for copy in copies:
        copy.start()
    chunks = chunks_of(images * SLOTS)
    for rows in chunks:
        eb_ref[rows, :] = e_ref[rows, :].astype(BF16)
    for copy in copies:
        copy.wait()
    inner_ref[...] = rows_nt(eb_ref[...], room[3])

    width = D // spans

    def one_image(i, carry):
        image = meta[2] + i
        start = pl.multiple_of(i * SLOTS, 8)

        def work(size):
            first, scores_of = image_setup(size, distance_ref, image, meta[3 + image])
            rows = pl.ds(start, size)
            for pair in range(HEADS // 2):
                low, high = pair * 2 * HEAD_DIM, (pair + 1) * 2 * HEAD_DIM
                half, inside = divmod(pair, HEADS // 2 // spans)
                qkv_ref, lse_ref = qkv_refs[half], lse_refs[half]
                at, to = inside * 2 * HEAD_DIM, (inside + 1) * 2 * HEAD_DIM
                queries = two_heads(qkv_ref[i, :size, at:to].astype(F32) * SCALE, first)
                incoming = two_heads(inner_ref[rows, low:high], first)
                k = qkv_ref[i, :size, width + at : width + to]
                v = qkv_ref[i, :size, 2 * width + at : 2 * width + to]
                scores = scores_of(k, queries, slopes, 2 * pair)
                probable = jnp.exp(scores - lse_ref[i, inside : inside + 1, : 2 * size])
                delta_p = rows_nt(v, incoming)
                shared = jnp.sum(delta_p * probable, 0, keepdims=True)
                delta_s = (probable * (delta_p - shared)).astype(BF16)
                wide[rows, low:high] = pick_heads(rows_tn(delta_s, k), first) * SCALE
                wide[rows, D + low : D + high] = rows_nn(delta_s, queries)
                wide[rows, 2 * D + low : 2 * D + high] = rows_nn(
                    probable.astype(BF16), incoming
                )
            if size < SLOTS:
                rest = pl.ds(pl.multiple_of(start + size, 8), SLOTS - size)
                wide[rest, :] = jnp.zeros((SLOTS - size, 3 * D), F32)

        by_size(meta[3 + image], work)
        return carry

    lax.fori_loop(0, images, one_image, 0)
    for rows in chunks:
        dqkv_ref[rows, :] = wide[rows, :].astype(BF16)
    delta = rows_nn(dqkv_ref[:, :D], room[0])
    side = rows_nn(dqkv_ref[:, D : 2 * D], room[1]) + rows_nn(dqkv_ref[:, 2 * D :], room[2])
    if cross:
        dc_ref[...] = side.astype(BF16)
        inner_ref[...] = delta
    else:
        inner_ref[...] = delta + side
    gain_total = jnp.zeros((1, D), F32)
    for rows in chunks:
        part, gain_part = norm_back(x_ref[rows, :].astype(F32), gain_ref[...], inner_ref[rows, :])
        dx_ref[rows, :] = e_ref[rows, :] + part
        gain_total = gain_total + gain_part
    dgain_ref[...] = gain_total
    if cross:

        @pl.when(meta[2] > 0)
        def _():
            leaving_ref[...] = dc_ref[...]

        @pl.when(meta[2] == 0)
        def _():
            leaving_ref[...] = dx_ref[...].astype(BF16)


def mix_back(meta, slopes, delta, x, gain, qkv, lse, pieces, distance, cross):
    images = qkv[0].shape[0]
    rows = images * SLOTS
    wide_rows = jax.ShapeDtypeStruct((rows, D), BF16)
    return pl.pallas_call(
        functools.partial(mix_back_kernel, cross, images, len(qkv)),
        in_specs=[SCALARS] * 2
        + [WHOLE] * (3 + 2 * len(qkv))
        + [ANYWHERE] * len(pieces)
        + [WHOLE],
        out_specs=[WHOLE] * (6 if cross else 4),
        out_shape=[
            jax.ShapeDtypeStruct((rows, D), F32),
            jax.ShapeDtypeStruct((1, D), F32),
            jax.ShapeDtypeStruct((rows, 3 * D), BF16),
            wide_rows,
        ]
        + ([wide_rows] * 2 if cross else []),
        scratch_shapes=[
            pltpu.VMEM((4, D, D), BF16),
            pltpu.VMEM((rows, D), F32),
            pltpu.VMEM((rows, 3 * D), F32),
            pltpu.SemaphoreType.DMA((16,)),
        ],
        compiler_params=pltpu.CompilerParams(vmem_limit_bytes=ROOM),
        cost_estimate=cost(rows, 5, 23),
        name="mix_back",
    )(meta, slopes, delta, x, gain, *qkv, *lse, *pieces, distance)


def mix_weights_kernel(more, place, dqkv_ref, *refs):
    if more:
        *refs, scratch = refs
        refs, outs = refs[:-2], refs[-2:]
        refs = (*refs, scratch)
    else:
        refs, outs = refs[:-2], refs[-2:]
    if more:
        gain_refs, refs, gains_ref = refs[:5], refs[5:-1], refs[-1]
    o_refs, (a_ref, c_ref, eb_ref) = refs[:-3], refs[-3:]
    kind = pl.program_id(0)

    def put(first, delta):
        for q in range(delta.shape[0] // PIECE):
            part = delta[q * PIECE : (q + 1) * PIECE].astype(BF16)
            outs[(first + q) % 2][(first + q) // 2, 0, :PIECE] = part

    @pl.when(kind == 0)
    def _():
        put(0, rows_tn(dqkv_ref[...], a_ref[...]))

    @pl.when(jnp.logical_or(kind == 1, kind == 2))
    def _():
        put(0, rows_tn(dqkv_ref[...], c_ref[...]))

    @pl.when(kind == 3)
    def _():
        for span, o_ref in enumerate(o_refs):
            put(span * 4 // len(o_refs), rows_tn(o_ref[...], eb_ref[...]))

    if more:
        gains_ref[...] = jnp.zeros_like(gains_ref)
        for i in range(2):
            gains_ref[pl.ds(2 * place[2] + i, 1), :] = gain_refs[i][...]
        for i in range(2, 5):
            gains_ref[2 + i : 3 + i, :] = gain_refs[i][...]
        for out in outs:
            for half in range(2):
                out[half, 0, PIECE:] = gains_ref[...].astype(BF16)


def mix_weights(place, dqkv, o, a, c, eb, gains=None):
    rows = a.shape[0]
    more = gains is not None
    fixed = pl.BlockSpec((rows, D), lambda kind, place: (0, 0))
    narrow = pl.BlockSpec((rows, D // len(o)), lambda kind, place: (0, 0))
    tall = PIECE + (16 if more else 0)
    out = pl.BlockSpec((2, 1, tall, D), lambda kind, place: (0, kind ^ place[0], 0, 0))
    shape = jax.ShapeDtypeStruct((2, PARTS, tall, D), BF16)
    return pl.pallas_call(
        functools.partial(mix_weights_kernel, more),
        grid_spec=pltpu.PrefetchScalarGridSpec(
            num_scalar_prefetch=1,
            grid=(4,),
            in_specs=[pl.BlockSpec((rows, D), lambda kind, place: (0, jnp.minimum(kind, 2)))]
            + [pl.BlockSpec((1, D), lambda kind, place: (0, 0))] * (5 if more else 0)
            + [narrow] * len(o)
            + [fixed] * 3,
            out_specs=[out, out],
            scratch_shapes=[pltpu.VMEM((16, D), F32)] if more else [],
        ),
        out_shape=[shape, shape],
        compiler_params=pltpu.CompilerParams(vmem_limit_bytes=ROOM),
        cost_estimate=cost(rows, 3.5, 7),
        name="mix_weights",
    )(place, dqkv, *(gains if more else []), *o, a, c, eb)


def fetch_quarter(step, copies):
    @pl.when(step == 0)
    def _():
        for group in copies[:2]:
            for copy in group:
                copy.start()

    for q, group in enumerate(copies):

        @pl.when(step == q)
        def _(q=q, group=group):
            for copy in group:
                copy.wait()
            for later in copies[q + 2 : q + 3]:
                for copy in later:
                    copy.start()


def feed_forward_kernel(local, n_pieces, meta, x_ref, norm_ref, *refs):
    pieces, refs = refs[:n_pieces], refs[n_pieces:]
    if local:
        b_ref, refs = refs[0], refs[1:]
    else:
        b_ref = norm_ref
    out_ref, h_ref, g_ref, room, sems, y_ref = refs
    step = pl.program_id(0)
    fetch_quarter(step, feed_copies(pieces, meta, room, sems))

    @pl.when(step == 0)
    def _():
        for rows in chunks_of(x_ref.shape[0]):
            values = x_ref[rows, :]
            y_ref[rows, :] = values
            if local:
                b_ref[rows, :] = layer_norm(values, norm_ref[...]).astype(BF16)

    before = rows_nn(b_ref[...], room[step, 0])
    bell = jnp.exp(-0.5 * before * before) * 0.3989422804014327
    share = 0.5 * (1.0 + lax.erf(before * 0.7071067811865476))
    h_ref[...] = (before * share).astype(BF16)
    g_ref[...] = (share + before * bell).astype(BF16)
    y_ref[...] += rows_nn(h_ref[...], room[step, 1])

    @pl.when(step == pl.num_programs(0) - 1)
    def _():
        out_ref[...] = y_ref[...].astype(BF16)


def feed_forward(meta, x, gain, normed, pieces):
    rows = x.shape[0]
    local = normed is None
    quarters = QUARTERS_IN[len(pieces)]
    fixed = pl.BlockSpec((rows, D), lambda q: (0, 0))
    moving = pl.BlockSpec((rows, D), lambda q: (0, q))
    hidden = jax.ShapeDtypeStruct((rows, quarters * D), BF16)
    return pl.pallas_call(
        functools.partial(feed_forward_kernel, local, len(pieces)),
        grid=(quarters,),
        in_specs=[SCALARS, fixed, pl.BlockSpec((1, D), lambda q: (0, 0)) if local else fixed]
        + [ANYWHERE] * len(pieces),
        out_specs=([fixed] if local else []) + [fixed, moving, moving],
        out_shape=([jax.ShapeDtypeStruct((rows, D), BF16)] if local else [])
        + [jax.ShapeDtypeStruct((rows, D), BF16), hidden, hidden],
        scratch_shapes=[
            pltpu.VMEM((quarters, 2, D, D), BF16),
            pltpu.SemaphoreType.DMA((16,)),
            pltpu.VMEM((rows, D), F32),
        ],
        compiler_params=pltpu.CompilerParams(vmem_limit_bytes=ROOM),
        cost_estimate=cost(rows, 3.6, 4 * quarters),
        name="feed_forward",
    )(meta, x, gain if local else normed, *pieces)


def feed_rows_kernel(leaving, meta, x_ref, gain_ref, next_gain_ref, *refs):
    pieces, refs = refs[:10], refs[10:]
    if not leaving:
        refs = refs[4:]
    y_ref, b_ref, h_ref, g_ref, out_ref, room, sems = refs
    step = pl.program_id(0)
    fetch_quarter(step, feed_copies(pieces, meta, room, sems))

    @pl.when(step == 0)
    def _():
        values = x_ref[...]
        y_ref[...] = values
        b_ref[...] = layer_norm(values, gain_ref[...]).astype(BF16)

    before = rows_nn(b_ref[...], room[step, 0])
    bell = jnp.exp(-0.5 * before * before) * 0.3989422804014327
    share = 0.5 * (1.0 + lax.erf(before * 0.7071067811865476))
    h_ref[...] = (before * share).astype(BF16)
    g_ref[...] = (share + before * bell).astype(BF16)
    y_ref[...] += rows_nn(h_ref[...], room[step, 1])

    @pl.when(jnp.logical_and(step == 3, jnp.logical_or(not leaving, meta[2] == 0)))
    def _():
        out_ref[...] = layer_norm(y_ref[...], next_gain_ref[...]).astype(BF16)

    if leaving:

        @pl.when(jnp.logical_and(step == 3, meta[2] == 1))
        def _():
            out_ref[...] = y_ref[...].astype(BF16)


def feed_rows(place, x, gain, next_gain, pieces, first=None):
    rows = x.shape[0] // 2
    leaving = first is None

    def block(place):
        return 1 - place[2] if leaving else place[2]

    fixed = pl.BlockSpec((rows, D), lambda q, place: (block(place), 0))
    moving = pl.BlockSpec((rows, D), lambda q, place: (block(place), q))
    narrow = pl.BlockSpec((1, D), lambda q, place: (0, 0))
    hidden = jax.ShapeDtypeStruct((2 * rows, 4 * D), BF16)
    return pl.pallas_call(
        functools.partial(feed_rows_kernel, leaving),
        grid_spec=pltpu.PrefetchScalarGridSpec(
            num_scalar_prefetch=1,
            grid=(4,),
            in_specs=[fixed, narrow, narrow] + [ANYWHERE] * (10 if leaving else 14),
            out_specs=[fixed, fixed, moving, moving]
            + [pl.BlockSpec((rows, D), lambda q, place: (0, 0))],
            scratch_shapes=[pltpu.VMEM((4, 2, D, D), BF16), pltpu.SemaphoreType.DMA((16,))],
        ),
        out_shape=[
            jax.ShapeDtypeStruct((2 * rows, D), F32),
            jax.ShapeDtypeStruct((2 * rows, D), BF16),
            hidden,
            hidden,
            jax.ShapeDtypeStruct((rows, D), BF16),
        ],
        input_output_aliases={} if leaving else {14 + i: i for i in range(4)},
        compiler_params=pltpu.CompilerParams(vmem_limit_bytes=ROOM),
        cost_estimate=cost(rows, 3.6, 16),
        name="feed_rows",
    )(place, x, gain, next_gain, *pieces, *([] if leaving else first))


def feed_back_kernel(n_pieces, meta, e_ref, x_ref, gain_ref, slope_ref, b_ref, h_ref, *refs):
    pieces, refs = refs[:n_pieces], refs[n_pieces:]
    dx_ref, dgain_ref, eb_ref, eu_ref, sent_ref, room, sems = refs
    step = pl.program_id(0)
    fetch_quarter(step, feed_copies(pieces, meta, room, sems))
    chunks = chunks_of(x_ref.shape[0])

    @pl.when(step == 0)
    def _():
        for rows in chunks:
            eb_ref[rows, :] = e_ref[rows, :].astype(BF16)
            dx_ref[rows, :] = jnp.zeros_like(dx_ref[rows, :])

    slope = slope_ref[...].astype(F32)
    eu_ref[...] = (rows_nt(eb_ref[...], room[step, 1]) * slope).astype(BF16)
    dx_ref[...] += rows_nt(eu_ref[...], room[step, 0])

    @pl.when(step % 2 == 1)
    def _():
        for kind, (left, right) in enumerate(((b_ref, eu_ref), (h_ref, eb_ref))):
            delta = rows_tn(left[...], right[...])
            for p in range(PARTS):
                rows = pl.ds(pl.multiple_of((meta[0] ^ p) * PIECE, PIECE), PIECE)
                sent_ref[0, kind, rows, :] = delta[p * PIECE : (p + 1) * PIECE].astype(BF16)

    @pl.when(step == 3)
    def _():
        gain_total = jnp.zeros((1, D), F32)
        for rows in chunks:
            part, gain_part = norm_back(x_ref[rows, :], gain_ref[...], dx_ref[rows, :])
            dx_ref[rows, :] = e_ref[rows, :].astype(F32) + part
            gain_total = gain_total + gain_part
        dgain_ref[...] = gain_total


def feed_back(meta, delta, x, gain, slope, pieces, b, h):
    rows = x.shape[0]
    fixed = pl.BlockSpec((rows, D), lambda q: (0, 0))
    moving = pl.BlockSpec((rows, D), lambda q: (0, q))
    narrow = pl.BlockSpec((1, D), lambda q: (0, 0))
    hidden = pl.BlockSpec((rows, D), lambda q: (0, 2 * (q // 2) + 1))
    return pl.pallas_call(
        functools.partial(feed_back_kernel, len(pieces)),
        grid=(4,),
        in_specs=[SCALARS, fixed, fixed, narrow, moving, fixed, hidden]
        + [ANYWHERE] * len(pieces),
        out_specs=[fixed, narrow, fixed, moving]
        + [pl.BlockSpec((1, 2, D, D), lambda q: (q // 2, 0, 0, 0))],
        out_shape=[
            jax.ShapeDtypeStruct((rows, D), F32),
            jax.ShapeDtypeStruct((1, D), F32),
            jax.ShapeDtypeStruct((rows, D), BF16),
            jax.ShapeDtypeStruct((rows, 4 * D), BF16),
            jax.ShapeDtypeStruct((2, 2, D, D), BF16),
        ],
        scratch_shapes=[pltpu.VMEM((4, 2, D, D), BF16), pltpu.SemaphoreType.DMA((16,))],
        compiler_params=pltpu.CompilerParams(vmem_limit_bytes=ROOM),
        cost_estimate=cost(rows, 5, 19),
        name="feed_back",
    )(meta, delta, x, gain, slope, b, h, *pieces)


def feed_weights_kernel(place, eu_ref, *refs):
    h_refs, (b_ref, eb_ref, out_ref) = refs[:-3], refs[-3:]
    j, kind = pl.program_id(0), pl.program_id(1)

    def put(delta):
        for p in range(PARTS):
            rows = pl.ds(pl.multiple_of((place[0] ^ p) * PIECE, PIECE), PIECE)
            out_ref[0, 0, rows, :] = delta[p * PIECE : (p + 1) * PIECE].astype(BF16)

    @pl.when(kind == 0)
    def _():
        put(rows_tn(b_ref[...], eu_ref[...]))

    for span, h_ref in enumerate(h_refs):

        @pl.when(jnp.logical_and(kind == 1, jnp.logical_or(len(h_refs) == 1, j == span)))
        def _(h_ref=h_ref):
            put(rows_tn(h_ref[...], eb_ref[...]))


def feed_weights(place, eu, h, b, eb, first):
    rows = b.shape[0]
    fixed = pl.BlockSpec((rows, D), lambda j, kind, place: (0, 0))
    moving = pl.BlockSpec((rows, D), lambda j, kind, place: (0, 2 * j + first))
    hidden = [moving]
    if len(h) == 2:
        hidden = [pl.BlockSpec((rows, D), lambda j, kind, place: (0, first))] * 2
    return pl.pallas_call(
        feed_weights_kernel,
        grid_spec=pltpu.PrefetchScalarGridSpec(
            num_scalar_prefetch=1,
            grid=(2, 2),
            in_specs=[moving] + hidden + [fixed, fixed],
            out_specs=pl.BlockSpec((1, 1, D, D), lambda j, kind, place: (j, kind, 0, 0)),
        ),
        out_shape=jax.ShapeDtypeStruct((2, 2, D, D), BF16),
        compiler_params=pltpu.CompilerParams(vmem_limit_bytes=ROOM),
        cost_estimate=cost(rows, 4, 6),
        name="feed_weights",
    )(place, eu, *h, b, eb)


def turn_back_kernel(
    meta, side, encoded, gain, context, returned, radar_part, cotangent, out, gain_out
):
    cut = context.shape[0]

    @pl.when(side[0] == 1)
    def _():
        out[:cut] = returned[...].astype(F32)
        out[cut:] = radar_part[...]
        gain_out[...] = jnp.zeros_like(gain_out)

    @pl.when(side[0] == 0)
    def _():
        total = jnp.zeros_like(gain_out)
        for part, incoming in enumerate((context, returned)):
            rows = slice(part * cut, (part + 1) * cut)
            delta, gain_part = norm_back(encoded[rows], gain[...], incoming[...].astype(F32))
            total = total + gain_part
            out[rows] = delta
        gain_out[...] = total

        def one_image(i, carry):
            rows = pl.ds(pl.multiple_of(i * SLOTS, 8), SLOTS)
            seen = lax.broadcasted_iota(jnp.int32, (SLOTS, 1), 0) < meta[3 + i]
            out[rows] += jnp.where(seen, cotangent[i].astype(F32), 0.0)
            return carry

        lax.fori_loop(0, cotangent.shape[0], one_image, 0)


def turn_back(meta, modality, encoded, gain, context, returned, radar_part, cotangent):
    return pl.pallas_call(
        turn_back_kernel,
        in_specs=[SCALARS] * 2 + [WHOLE] * 6,
        out_specs=[WHOLE] * 2,
        out_shape=[
            jax.ShapeDtypeStruct(encoded.shape, F32),
            jax.ShapeDtypeStruct((1, D), F32),
        ],
        compiler_params=pltpu.CompilerParams(vmem_limit_bytes=ROOM),
        cost_estimate=cost(816, 5, 0),
        name="turn_back",
    )(meta, modality[None], encoded, gain, context, returned, radar_part, cotangent)


def relative_parts(parts, own):
    return jnp.stack(
        [lax.dynamic_index_in_dim(parts, r ^ own, 0, keepdims=False) for r in range(PARTS)]
    )


def pack_mix(triple, out_weight):
    return jnp.concatenate([triple.transpose(1, 2, 0), out_weight[None]], 0)


def piece_of(quarter, part):
    if quarter.shape[1] == PIECE:
        return lax.dynamic_index_in_dim(quarter, part, 0, keepdims=False)
    return lax.dynamic_slice_in_dim(quarter, part * PIECE, PIECE, 1)


def unpack_mix(parts):
    return parts[:3].transpose(2, 0, 1).astype(F32), parts[3].astype(F32)


def unpack_feed_kernel(place, *refs):
    refs, (expand_ref, reduce_ref) = refs[:-2], refs[-2:]
    step = PIECE // 2
    for n in range(len(refs) // 5):

        @pl.when(pl.program_id(0) == n)
        def _(n=n):
            part, low, high, low_far, high_far = refs[5 * n : 5 * n + 5]
            for kind, out in enumerate((expand_ref, reduce_ref)):
                lows = [part[kind, :step], low[kind], low_far[0, kind], low_far[1, kind]]
                highs = [part[kind, step:], high_far[0, kind], high[kind], high_far[1, kind]]
                for p in range(PARTS):
                    start = pl.multiple_of((place[0] ^ p) * PIECE, PIECE)
                    out[0, pl.ds(start, step), :] = lows[p].astype(F32)
                    out[0, pl.ds(start + step, step), :] = highs[p].astype(F32)


def unpack_feed(place, *gathered):
    count = len(gathered)
    operands = [piece for pieces in gathered for piece in pieces]
    if count == 1:
        out = pl.BlockSpec((1, D, D), lambda n, place: (n, 0, 0))
    else:
        out = pl.BlockSpec((1, D, D), lambda n, place: (n ^ place[2], 0, 0))
    shape = jax.ShapeDtypeStruct((count, D, D), F32)
    return pl.pallas_call(
        unpack_feed_kernel,
        grid_spec=pltpu.PrefetchScalarGridSpec(
            num_scalar_prefetch=1,
            grid=(count,),
            in_specs=[WHOLE] * len(operands),
            out_specs=[out, out],
        ),
        out_shape=[shape, shape],
        compiler_params=pltpu.CompilerParams(vmem_limit_bytes=ROOM),
        cost_estimate=cost(816, 1, 2 * count),
        name="unpack_feed",
    )(place, *operands)


def fetch_relayed(zero, three):
    return (zero, swap(zero, dp_mask=1), swap(zero, dp_mask=2), three)


def fetch_beside(pieces):
    return pieces + tuple(swap(piece, head_mask=CORE) for piece in pieces)


AXES = {"x": (0, 0, ACROSS), "y": (3, 1, 0), "z": (2, 2, 0)}
THIRDS = ("xyz", "yxz", "zxy")
HALVES = ("xyz", "yzx")
LAST = ("xyz", "yxz")
CROSS = ("yxz", "zxy")


def halves(array, axis):
    return lax.slice_in_dim(array, 0, 1, axis=axis), lax.slice_in_dim(array, 1, 2, axis=axis)


def add_split(keep, beside, orders=THIRDS):
    kinds, rows = keep.shape[1:3]
    kinds, rows = (1, rows) if kinds == PARTS else (kinds, rows // PARTS)
    total = (keep + beside).reshape(2, kinds, 2, 2, rows, D)
    step = PIECE // len(orders)
    cuts = [i * step for i in range(len(orders))] + [rows]
    return [total[:, :, :, :, low:high] for low, high in zip(cuts[:-1], cuts[1:])]


def link_send(shares, stage, orders=THIRDS):
    out = []
    for array, order in zip(shares, orders, strict=True):
        axis, dp_mask, head_mask = AXES[order[stage]]
        keep, sent = halves(array, axis)
        out.append((keep, swap(sent, dp_mask, head_mask)))
    return out


def link_first(keep, beside, orders=THIRDS):
    shape = (2, -1, 2, 2, PIECE, D)
    step = PIECE // len(orders)

    def split(keep, beside):
        out = []
        for i, order in enumerate(orders):
            rows = slice(i * step, (i + 1) * step)
            share = keep[:, :, :, :, rows] + beside[:, :, :, :, rows]
            out.append(halves(share, AXES[order[0]][0]))
        return out

    return glue(split, keep.reshape(shape), beside.reshape(shape))


def link_swap(parts, stage, orders=THIRDS):
    return [
        (keep, swap(sent, *AXES[order[stage]][1:]))
        for (keep, sent), order in zip(parts, orders, strict=True)
    ]


def link_next(pairs, stage, orders=THIRDS):
    def split(pairs):
        return [
            halves(keep + received, AXES[order[stage]][0])
            for (keep, received), order in zip(pairs, orders, strict=True)
        ]

    return link_swap(glue(split, pairs), stage, orders)


def link_add(pairs):
    return [keep + received for keep, received in pairs]


def join(shares):
    return jnp.concatenate([share[0, :, 0, 0] for share in shares], 1)


def rest_send(array, stop):
    mask = PARTS
    while 2 * mask < stop:
        array = array + swap(array, dp_mask=mask)
        mask *= 2
    return array, swap(array, dp_mask=mask)


def rest_add(pair):
    return pair[0] + pair[1]


def over_rest(array, stop):
    mask = PARTS
    while mask < stop:
        array = array + swap(array, dp_mask=mask)
        mask *= 2
    return array


def gather_first(part):
    step = PIECE // 2
    return part, swap(part[:, :step], dp_mask=1), swap(part[:, step:PIECE], dp_mask=2)


def gather_second(first):
    part, low, high = first
    step = PIECE // 2
    return (
        part,
        low,
        high,
        swap(jnp.stack([part[:, :step], low]), dp_mask=2),
        swap(jnp.stack([part[:, step:PIECE], high]), dp_mask=1),
    )


def gather_join(pieces):
    part, low, high, low_far, high_far = pieces
    step = PIECE // 2
    lows = [part[:, :step], low, low_far[0], low_far[1]]
    highs = [part[:, step:PIECE], high_far[0], high, high_far[1]]
    return jnp.stack([jnp.concatenate(pair, 1) for pair in zip(lows, highs, strict=True)])


def on_device(
    tokens,
    cotangent,
    ratios,
    patch_index,
    encoder_gains,
    encoder_attend_in,
    encoder_attend_out,
    encoder_expand,
    encoder_reduce,
    uniting_gains,
    uniting_query,
    uniting_pair,
    uniting_attend_out,
    uniting_expand,
    uniting_reduce,
):
    groups = lax.axis_size("dp")
    side = groups // 2
    group, lane = lax.axis_index("dp"), lax.axis_index("head")
    radar = group >= side
    modality = radar.astype(jnp.int32)
    own = group % PARTS
    images = tokens.shape[0]
    some = images // 2
    cut = some * SLOTS

    def select_slot(stacked):
        return lax.dynamic_index_in_dim(stacked, modality, 0, keepdims=False)

    gains = select_slot(encoder_gains)[:, None]
    uni_gains = uniting_gains[:, None]

    own_ratios = lax.dynamic_slice_in_dim(ratios, lane * images, images, 0)
    patches = lax.dynamic_slice_in_dim(patch_index, lane * images, images, 0)
    counts = PATCHES * (100 - own_ratios) // 100
    first = modality * some
    meta = jnp.concatenate([jnp.stack([own, lane, 0 * first]), counts])
    pair_meta = jnp.concatenate([jnp.stack([own, lane, first]), counts])
    place = jnp.stack([own, lane, modality])
    visible = (jnp.arange(SLOTS)[None, :] < counts[:, None])[:, :, None]
    queries = patches[:, None, :]
    row_gap = (patches // GRID)[:, :, None] - queries // GRID
    col_gap = (patches % GRID)[:, :, None] - queries % GRID
    distance = jnp.sqrt((row_gap * row_gap + col_gap * col_gap).astype(F32))
    per_lane = HEADS // lax.axis_size("head")
    heads = jnp.concatenate(
        [(lane ^ mask) * per_lane + jnp.arange(per_lane) for mask in range(4)]
    )
    slopes = 2.0 ** (-8.0 * (heads.astype(F32) + 1.0) / HEADS)

    mix_quarter = pack_mix(select_slot(encoder_attend_in), select_slot(encoder_attend_out))
    mix_zero = swap(piece_of(mix_quarter, own), head_mask=ACROSS)
    mix_near = (mix_quarter, swap(mix_quarter, head_mask=CORE))
    mix_quarter, encoder_expand, encoder_reduce = tie(
        mix_quarter, encoder_expand, encoder_reduce
    )
    feed_quarter = jnp.stack([select_slot(encoder_expand), select_slot(encoder_reduce)])
    feed_quarter, mix_quarter, mix_zero, flat, uni_feed_quarter, meta, slopes, distance = tie(
        feed_quarter,
        mix_quarter,
        mix_zero,
        tokens.reshape(-1, D),
        jnp.stack([uniting_expand, uniting_reduce]),
        meta,
        slopes,
        distance,
    )
    mix_pieces = fetch_relayed(
        mix_zero, swap(piece_of(mix_quarter, own ^ 3), head_mask=ACROSS)
    )
    feed_zero = swap(piece_of(feed_quarter, own), head_mask=ACROSS)
    feed_near = (feed_quarter, swap(feed_quarter, head_mask=CORE))

    normed_one, middle, *near = mix_forward(
        meta, slopes, flat, None, gains[0], None, mix_near, distance
    )
    middle, mix_pieces, feed_zero, feed_near = tie(middle, mix_pieces, feed_zero, feed_near)
    feed_quarter = feed_near[0]
    mix_far = fetch_beside(mix_pieces)
    feed_pieces = fetch_relayed(
        feed_zero, swap(piece_of(feed_quarter, own ^ 3), head_mask=ACROSS)
    )
    feed_zero, uniting_query, uniting_pair, uniting_attend_out = tie(
        feed_zero, uniting_query, uniting_pair, uniting_attend_out
    )
    uni_quarter = pack_mix(
        jnp.concatenate([uniting_query[:, None], uniting_pair], 1), uniting_attend_out
    )
    middle, mix_far, uni_feed_quarter = tie(middle, mix_far, uni_feed_quarter)
    uni_feed = (lax.all_gather(uni_feed_quarter, "head"),)
    middle, *far = mix_forward(
        meta, slopes, middle, None, None, normed_one, mix_far, distance, HEADS // 2
    )
    qkv, mixed, lse = zip(near, far)
    middle, feed_pieces, uni_quarter = tie(middle, feed_pieces, uni_quarter)
    feed_far = fetch_beside(feed_pieces)
    uni_zero = swap(piece_of(uni_quarter, own), head_mask=ACROSS)
    uni_three = swap(piece_of(uni_quarter, own ^ 3), head_mask=ACROSS)
    enc_mix, enc_feed = mix_near + mix_far, feed_near + feed_far

    *half_fed, leaving = feed_rows(place, middle, gains[1], uni_gains[0], enc_feed)
    leaving, half_fed, uni_zero = tie(leaving, half_fed, uni_zero)
    received = swap(leaving, dp_mask=side)
    uni_mix_pieces = fetch_relayed(uni_zero, uni_three)
    uni_mix_near = (uni_quarter, swap(uni_quarter, head_mask=CORE))
    encoded, normed_two, *stored, context = feed_rows(
        place, middle, gains[1], uni_gains[0], enc_feed, half_fed
    )
    hidden, bend = ([part] for part in stored)
    encoded, received, uni_mix_pieces = tie(encoded, received, uni_mix_pieces)
    uni_mix = uni_mix_near + fetch_beside(uni_mix_pieces)
    received, cotangent = tie(received, cotangent)
    sent_cotangent = swap(cotangent[:some], dp_mask=side)
    radar_rows = jnp.where(radar, encoded[cut:], received.astype(F32))
    context_rows = jnp.where(radar, received, context)

    uni_normed, uni_middle, *stored = mix_forward(
        pair_meta, slopes, radar_rows, context_rows, uni_gains[1], None, uni_mix, distance
    )
    uni_qkv, uni_mixed, uni_lse = ([part] for part in stored)
    uni_normed_two, joined, *stored = feed_forward(
        meta, uni_middle, uni_gains[2], None, uni_feed
    )
    uni_hidden, uni_bend = ([part] for part in stored)

    joined, sent_cotangent = tie(joined, sent_cotangent)
    joined_half = joined.reshape(some, SLOTS, D)
    other_half = [swap(joined_half[i : i + 1], dp_mask=side) for i in range(some)]
    pair_cotangent = jnp.where(radar, cotangent[some:], sent_cotangent)
    pair_visible = lax.dynamic_slice_in_dim(visible, first, some, 0)
    delta_joined = jnp.where(pair_visible, pair_cotangent, 0).reshape(-1, D)
    delta_middle, gain_three, eb, eu, sent = feed_back(
        meta,
        delta_joined,
        uni_middle,
        uni_gains[2],
        uni_bend[0],
        uni_feed,
        uni_normed_two,
        uni_hidden[0],
    )
    sent, eu, other_half[:2] = tie(sent, eu, other_half[:2])
    beside = swap(sent, head_mask=CORE)
    keep = feed_weights(place, eu, uni_hidden, uni_normed_two, eb, 0)
    keep, beside, other_half[2:] = tie(keep, beside, other_half[2:])
    uni_feed_parts, delta_middle = tie(link_first(keep, beside), delta_middle)
    uni_feed_pairs = link_swap(uni_feed_parts, 0)
    delta_radar, gain_two, dqkv, mix_eb, delta_context, leaving = mix_back(
        pair_meta,
        slopes,
        delta_middle,
        radar_rows,
        uni_gains[1],
        uni_qkv,
        uni_lse,
        uni_mix,
        distance,
        True,
    )
    leaving, dqkv, uni_feed_pairs = tie(leaving, dqkv, uni_feed_pairs)
    other_half = jnp.concatenate(other_half, 0)
    returned = swap(leaving, dp_mask=side)
    uni_feed_pairs = link_next(uni_feed_pairs, 1)
    keep, sent = mix_weights(place, dqkv, uni_mixed, uni_normed, context_rows, mix_eb)
    layer_output = jnp.where(
        visible,
        jnp.where(
            radar,
            jnp.concatenate([other_half, joined_half], 0),
            encoded.astype(BF16).reshape(images, SLOTS, D),
        ),
        0,
    )
    sent, returned, uni_feed_pairs, layer_output = tie(
        sent, returned, uni_feed_pairs, layer_output
    )
    beside = swap(sent, head_mask=CORE)
    uni_feed_pairs = link_send(link_add(uni_feed_pairs), 2)
    delta_encoded, gain_one = turn_back(
        meta, modality, encoded, uni_gains[0], delta_context, returned, delta_radar, cotangent
    )
    delta_encoded, beside, uni_feed_pairs = tie(delta_encoded, beside, uni_feed_pairs)
    uni_mix_sum, uni_feed_part = add_split(keep, beside, CROSS), join(link_add(uni_feed_pairs))
    delta_encoded, uni_mix_sum, uni_feed_part = tie(delta_encoded, uni_mix_sum, uni_feed_part)
    uni_feed_rest = rest_send(uni_feed_part, groups)
    uni_mix_pairs = link_send(uni_mix_sum, 0, CROSS)

    delta_middle, gain_b, eb, eu, sent = feed_back(
        meta, delta_encoded, middle, gains[1], bend[0], enc_feed, normed_two, hidden[0]
    )
    sent, eu, uni_feed_rest, uni_mix_pairs = tie(sent, eu, uni_feed_rest, uni_mix_pairs)
    uni_feed_part, uni_mix_sum = rest_add(uni_feed_rest), link_add(uni_mix_pairs)
    eu, uni_feed_part, uni_mix_sum = tie(eu, uni_feed_part, uni_mix_sum)
    beside = swap(sent, head_mask=CORE)
    uni_feed_near = swap(uni_feed_part, dp_mask=1)
    uni_mix_pairs = link_send(uni_mix_sum, 1, CROSS)
    keep = feed_weights(place, eu, hidden, normed_two, eb, 0)
    keep, beside, uni_feed_near, uni_mix_pairs = tie(keep, beside, uni_feed_near, uni_mix_pairs)
    uni_feed_near = jnp.stack([uni_feed_part, uni_feed_near])
    enc_feed_sum, uni_mix_sum = add_split(keep, beside, HALVES), link_add(uni_mix_pairs)
    delta_middle, enc_feed_sum, uni_mix_sum, uni_feed_near = tie(
        delta_middle, enc_feed_sum, uni_mix_sum, uni_feed_near
    )
    enc_feed_pairs = link_send(enc_feed_sum, 0, HALVES)
    uni_mix_pairs = link_send(uni_mix_sum, 2, CROSS)
    uni_feed_far = swap(uni_feed_near, dp_mask=2)
    delta_inputs, gain_a, dqkv, eb = mix_back(
        meta, slopes, delta_middle, flat, gains[0], qkv, lse, enc_mix, distance, False
    )
    dqkv, enc_feed_pairs, uni_mix_pairs, uni_feed_far = tie(
        dqkv, enc_feed_pairs, uni_mix_pairs, uni_feed_far
    )
    enc_feed_sum, uni_mix_part = link_add(enc_feed_pairs), join(link_add(uni_mix_pairs))
    dqkv, enc_feed_sum, uni_mix_part = tie(dqkv, enc_feed_sum, uni_mix_part)
    enc_feed_pairs = link_send(enc_feed_sum, 1, HALVES)
    uni_mix_rest = rest_send(uni_mix_part, groups)

    totals = (gain_a, gain_b, gain_one, gain_two, gain_three)
    keep, sent = mix_weights(place, dqkv, mixed, normed_one, normed_one, eb, totals)
    sent, enc_feed_pairs, uni_mix_rest = tie(sent, enc_feed_pairs, uni_mix_rest)
    uni_mix_gather = gather_first(rest_add(uni_mix_rest))
    beside = swap(sent, head_mask=CORE)
    enc_feed_pairs = link_send(link_add(enc_feed_pairs), 2, HALVES)
    enc_mix_pairs = link_send(add_split(keep, beside, LAST), 0, LAST)
    feed_part = over_rest(join(link_add(enc_feed_pairs)), side)
    feed_other = swap(feed_part, dp_mask=side)
    enc_mix_pairs, feed_part, uni_mix_gather = tie(enc_mix_pairs, feed_part, uni_mix_gather)
    enc_mix_pairs = link_send(link_add(enc_mix_pairs), 1, LAST)
    feed_gather = gather_first(feed_part)
    enc_mix_pairs = link_send(link_add(enc_mix_pairs), 2, LAST)
    enc_mix_pairs, feed_gather = tie(enc_mix_pairs, feed_gather)
    feed_gather = gather_second(feed_gather)
    enc_mix_pairs, feed_other = tie(enc_mix_pairs, feed_other)
    mix_part = over_rest(join(link_add(enc_mix_pairs)), side)
    mix_part, feed_other = tie(mix_part, feed_other)
    mix_other = swap(mix_part, dp_mask=side)
    feed_other_gather = gather_first(feed_other)
    feed_gather, uni_feed_near = tie(feed_gather, uni_feed_near)
    uni_feed_all = relative_parts(jnp.concatenate([uni_feed_near, uni_feed_far], 0), own)
    fexpand, freduce = (uni_feed_all[:, i].reshape(D, D).astype(F32) for i in range(2))
    mix_other, feed_other_gather, feed_gather, uni_mix_gather, fexpand, freduce = tie(
        mix_other, feed_other_gather, feed_gather, uni_mix_gather, fexpand, freduce
    )
    mix_gather = gather_first(jnp.concatenate([mix_part, mix_other], 0))
    feed_other_gather = gather_second(feed_other_gather)
    mix_gather, uni_mix_gather = tie(mix_gather, uni_mix_gather)
    mix_gather, uni_mix_gather = gather_second(mix_gather), gather_second(uni_mix_gather)
    totals = (mix_part + mix_other)[0, PIECE:].astype(F32)

    ftriple, fout = unpack_mix(relative_parts(gather_join(uni_mix_gather)[:, 0], own))
    expands, reduces = unpack_feed(place, feed_gather, feed_other_gather)
    mix_all = gather_join(mix_gather)
    mine, theirs = mix_all[:, 0], mix_all[:, 1]
    mixes = [
        unpack_mix(relative_parts(part, own))
        for part in (jnp.where(radar, theirs, mine), jnp.where(radar, mine, theirs))
    ]

    return (
        layer_output,
        delta_inputs.reshape(images, SLOTS, D),
        totals[:4].reshape(2, 2, D),
        jnp.stack([mixes[0][0], mixes[1][0]]),
        jnp.stack([mixes[0][1], mixes[1][1]]),
        expands,
        reduces,
        totals[4:7],
        ftriple[:, 0],
        ftriple[:, 1:],
        fout,
        fexpand,
        freduce,
    )


def solution(mesh):
    return jax.shard_map(
        on_device,
        mesh=mesh,
        in_specs=(
            P(("dp", "head"), None, None),
            P(("dp", "head"), None, None),
            P("dp"),
            P("dp", None),
            P(),
            P(None, None, None, "head"),
            P(None, "head", None),
            P(None, None, "head"),
            P(None, "head", None),
            P(),
            P(None, "head"),
            P(None, None, "head"),
            P("head", None),
            P(None, "head"),
            P("head", None),
        ),
        out_specs=(
            P(("dp", "head"), None, None),
            P(("dp", "head"), None, None),
            P(),
            P(None, None, None, "head"),
            P(None, "head", None),
            P(None, None, "head"),
            P(None, "head", None),
            P(),
            P(None, "head"),
            P(None, None, "head"),
            P("head", None),
            P(None, "head"),
            P("head", None),
        ),
        check_vma=False,
    )
```

```python
import functools

import jax
import jax.numpy as jnp
from jax import lax
from jax.experimental import pallas as pl
from jax.experimental.pallas import tpu as pltpu
from jax.sharding import PartitionSpec as P

D = 768
HEADS = 12
HEAD_DIM = 64
GRID = 15
PATCHES = 225
SLOTS = 136
PARTS = 4
PIECE = D // PARTS
CORE, ACROSS = 1, 2
SCALE = HEAD_DIM**-0.5

EPSILON = 1e-06
NEGATIVE = -1e30
F32, BF16 = jnp.float32, jnp.bfloat16
WHOLE = pl.BlockSpec(memory_space=pltpu.VMEM)
ANYWHERE = pl.BlockSpec(memory_space=pl.ANY)
SCALARS = pl.BlockSpec(memory_space=pltpu.SMEM)
ROOM = 56 << 20


def cost(rows, fixed, each):
    return pl.CostEstimate(
        flops=int((fixed + each * rows / 816) * 1e7), bytes_accessed=1, transcendentals=0
    )


def swap(array, dp_mask=0, head_mask=0, senders=None):
    groups, lanes = lax.axis_size("dp"), lax.axis_size("head")
    pairs = [
        (g * lanes + h, (g ^ dp_mask) * lanes + (h ^ head_mask))
        for g in (range(groups) if senders is None else senders)
        for h in range(lanes)
    ]
    return lax.ppermute(array, ("dp", "head"), pairs)


def tie(*arrays):
    return lax.optimization_barrier(arrays)


def rows_nt(left, right):
    return lax.dot_general(left, right, (((1,), (1,)), ((), ())), preferred_element_type=F32)


def rows_nn(left, right):
    return lax.dot_general(left, right, (((1,), (0,)), ((), ())), preferred_element_type=F32)


def rows_tn(left, right):
    return lax.dot_general(left, right, (((0,), (0,)), ((), ())), preferred_element_type=F32)


def normalize(values):
    centered = values - jnp.mean(values, -1, keepdims=True)
    spread = lax.rsqrt(jnp.mean(centered * centered, -1, keepdims=True) + EPSILON)
    return centered * spread, spread


def layer_norm(values, gain):
    return normalize(values)[0] * gain


def norm_back(values, gain, incoming):
    unit, spread = normalize(values)
    scaled = incoming * gain
    delta = spread * (
        scaled
        - jnp.mean(scaled, -1, keepdims=True)
        - unit * jnp.mean(scaled * unit, -1, keepdims=True)
    )
    return delta, jnp.sum(incoming * unit, 0, keepdims=True)


def glue(function, *arrays):
    leaves, tree = jax.tree.flatten(arrays)
    results, result_tree = jax.tree.flatten(jax.eval_shape(function, *arrays))

    def kernel(*refs):
        values = tree.unflatten([ref[...] for ref in refs[: len(leaves)]])
        for ref, value in zip(refs[len(leaves) :], jax.tree.leaves(function(*values))):
            ref[...] = value

    out = pl.pallas_call(
        kernel,
        in_specs=[WHOLE] * len(leaves),
        out_specs=[WHOLE] * len(results),
        out_shape=results,
        compiler_params=pltpu.CompilerParams(vmem_limit_bytes=ROOM),
        cost_estimate=cost(816, 1, 0),
        name="glue",
    )(*leaves)
    return result_tree.unflatten(out)


def chunks_of(rows):
    step = 2 * SLOTS if rows % (2 * SLOTS) == 0 else rows
    return [slice(start, start + step) for start in range(0, rows, step)]


QUARTERS_IN = {1: 4, 2: 2, 8: 2, 10: 4}


def feed_copies(pieces, meta, room, sems):
    if len(pieces) == 1:
        return [
            [pltpu.make_async_copy(pieces[0].at[meta[1] ^ q], room.at[q], sems.at[q])]
            for q in range(4)
        ]
    near = len(pieces) % 8
    copies = [
        [pltpu.make_async_copy(pieces[q], room.at[q], sems.at[q])] for q in range(near)
    ]
    for q in range(near, near + (len(pieces) - near) // PARTS):
        group = []
        for r in range(PARTS):
            at = near + (q - near) * PARTS + r
            rows = pl.ds(pl.multiple_of((meta[0] ^ r) * PIECE, PIECE), PIECE)
            group.append(
                pltpu.make_async_copy(pieces[at], room.at[q, :, rows, :], sems.at[at])
            )
        copies.append(group)
    return copies


def mix_copies(pieces, meta, room, sems):
    near = len(pieces) % 8
    copies = [
        pltpu.make_async_copy(
            pieces[q], room.at[:, pl.ds(q * PIECE, PIECE), :], sems.at[q]
        )
        for q in range(near)
    ]
    for at in range(near, len(pieces)):
        q, r = divmod(at - near, PARTS)
        rows = pl.ds((near + q) * PIECE, PIECE)
        copies.append(
            pltpu.make_async_copy(pieces[at], room.at[meta[0] ^ r, rows, :], sems.at[at])
        )
    return copies


SIZES = (64, 96, 128, SLOTS)


def by_size(count, branch):
    which = sum((count > size).astype(jnp.int32) for size in SIZES[:-1])
    lax.switch(which, [functools.partial(branch, size) for size in SIZES])


def two_heads(block, first):
    zero = jnp.zeros_like(block)
    return jnp.concatenate(
        [jnp.where(first, block, zero), jnp.where(first, zero, block)], 0
    ).astype(BF16)


def pick_heads(stacked, first):
    size = stacked.shape[0] // 2
    return jnp.where(first, stacked[:size], stacked[size:])


def image_setup(size, distance_ref, image, count):
    first = lax.broadcasted_iota(jnp.int32, (size, 2 * HEAD_DIM), 1) < HEAD_DIM
    distance = distance_ref[image, :size, :size]
    distance = jnp.concatenate([distance, distance], 1)
    seen = lax.broadcasted_iota(jnp.int32, (size, 1), 0) < count
    lanes = lax.broadcasted_iota(jnp.int32, (1, 2 * size), 1) < size

    def scores_of(keys, queries, slopes, head):
        slope = jnp.where(lanes, slopes[head], slopes[head + 1])
        return jnp.where(seen, rows_nt(keys, queries) - distance * slope, NEGATIVE)

    return first, scores_of


def mix_forward_kernel(local, cross, images, head, n_pieces, *refs):
    meta, slopes, x_ref = refs[:3]
    refs = refs[3:]
    if cross:
        c_ref, refs = refs[0], refs[1:]
    if local:
        gain_ref, refs = refs[0], refs[1:]
    else:
        a_ref, refs = refs[0], refs[1:]
    pieces, refs = refs[:n_pieces], refs[n_pieces:]
    distance_ref, refs = refs[0], refs[1:]
    if local:
        a_ref, refs = refs[0], refs[1:]
    out_ref, qkv_ref, o_ref, lse_ref, room, wide, sems = refs
    copies = mix_copies(pieces, meta, room, sems)
    for copy in copies:
        copy.start()
    chunks = chunks_of(images * SLOTS)
    if local:
        for rows in chunks:
            a_ref[rows, :] = layer_norm(x_ref[rows, :].astype(F32), gain_ref[...]).astype(BF16)
    for copy in copies:
        copy.wait()
    width = o_ref.shape[1]
    if cross:
        wide[:, :width] = rows_nt(a_ref[...], room[0])
        wide[:, width:] = rows_nt(c_ref[...], room[1:3].reshape(2 * width, D))
    else:
        wide[...] = rows_nt(a_ref[...], room[:3].reshape(3 * width, D))

    def one_image(i, carry):
        image = meta[2] + i
        start = pl.multiple_of(i * SLOTS, 8)
        qkv_ref[i] = wide[pl.ds(start, SLOTS), :].astype(BF16)

        def work(size):
            first, scores_of = image_setup(size, distance_ref, image, meta[3 + image])
            rows = pl.ds(start, size)
            for pair in range(width // (2 * HEAD_DIM)):
                low, high = pair * 2 * HEAD_DIM, (pair + 1) * 2 * HEAD_DIM
                k = wide[rows, width + low : width + high].astype(BF16)
                v = wide[rows, 2 * width + low : 2 * width + high].astype(BF16)
                queries = two_heads(
                    wide[rows, low:high].astype(BF16).astype(F32) * SCALE, first
                )
                scores = scores_of(k, queries, slopes, head + 2 * pair)
                top = jnp.max(scores, 0, keepdims=True)
                exponent = jnp.exp(scores - top)
                total = jnp.sum(exponent, 0, keepdims=True)
                weights = (exponent * (1.0 / total)).astype(BF16)
                wide[rows, low:high] = pick_heads(rows_tn(weights, v), first)
                lse_ref[i, pair : pair + 1, : 2 * size] = top + jnp.log(total)
            if size < SLOTS:
                rest = pl.ds(pl.multiple_of(start + size, 8), SLOTS - size)
                wide[rest, :width] = jnp.zeros((SLOTS - size, width), F32)

        by_size(meta[3 + image], work)
        return carry

    lax.fori_loop(0, images, one_image, 0)
    for rows in chunks:
        o_ref[rows, :] = wide[rows, :width].astype(BF16)
    out_ref[...] = x_ref[...].astype(F32) + rows_nn(o_ref[...], room[3])


def mix_forward(meta, slopes, x, context, gain, normed, pieces, distance, head=0):
    images = x.shape[0] // SLOTS
    rows = images * SLOTS
    cross, local = context is not None, normed is None
    width = PIECE * QUARTERS_IN[len(pieces)]
    operands = [meta, slopes, x] + ([context] if cross else [])
    operands += [gain if local else normed, *pieces, distance]
    specs = [SCALARS] * 2 + [WHOLE] * (3 if cross else 2) + [ANYWHERE] * len(pieces) + [WHOLE]
    narrow = jax.ShapeDtypeStruct((rows, D), BF16)
    return pl.pallas_call(
        functools.partial(mix_forward_kernel, local, cross, images, head, len(pieces)),
        in_specs=specs,
        out_specs=[WHOLE] * (5 if local else 4),
        out_shape=([narrow] if local else [])
        + [
            jax.ShapeDtypeStruct((rows, D), F32),
            jax.ShapeDtypeStruct((images, SLOTS, 3 * width), BF16),
            jax.ShapeDtypeStruct((rows, width), BF16),
            jax.ShapeDtypeStruct((images, width // (2 * HEAD_DIM), 2 * SLOTS), F32),
        ],
        scratch_shapes=[
            pltpu.VMEM((4, width, D), BF16),
            pltpu.VMEM((rows, 3 * width), F32),
            pltpu.SemaphoreType.DMA((16,)),
        ],
        compiler_params=pltpu.CompilerParams(vmem_limit_bytes=ROOM),
        cost_estimate=cost(rows, 4, 8 * width / 384),
        name="mix_forward",
    )(*operands)


def mix_back_kernel(cross, images, spans, *refs):
    meta, slopes, e_ref, x_ref, gain_ref = refs[:5]
    refs = refs[5:]
    qkv_refs, lse_refs, refs = refs[:spans], refs[spans : 2 * spans], refs[2 * spans :]
    pieces, refs = refs[:10], refs[10:]
    distance_ref, dx_ref, dgain_ref, dqkv_ref, eb_ref = refs[:5]
    refs = refs[5:]
    if cross:
        dc_ref, leaving_ref, refs = refs[0], refs[1], refs[2:]
    room, inner_ref, wide, sems = refs
    copies = mix_copies(pieces, meta, room, sems)
    for copy in copies:
        copy.start()
    chunks = chunks_of(images * SLOTS)
    for rows in chunks:
        eb_ref[rows, :] = e_ref[rows, :].astype(BF16)
    for copy in copies:
        copy.wait()
    inner_ref[...] = rows_nt(eb_ref[...], room[3])

    width = D // spans

    def one_image(i, carry):
        image = meta[2] + i
        start = pl.multiple_of(i * SLOTS, 8)

        def work(size):
            first, scores_of = image_setup(size, distance_ref, image, meta[3 + image])
            rows = pl.ds(start, size)
            for pair in range(HEADS // 2):
                low, high = pair * 2 * HEAD_DIM, (pair + 1) * 2 * HEAD_DIM
                half, inside = divmod(pair, HEADS // 2 // spans)
                qkv_ref, lse_ref = qkv_refs[half], lse_refs[half]
                at, to = inside * 2 * HEAD_DIM, (inside + 1) * 2 * HEAD_DIM
                queries = two_heads(qkv_ref[i, :size, at:to].astype(F32) * SCALE, first)
                incoming = two_heads(inner_ref[rows, low:high], first)
                k = qkv_ref[i, :size, width + at : width + to]
                v = qkv_ref[i, :size, 2 * width + at : 2 * width + to]
                scores = scores_of(k, queries, slopes, 2 * pair)
                probable = jnp.exp(scores - lse_ref[i, inside : inside + 1, : 2 * size])
                delta_p = rows_nt(v, incoming)
                shared = jnp.sum(delta_p * probable, 0, keepdims=True)
                delta_s = (probable * (delta_p - shared)).astype(BF16)
                wide[rows, low:high] = pick_heads(rows_tn(delta_s, k), first) * SCALE
                wide[rows, D + low : D + high] = rows_nn(delta_s, queries)
                wide[rows, 2 * D + low : 2 * D + high] = rows_nn(
                    probable.astype(BF16), incoming
                )
            if size < SLOTS:
                rest = pl.ds(pl.multiple_of(start + size, 8), SLOTS - size)
                wide[rest, :] = jnp.zeros((SLOTS - size, 3 * D), F32)

        by_size(meta[3 + image], work)
        return carry

    lax.fori_loop(0, images, one_image, 0)
    for rows in chunks:
        dqkv_ref[rows, :] = wide[rows, :].astype(BF16)
    delta = rows_nn(dqkv_ref[:, :D], room[0])
    side = rows_nn(dqkv_ref[:, D : 2 * D], room[1]) + rows_nn(dqkv_ref[:, 2 * D :], room[2])
    if cross:
        dc_ref[...] = side.astype(BF16)
        inner_ref[...] = delta
    else:
        inner_ref[...] = delta + side
    gain_total = jnp.zeros((1, D), F32)
    for rows in chunks:
        part, gain_part = norm_back(x_ref[rows, :].astype(F32), gain_ref[...], inner_ref[rows, :])
        dx_ref[rows, :] = e_ref[rows, :] + part
        gain_total = gain_total + gain_part
    dgain_ref[...] = gain_total
    if cross:

        @pl.when(meta[2] > 0)
        def _():
            leaving_ref[...] = dc_ref[...]

        @pl.when(meta[2] == 0)
        def _():
            leaving_ref[...] = dx_ref[...].astype(BF16)


def mix_back(meta, slopes, delta, x, gain, qkv, lse, pieces, distance, cross):
    images = qkv[0].shape[0]
    rows = images * SLOTS
    wide_rows = jax.ShapeDtypeStruct((rows, D), BF16)
    return pl.pallas_call(
        functools.partial(mix_back_kernel, cross, images, len(qkv)),
        in_specs=[SCALARS] * 2
        + [WHOLE] * (3 + 2 * len(qkv))
        + [ANYWHERE] * len(pieces)
        + [WHOLE],
        out_specs=[WHOLE] * (6 if cross else 4),
        out_shape=[
            jax.ShapeDtypeStruct((rows, D), F32),
            jax.ShapeDtypeStruct((1, D), F32),
            jax.ShapeDtypeStruct((rows, 3 * D), BF16),
            wide_rows,
        ]
        + ([wide_rows] * 2 if cross else []),
        scratch_shapes=[
            pltpu.VMEM((4, D, D), BF16),
            pltpu.VMEM((rows, D), F32),
            pltpu.VMEM((rows, 3 * D), F32),
            pltpu.SemaphoreType.DMA((16,)),
        ],
        compiler_params=pltpu.CompilerParams(vmem_limit_bytes=ROOM),
        cost_estimate=cost(rows, 5, 23),
        name="mix_back",
    )(meta, slopes, delta, x, gain, *qkv, *lse, *pieces, distance)


def mix_weights_kernel(more, place, dqkv_ref, *refs):
    if more:
        *refs, scratch = refs
        refs, outs = refs[:-2], refs[-2:]
        refs = (*refs, scratch)
    else:
        refs, outs = refs[:-2], refs[-2:]
    if more:
        gain_refs, refs, gains_ref = refs[:5], refs[5:-1], refs[-1]
    o_refs, (a_ref, c_ref, eb_ref) = refs[:-3], refs[-3:]
    kind = pl.program_id(0)

    def put(first, delta):
        for q in range(delta.shape[0] // PIECE):
            part = delta[q * PIECE : (q + 1) * PIECE].astype(BF16)
            outs[(first + q) % 2][(first + q) // 2, 0, :PIECE] = part

    @pl.when(kind == 0)
    def _():
        put(0, rows_tn(dqkv_ref[...], a_ref[...]))

    @pl.when(jnp.logical_or(kind == 1, kind == 2))
    def _():
        put(0, rows_tn(dqkv_ref[...], c_ref[...]))

    @pl.when(kind == 3)
    def _():
        for span, o_ref in enumerate(o_refs):
            put(span * 4 // len(o_refs), rows_tn(o_ref[...], eb_ref[...]))

    if more:
        gains_ref[...] = jnp.zeros_like(gains_ref)
        for i in range(2):
            gains_ref[pl.ds(2 * place[2] + i, 1), :] = gain_refs[i][...]
        for i in range(2, 5):
            gains_ref[2 + i : 3 + i, :] = gain_refs[i][...]
        for out in outs:
            for half in range(2):
                out[half, 0, PIECE:] = gains_ref[...].astype(BF16)


def mix_weights(place, dqkv, o, a, c, eb, gains=None):
    rows = a.shape[0]
    more = gains is not None
    fixed = pl.BlockSpec((rows, D), lambda kind, place: (0, 0))
    narrow = pl.BlockSpec((rows, D // len(o)), lambda kind, place: (0, 0))
    tall = PIECE + (16 if more else 0)
    out = pl.BlockSpec((2, 1, tall, D), lambda kind, place: (0, kind ^ place[0], 0, 0))
    shape = jax.ShapeDtypeStruct((2, PARTS, tall, D), BF16)
    return pl.pallas_call(
        functools.partial(mix_weights_kernel, more),
        grid_spec=pltpu.PrefetchScalarGridSpec(
            num_scalar_prefetch=1,
            grid=(4,),
            in_specs=[pl.BlockSpec((rows, D), lambda kind, place: (0, jnp.minimum(kind, 2)))]
            + [pl.BlockSpec((1, D), lambda kind, place: (0, 0))] * (5 if more else 0)
            + [narrow] * len(o)
            + [fixed] * 3,
            out_specs=[out, out],
            scratch_shapes=[pltpu.VMEM((16, D), F32)] if more else [],
        ),
        out_shape=[shape, shape],
        compiler_params=pltpu.CompilerParams(vmem_limit_bytes=ROOM),
        cost_estimate=cost(rows, 3.5, 7),
        name="mix_weights",
    )(place, dqkv, *(gains if more else []), *o, a, c, eb)


def fetch_quarter(step, copies):
    @pl.when(step == 0)
    def _():
        for group in copies[:2]:
            for copy in group:
                copy.start()

    for q, group in enumerate(copies):

        @pl.when(step == q)
        def _(q=q, group=group):
            for copy in group:
                copy.wait()
            for later in copies[q + 2 : q + 3]:
                for copy in later:
                    copy.start()


def feed_forward_kernel(local, n_pieces, meta, x_ref, norm_ref, *refs):
    pieces, refs = refs[:n_pieces], refs[n_pieces:]
    if local:
        b_ref, refs = refs[0], refs[1:]
    else:
        b_ref = norm_ref
    out_ref, h_ref, g_ref, room, sems, y_ref = refs
    step = pl.program_id(0)
    fetch_quarter(step, feed_copies(pieces, meta, room, sems))

    @pl.when(step == 0)
    def _():
        for rows in chunks_of(x_ref.shape[0]):
            values = x_ref[rows, :]
            y_ref[rows, :] = values
            if local:
                b_ref[rows, :] = layer_norm(values, norm_ref[...]).astype(BF16)

    before = rows_nn(b_ref[...], room[step, 0])
    bell = jnp.exp(-0.5 * before * before) * 0.3989422804014327
    share = 0.5 * (1.0 + lax.erf(before * 0.7071067811865476))
    h_ref[...] = (before * share).astype(BF16)
    g_ref[...] = (share + before * bell).astype(BF16)
    y_ref[...] += rows_nn(h_ref[...], room[step, 1])

    @pl.when(step == pl.num_programs(0) - 1)
    def _():
        out_ref[...] = y_ref[...].astype(BF16)


def feed_forward(meta, x, gain, normed, pieces):
    rows = x.shape[0]
    local = normed is None
    quarters = QUARTERS_IN[len(pieces)]
    fixed = pl.BlockSpec((rows, D), lambda q: (0, 0))
    moving = pl.BlockSpec((rows, D), lambda q: (0, q))
    hidden = jax.ShapeDtypeStruct((rows, quarters * D), BF16)
    return pl.pallas_call(
        functools.partial(feed_forward_kernel, local, len(pieces)),
        grid=(quarters,),
        in_specs=[SCALARS, fixed, pl.BlockSpec((1, D), lambda q: (0, 0)) if local else fixed]
        + [ANYWHERE] * len(pieces),
        out_specs=([fixed] if local else []) + [fixed, moving, moving],
        out_shape=([jax.ShapeDtypeStruct((rows, D), BF16)] if local else [])
        + [jax.ShapeDtypeStruct((rows, D), BF16), hidden, hidden],
        scratch_shapes=[
            pltpu.VMEM((quarters, 2, D, D), BF16),
            pltpu.SemaphoreType.DMA((16,)),
            pltpu.VMEM((rows, D), F32),
        ],
        compiler_params=pltpu.CompilerParams(vmem_limit_bytes=ROOM),
        cost_estimate=cost(rows, 3.6, 4 * quarters),
        name="feed_forward",
    )(meta, x, gain if local else normed, *pieces)


def feed_rows_kernel(leaving, meta, x_ref, gain_ref, next_gain_ref, *refs):
    pieces, refs = refs[:10], refs[10:]
    if not leaving:
        refs = refs[4:]
    y_ref, b_ref, h_ref, g_ref, out_ref, room, sems = refs
    step = pl.program_id(0)
    fetch_quarter(step, feed_copies(pieces, meta, room, sems))

    @pl.when(step == 0)
    def _():
        values = x_ref[...]
        y_ref[...] = values
        b_ref[...] = layer_norm(values, gain_ref[...]).astype(BF16)

    before = rows_nn(b_ref[...], room[step, 0])
    bell = jnp.exp(-0.5 * before * before) * 0.3989422804014327
    share = 0.5 * (1.0 + lax.erf(before * 0.7071067811865476))
    h_ref[...] = (before * share).astype(BF16)
    g_ref[...] = (share + before * bell).astype(BF16)
    y_ref[...] += rows_nn(h_ref[...], room[step, 1])

    @pl.when(jnp.logical_and(step == 3, jnp.logical_or(not leaving, meta[2] == 0)))
    def _():
        out_ref[...] = layer_norm(y_ref[...], next_gain_ref[...]).astype(BF16)

    if leaving:

        @pl.when(jnp.logical_and(step == 3, meta[2] == 1))
        def _():
            out_ref[...] = y_ref[...].astype(BF16)


def feed_rows(place, x, gain, next_gain, pieces, first=None):
    rows = x.shape[0] // 2
    leaving = first is None

    def block(place):
        return 1 - place[2] if leaving else place[2]

    fixed = pl.BlockSpec((rows, D), lambda q, place: (block(place), 0))
    moving = pl.BlockSpec((rows, D), lambda q, place: (block(place), q))
    narrow = pl.BlockSpec((1, D), lambda q, place: (0, 0))
    hidden = jax.ShapeDtypeStruct((2 * rows, 4 * D), BF16)
    return pl.pallas_call(
        functools.partial(feed_rows_kernel, leaving),
        grid_spec=pltpu.PrefetchScalarGridSpec(
            num_scalar_prefetch=1,
            grid=(4,),
            in_specs=[fixed, narrow, narrow] + [ANYWHERE] * (10 if leaving else 14),
            out_specs=[fixed, fixed, moving, moving]
            + [pl.BlockSpec((rows, D), lambda q, place: (0, 0))],
            scratch_shapes=[pltpu.VMEM((4, 2, D, D), BF16), pltpu.SemaphoreType.DMA((16,))],
        ),
        out_shape=[
            jax.ShapeDtypeStruct((2 * rows, D), F32),
            jax.ShapeDtypeStruct((2 * rows, D), BF16),
            hidden,
            hidden,
            jax.ShapeDtypeStruct((rows, D), BF16),
        ],
        input_output_aliases={} if leaving else {14 + i: i for i in range(4)},
        compiler_params=pltpu.CompilerParams(vmem_limit_bytes=ROOM),
        cost_estimate=cost(rows, 3.6, 16),
        name="feed_rows",
    )(place, x, gain, next_gain, *pieces, *([] if leaving else first))


def feed_back_kernel(n_pieces, meta, e_ref, x_ref, gain_ref, slope_ref, b_ref, h_ref, *refs):
    pieces, refs = refs[:n_pieces], refs[n_pieces:]
    dx_ref, dgain_ref, eb_ref, eu_ref, sent_ref, room, sems = refs
    step = pl.program_id(0)
    fetch_quarter(step, feed_copies(pieces, meta, room, sems))
    chunks = chunks_of(x_ref.shape[0])

    @pl.when(step == 0)
    def _():
        for rows in chunks:
            eb_ref[rows, :] = e_ref[rows, :].astype(BF16)
            dx_ref[rows, :] = jnp.zeros_like(dx_ref[rows, :])

    slope = slope_ref[...].astype(F32)
    eu_ref[...] = (rows_nt(eb_ref[...], room[step, 1]) * slope).astype(BF16)
    dx_ref[...] += rows_nt(eu_ref[...], room[step, 0])

    @pl.when(step % 2 == 1)
    def _():
        for kind, (left, right) in enumerate(((b_ref, eu_ref), (h_ref, eb_ref))):
            delta = rows_tn(left[...], right[...])
            for p in range(PARTS):
                rows = pl.ds(pl.multiple_of((meta[0] ^ p) * PIECE, PIECE), PIECE)
                sent_ref[0, kind, rows, :] = delta[p * PIECE : (p + 1) * PIECE].astype(BF16)

    @pl.when(step == 3)
    def _():
        gain_total = jnp.zeros((1, D), F32)
        for rows in chunks:
            part, gain_part = norm_back(x_ref[rows, :], gain_ref[...], dx_ref[rows, :])
            dx_ref[rows, :] = e_ref[rows, :].astype(F32) + part
            gain_total = gain_total + gain_part
        dgain_ref[...] = gain_total


def feed_back(meta, delta, x, gain, slope, pieces, b, h):
    rows = x.shape[0]
    fixed = pl.BlockSpec((rows, D), lambda q: (0, 0))
    moving = pl.BlockSpec((rows, D), lambda q: (0, q))
    narrow = pl.BlockSpec((1, D), lambda q: (0, 0))
    hidden = pl.BlockSpec((rows, D), lambda q: (0, 2 * (q // 2) + 1))
    return pl.pallas_call(
        functools.partial(feed_back_kernel, len(pieces)),
        grid=(4,),
        in_specs=[SCALARS, fixed, fixed, narrow, moving, fixed, hidden]
        + [ANYWHERE] * len(pieces),
        out_specs=[fixed, narrow, fixed, moving]
        + [pl.BlockSpec((1, 2, D, D), lambda q: (q // 2, 0, 0, 0))],
        out_shape=[
            jax.ShapeDtypeStruct((rows, D), F32),
            jax.ShapeDtypeStruct((1, D), F32),
            jax.ShapeDtypeStruct((rows, D), BF16),
            jax.ShapeDtypeStruct((rows, 4 * D), BF16),
            jax.ShapeDtypeStruct((2, 2, D, D), BF16),
        ],
        scratch_shapes=[pltpu.VMEM((4, 2, D, D), BF16), pltpu.SemaphoreType.DMA((16,))],
        compiler_params=pltpu.CompilerParams(vmem_limit_bytes=ROOM),
        cost_estimate=cost(rows, 5, 19),
        name="feed_back",
    )(meta, delta, x, gain, slope, b, h, *pieces)


def feed_weights_kernel(place, eu_ref, *refs):
    h_refs, (b_ref, eb_ref, out_ref) = refs[:-3], refs[-3:]
    j, kind = pl.program_id(0), pl.program_id(1)

    def put(delta):
        for p in range(PARTS):
            rows = pl.ds(pl.multiple_of((place[0] ^ p) * PIECE, PIECE), PIECE)
            out_ref[0, 0, rows, :] = delta[p * PIECE : (p + 1) * PIECE].astype(BF16)

    @pl.when(kind == 0)
    def _():
        put(rows_tn(b_ref[...], eu_ref[...]))

    for span, h_ref in enumerate(h_refs):

        @pl.when(jnp.logical_and(kind == 1, jnp.logical_or(len(h_refs) == 1, j == span)))
        def _(h_ref=h_ref):
            put(rows_tn(h_ref[...], eb_ref[...]))


def feed_weights(place, eu, h, b, eb, first):
    rows = b.shape[0]
    fixed = pl.BlockSpec((rows, D), lambda j, kind, place: (0, 0))
    moving = pl.BlockSpec((rows, D), lambda j, kind, place: (0, 2 * j + first))
    hidden = [moving]
    if len(h) == 2:
        hidden = [pl.BlockSpec((rows, D), lambda j, kind, place: (0, first))] * 2
    return pl.pallas_call(
        feed_weights_kernel,
        grid_spec=pltpu.PrefetchScalarGridSpec(
            num_scalar_prefetch=1,
            grid=(2, 2),
            in_specs=[moving] + hidden + [fixed, fixed],
            out_specs=pl.BlockSpec((1, 1, D, D), lambda j, kind, place: (j, kind, 0, 0)),
        ),
        out_shape=jax.ShapeDtypeStruct((2, 2, D, D), BF16),
        compiler_params=pltpu.CompilerParams(vmem_limit_bytes=ROOM),
        cost_estimate=cost(rows, 4, 6),
        name="feed_weights",
    )(place, eu, *h, b, eb)


def turn_back_kernel(
    meta, side, encoded, gain, context, returned, radar_part, cotangent, out, gain_out
):
    cut = context.shape[0]

    @pl.when(side[0] == 1)
    def _():
        out[:cut] = returned[...].astype(F32)
        out[cut:] = radar_part[...]
        gain_out[...] = jnp.zeros_like(gain_out)

    @pl.when(side[0] == 0)
    def _():
        total = jnp.zeros_like(gain_out)
        for part, incoming in enumerate((context, returned)):
            rows = slice(part * cut, (part + 1) * cut)
            delta, gain_part = norm_back(encoded[rows], gain[...], incoming[...].astype(F32))
            total = total + gain_part
            out[rows] = delta
        gain_out[...] = total

        def one_image(i, carry):
            rows = pl.ds(pl.multiple_of(i * SLOTS, 8), SLOTS)
            seen = lax.broadcasted_iota(jnp.int32, (SLOTS, 1), 0) < meta[3 + i]
            out[rows] += jnp.where(seen, cotangent[i].astype(F32), 0.0)
            return carry

        lax.fori_loop(0, cotangent.shape[0], one_image, 0)


def turn_back(meta, modality, encoded, gain, context, returned, radar_part, cotangent):
    return pl.pallas_call(
        turn_back_kernel,
        in_specs=[SCALARS] * 2 + [WHOLE] * 6,
        out_specs=[WHOLE] * 2,
        out_shape=[
            jax.ShapeDtypeStruct(encoded.shape, F32),
            jax.ShapeDtypeStruct((1, D), F32),
        ],
        compiler_params=pltpu.CompilerParams(vmem_limit_bytes=ROOM),
        cost_estimate=cost(816, 5, 0),
        name="turn_back",
    )(meta, modality[None], encoded, gain, context, returned, radar_part, cotangent)


def relative_parts(parts, own):
    return jnp.stack(
        [lax.dynamic_index_in_dim(parts, r ^ own, 0, keepdims=False) for r in range(PARTS)]
    )


def pack_mix(triple, out_weight):
    return jnp.concatenate([triple.transpose(1, 2, 0), out_weight[None]], 0)


def piece_of(quarter, part):
    if quarter.shape[1] == PIECE:
        return lax.dynamic_index_in_dim(quarter, part, 0, keepdims=False)
    return lax.dynamic_slice_in_dim(quarter, part * PIECE, PIECE, 1)


def unpack_mix(parts):
    return parts[:3].transpose(2, 0, 1).astype(F32), parts[3].astype(F32)


def unpack_feed_kernel(place, *refs):
    refs, (expand_ref, reduce_ref) = refs[:-2], refs[-2:]
    step = PIECE // 2
    for n in range(len(refs) // 5):

        @pl.when(pl.program_id(0) == n)
        def _(n=n):
            part, low, high, low_far, high_far = refs[5 * n : 5 * n + 5]
            for kind, out in enumerate((expand_ref, reduce_ref)):
                lows = [part[kind, :step], low[kind], low_far[0, kind], low_far[1, kind]]
                highs = [part[kind, step:], high_far[0, kind], high[kind], high_far[1, kind]]
                for p in range(PARTS):
                    start = pl.multiple_of((place[0] ^ p) * PIECE, PIECE)
                    out[0, pl.ds(start, step), :] = lows[p].astype(F32)
                    out[0, pl.ds(start + step, step), :] = highs[p].astype(F32)


def unpack_feed(place, *gathered):
    count = len(gathered)
    operands = [piece for pieces in gathered for piece in pieces]
    if count == 1:
        out = pl.BlockSpec((1, D, D), lambda n, place: (n, 0, 0))
    else:
        out = pl.BlockSpec((1, D, D), lambda n, place: (n ^ place[2], 0, 0))
    shape = jax.ShapeDtypeStruct((count, D, D), F32)
    return pl.pallas_call(
        unpack_feed_kernel,
        grid_spec=pltpu.PrefetchScalarGridSpec(
            num_scalar_prefetch=1,
            grid=(count,),
            in_specs=[WHOLE] * len(operands),
            out_specs=[out, out],
        ),
        out_shape=[shape, shape],
        compiler_params=pltpu.CompilerParams(vmem_limit_bytes=ROOM),
        cost_estimate=cost(816, 1, 2 * count),
        name="unpack_feed",
    )(place, *operands)


def fetch_relayed(zero, three):
    return (zero, swap(zero, dp_mask=1), swap(zero, dp_mask=2), three)


def fetch_beside(pieces):
    return pieces + tuple(swap(piece, head_mask=CORE) for piece in pieces)


AXES = {"x": (0, 0, ACROSS), "y": (3, 1, 0), "z": (2, 2, 0)}
THIRDS = ("xyz", "yzx", "zxy")
HALVES = ("xyz", "yzx")
LAST = ("xyz", "yxz")
CROSS = ("yxz", "zxy")


def halves(array, axis):
    return lax.slice_in_dim(array, 0, 1, axis=axis), lax.slice_in_dim(array, 1, 2, axis=axis)


def add_split(keep, beside, orders=THIRDS):
    kinds, rows = keep.shape[1:3]
    kinds, rows = (1, rows) if kinds == PARTS else (kinds, rows // PARTS)
    total = (keep + beside).reshape(2, kinds, 2, 2, rows, D)
    step = PIECE // len(orders)
    cuts = [i * step for i in range(len(orders))] + [rows]
    return [total[:, :, :, :, low:high] for low, high in zip(cuts[:-1], cuts[1:])]


def link_send(shares, stage, orders=THIRDS):
    out = []
    for array, order in zip(shares, orders, strict=True):
        axis, dp_mask, head_mask = AXES[order[stage]]
        keep, sent = halves(array, axis)
        out.append((keep, swap(sent, dp_mask, head_mask)))
    return out


def link_first(keep, beside, orders=THIRDS):
    shape = (2, -1, 2, 2, PIECE, D)
    step = PIECE // len(orders)

    def split(keep, beside):
        out = []
        for i, order in enumerate(orders):
            rows = slice(i * step, (i + 1) * step)
            share = keep[:, :, :, :, rows] + beside[:, :, :, :, rows]
            out.append(halves(share, AXES[order[0]][0]))
        return out

    return glue(split, keep.reshape(shape), beside.reshape(shape))


def link_swap(parts, stage, orders=THIRDS):
    return [
        (keep, swap(sent, *AXES[order[stage]][1:]))
        for (keep, sent), order in zip(parts, orders, strict=True)
    ]


def link_next(pairs, stage, orders=THIRDS):
    def split(pairs):
        return [
            halves(keep + received, AXES[order[stage]][0])
            for (keep, received), order in zip(pairs, orders, strict=True)
        ]

    return link_swap(glue(split, pairs), stage, orders)


def link_add(pairs):
    return [keep + received for keep, received in pairs]


def join(shares):
    return jnp.concatenate([share[0, :, 0, 0] for share in shares], 1)


def rest_send(array, stop):
    mask = PARTS
    while 2 * mask < stop:
        array = array + swap(array, dp_mask=mask)
        mask *= 2
    return array, swap(array, dp_mask=mask)


def rest_add(pair):
    return pair[0] + pair[1]


def over_rest(array, stop):
    mask = PARTS
    while mask < stop:
        array = array + swap(array, dp_mask=mask)
        mask *= 2
    return array


def gather_first(part):
    step = PIECE // 2
    return part, swap(part[:, :step], dp_mask=1), swap(part[:, step:PIECE], dp_mask=2)


def gather_second(first):
    part, low, high = first
    step = PIECE // 2
    return (
        part,
        low,
        high,
        swap(jnp.stack([part[:, :step], low]), dp_mask=2),
        swap(jnp.stack([part[:, step:PIECE], high]), dp_mask=1),
    )


def gather_join(pieces):
    part, low, high, low_far, high_far = pieces
    step = PIECE // 2
    lows = [part[:, :step], low, low_far[0], low_far[1]]
    highs = [part[:, step:PIECE], high_far[0], high, high_far[1]]
    return jnp.stack([jnp.concatenate(pair, 1) for pair in zip(lows, highs, strict=True)])


def on_device(
    tokens,
    cotangent,
    ratios,
    patch_index,
    encoder_gains,
    encoder_attend_in,
    encoder_attend_out,
    encoder_expand,
    encoder_reduce,
    uniting_gains,
    uniting_query,
    uniting_pair,
    uniting_attend_out,
    uniting_expand,
    uniting_reduce,
):
    groups = lax.axis_size("dp")
    side = groups // 2
    group, lane = lax.axis_index("dp"), lax.axis_index("head")
    radar = group >= side
    modality = radar.astype(jnp.int32)
    own = group % PARTS
    images = tokens.shape[0]
    some = images // 2
    cut = some * SLOTS

    def select_slot(stacked):
        return lax.dynamic_index_in_dim(stacked, modality, 0, keepdims=False)

    gains = select_slot(encoder_gains)[:, None]
    uni_gains = uniting_gains[:, None]

    own_ratios = lax.dynamic_slice_in_dim(ratios, lane * images, images, 0)
    patches = lax.dynamic_slice_in_dim(patch_index, lane * images, images, 0)
    counts = PATCHES * (100 - own_ratios) // 100
    first = modality * some
    meta = jnp.concatenate([jnp.stack([own, lane, 0 * first]), counts])
    pair_meta = jnp.concatenate([jnp.stack([own, lane, first]), counts])
    place = jnp.stack([own, lane, modality])
    visible = (jnp.arange(SLOTS)[None, :] < counts[:, None])[:, :, None]
    queries = patches[:, None, :]
    row_gap = (patches // GRID)[:, :, None] - queries // GRID
    col_gap = (patches % GRID)[:, :, None] - queries % GRID
    distance = jnp.sqrt((row_gap * row_gap + col_gap * col_gap).astype(F32))
    per_lane = HEADS // lax.axis_size("head")
    heads = jnp.concatenate(
        [(lane ^ mask) * per_lane + jnp.arange(per_lane) for mask in range(4)]
    )
    slopes = 2.0 ** (-8.0 * (heads.astype(F32) + 1.0) / HEADS)

    mix_quarter = pack_mix(select_slot(encoder_attend_in), select_slot(encoder_attend_out))
    mix_zero = swap(piece_of(mix_quarter, own), head_mask=ACROSS)
    mix_near = (mix_quarter, swap(mix_quarter, head_mask=CORE))
    mix_quarter, encoder_expand, encoder_reduce = tie(
        mix_quarter, encoder_expand, encoder_reduce
    )
    feed_quarter = jnp.stack([select_slot(encoder_expand), select_slot(encoder_reduce)])
    feed_quarter, mix_quarter, mix_zero, flat, uni_feed_quarter, meta, slopes, distance = tie(
        feed_quarter,
        mix_quarter,
        mix_zero,
        tokens.reshape(-1, D),
        jnp.stack([uniting_expand, uniting_reduce]),
        meta,
        slopes,
        distance,
    )
    mix_pieces = fetch_relayed(
        mix_zero, swap(piece_of(mix_quarter, own ^ 3), head_mask=ACROSS)
    )
    feed_zero = swap(piece_of(feed_quarter, own), head_mask=ACROSS)
    feed_near = (feed_quarter, swap(feed_quarter, head_mask=CORE))

    normed_one, middle, *near = mix_forward(
        meta, slopes, flat, None, gains[0], None, mix_near, distance
    )
    middle, mix_pieces, feed_zero, feed_near = tie(middle, mix_pieces, feed_zero, feed_near)
    feed_quarter = feed_near[0]
    mix_far = fetch_beside(mix_pieces)
    feed_pieces = fetch_relayed(
        feed_zero, swap(piece_of(feed_quarter, own ^ 3), head_mask=ACROSS)
    )
    feed_zero, uniting_query, uniting_pair, uniting_attend_out = tie(
        feed_zero, uniting_query, uniting_pair, uniting_attend_out
    )
    uni_quarter = pack_mix(
        jnp.concatenate([uniting_query[:, None], uniting_pair], 1), uniting_attend_out
    )
    middle, mix_far, uni_feed_quarter = tie(middle, mix_far, uni_feed_quarter)
    uni_feed = (lax.all_gather(uni_feed_quarter, "head"),)
    middle, *far = mix_forward(
        meta, slopes, middle, None, None, normed_one, mix_far, distance, HEADS // 2
    )
    qkv, mixed, lse = zip(near, far)
    middle, feed_pieces, uni_quarter = tie(middle, feed_pieces, uni_quarter)
    feed_far = fetch_beside(feed_pieces)
    uni_zero = swap(piece_of(uni_quarter, own), head_mask=ACROSS)
    uni_three = swap(piece_of(uni_quarter, own ^ 3), head_mask=ACROSS)
    enc_mix, enc_feed = mix_near + mix_far, feed_near + feed_far

    *half_fed, leaving = feed_rows(place, middle, gains[1], uni_gains[0], enc_feed)
    leaving, half_fed, uni_zero = tie(leaving, half_fed, uni_zero)
    received = swap(leaving, dp_mask=side)
    uni_mix_pieces = fetch_relayed(uni_zero, uni_three)
    uni_mix_near = (uni_quarter, swap(uni_quarter, head_mask=CORE))
    encoded, normed_two, *stored, context = feed_rows(
        place, middle, gains[1], uni_gains[0], enc_feed, half_fed
    )
    hidden, bend = ([part] for part in stored)
    encoded, received, uni_mix_pieces = tie(encoded, received, uni_mix_pieces)
    uni_mix = uni_mix_near + fetch_beside(uni_mix_pieces)
    received, cotangent = tie(received, cotangent)
    sent_cotangent = swap(cotangent[:some], dp_mask=side)
    radar_rows = jnp.where(radar, encoded[cut:], received.astype(F32))
    context_rows = jnp.where(radar, received, context)

    uni_normed, uni_middle, *stored = mix_forward(
        pair_meta, slopes, radar_rows, context_rows, uni_gains[1], None, uni_mix, distance
    )
    uni_qkv, uni_mixed, uni_lse = ([part] for part in stored)
    uni_normed_two, joined, *stored = feed_forward(
        meta, uni_middle, uni_gains[2], None, uni_feed
    )
    uni_hidden, uni_bend = ([part] for part in stored)

    joined, sent_cotangent = tie(joined, sent_cotangent)
    joined_half = joined.reshape(some, SLOTS, D)
    other_half = [swap(joined_half[i : i + 1], dp_mask=side) for i in range(some)]
    pair_cotangent = jnp.where(radar, cotangent[some:], sent_cotangent)
    pair_visible = lax.dynamic_slice_in_dim(visible, first, some, 0)
    delta_joined = jnp.where(pair_visible, pair_cotangent, 0).reshape(-1, D)
    delta_middle, gain_three, eb, eu, sent = feed_back(
        meta,
        delta_joined,
        uni_middle,
        uni_gains[2],
        uni_bend[0],
        uni_feed,
        uni_normed_two,
        uni_hidden[0],
    )
    sent, eu, other_half[:2] = tie(sent, eu, other_half[:2])
    beside = swap(sent, head_mask=CORE)
    keep = feed_weights(place, eu, uni_hidden, uni_normed_two, eb, 0)
    keep, beside, other_half[2:] = tie(keep, beside, other_half[2:])
    uni_feed_parts, delta_middle = tie(link_first(keep, beside), delta_middle)
    uni_feed_pairs = link_swap(uni_feed_parts, 0)
    delta_radar, gain_two, dqkv, mix_eb, delta_context, leaving = mix_back(
        pair_meta,
        slopes,
        delta_middle,
        radar_rows,
        uni_gains[1],
        uni_qkv,
        uni_lse,
        uni_mix,
        distance,
        True,
    )
    leaving, dqkv, uni_feed_pairs = tie(leaving, dqkv, uni_feed_pairs)
    other_half = jnp.concatenate(other_half, 0)
    returned = swap(leaving, dp_mask=side)
    uni_feed_pairs = link_next(uni_feed_pairs, 1)
    keep, sent = mix_weights(place, dqkv, uni_mixed, uni_normed, context_rows, mix_eb)
    layer_output = jnp.where(
        visible,
        jnp.where(
            radar,
            jnp.concatenate([other_half, joined_half], 0),
            encoded.astype(BF16).reshape(images, SLOTS, D),
        ),
        0,
    )
    sent, returned, uni_feed_pairs, layer_output = tie(
        sent, returned, uni_feed_pairs, layer_output
    )
    beside = swap(sent, head_mask=CORE)
    uni_feed_pairs = link_send(link_add(uni_feed_pairs), 2)
    delta_encoded, gain_one = turn_back(
        meta, modality, encoded, uni_gains[0], delta_context, returned, delta_radar, cotangent
    )
    delta_encoded, beside, uni_feed_pairs = tie(delta_encoded, beside, uni_feed_pairs)
    uni_mix_sum, uni_feed_part = add_split(keep, beside, CROSS), join(link_add(uni_feed_pairs))
    delta_encoded, uni_mix_sum, uni_feed_part = tie(delta_encoded, uni_mix_sum, uni_feed_part)
    uni_feed_rest = rest_send(uni_feed_part, groups)
    uni_mix_pairs = link_send(uni_mix_sum, 0, CROSS)

    delta_middle, gain_b, eb, eu, sent = feed_back(
        meta, delta_encoded, middle, gains[1], bend[0], enc_feed, normed_two, hidden[0]
    )
    sent, eu, uni_feed_rest, uni_mix_pairs = tie(sent, eu, uni_feed_rest, uni_mix_pairs)
    uni_feed_part, uni_mix_sum = rest_add(uni_feed_rest), link_add(uni_mix_pairs)
    eu, uni_feed_part, uni_mix_sum = tie(eu, uni_feed_part, uni_mix_sum)
    beside = swap(sent, head_mask=CORE)
    uni_feed_near = swap(uni_feed_part, dp_mask=1)
    uni_mix_pairs = link_send(uni_mix_sum, 1, CROSS)
    keep = feed_weights(place, eu, hidden, normed_two, eb, 0)
    keep, beside, uni_feed_near, uni_mix_pairs = tie(keep, beside, uni_feed_near, uni_mix_pairs)
    uni_feed_near = jnp.stack([uni_feed_part, uni_feed_near])
    enc_feed_sum, uni_mix_sum = add_split(keep, beside, HALVES), link_add(uni_mix_pairs)
    delta_middle, enc_feed_sum, uni_mix_sum, uni_feed_near = tie(
        delta_middle, enc_feed_sum, uni_mix_sum, uni_feed_near
    )
    enc_feed_pairs = link_send(enc_feed_sum, 0, HALVES)
    uni_mix_pairs = link_send(uni_mix_sum, 2, CROSS)
    uni_feed_far = swap(uni_feed_near, dp_mask=2)
    delta_inputs, gain_a, dqkv, eb = mix_back(
        meta, slopes, delta_middle, flat, gains[0], qkv, lse, enc_mix, distance, False
    )
    dqkv, enc_feed_pairs, uni_mix_pairs, uni_feed_far = tie(
        dqkv, enc_feed_pairs, uni_mix_pairs, uni_feed_far
    )
    enc_feed_sum, uni_mix_part = link_add(enc_feed_pairs), join(link_add(uni_mix_pairs))
    dqkv, enc_feed_sum, uni_mix_part = tie(dqkv, enc_feed_sum, uni_mix_part)
    enc_feed_pairs = link_send(enc_feed_sum, 1, HALVES)
    uni_mix_rest = rest_send(uni_mix_part, groups)

    totals = (gain_a, gain_b, gain_one, gain_two, gain_three)
    keep, sent = mix_weights(place, dqkv, mixed, normed_one, normed_one, eb, totals)
    sent, enc_feed_pairs, uni_mix_rest = tie(sent, enc_feed_pairs, uni_mix_rest)
    uni_mix_gather = gather_first(rest_add(uni_mix_rest))
    beside = swap(sent, head_mask=CORE)
    enc_feed_pairs = link_send(link_add(enc_feed_pairs), 2, HALVES)
    enc_mix_pairs = link_send(add_split(keep, beside, LAST), 0, LAST)
    feed_part = over_rest(join(link_add(enc_feed_pairs)), side)
    feed_other = swap(feed_part, dp_mask=side)
    enc_mix_pairs, feed_part, uni_mix_gather = tie(enc_mix_pairs, feed_part, uni_mix_gather)
    enc_mix_pairs = link_send(link_add(enc_mix_pairs), 1, LAST)
    feed_gather = gather_first(feed_part)
    enc_mix_pairs = link_send(link_add(enc_mix_pairs), 2, LAST)
    enc_mix_pairs, feed_gather = tie(enc_mix_pairs, feed_gather)
    feed_gather = gather_second(feed_gather)
    enc_mix_pairs, feed_other = tie(enc_mix_pairs, feed_other)
    mix_part = over_rest(join(link_add(enc_mix_pairs)), side)
    mix_part, feed_other = tie(mix_part, feed_other)
    mix_other = swap(mix_part, dp_mask=side)
    feed_other_gather = gather_first(feed_other)
    feed_gather, uni_feed_near = tie(feed_gather, uni_feed_near)
    uni_feed_all = relative_parts(jnp.concatenate([uni_feed_near, uni_feed_far], 0), own)
    fexpand, freduce = (uni_feed_all[:, i].reshape(D, D).astype(F32) for i in range(2))
    mix_other, feed_other_gather, feed_gather, uni_mix_gather, fexpand, freduce = tie(
        mix_other, feed_other_gather, feed_gather, uni_mix_gather, fexpand, freduce
    )
    mix_gather = gather_first(jnp.concatenate([mix_part, mix_other], 0))
    feed_other_gather = gather_second(feed_other_gather)
    mix_gather, uni_mix_gather = tie(mix_gather, uni_mix_gather)
    mix_gather, uni_mix_gather = gather_second(mix_gather), gather_second(uni_mix_gather)
    totals = (mix_part + mix_other)[0, PIECE:].astype(F32)

    ftriple, fout = unpack_mix(relative_parts(gather_join(uni_mix_gather)[:, 0], own))
    expands, reduces = unpack_feed(place, feed_gather, feed_other_gather)
    mix_all = gather_join(mix_gather)
    mine, theirs = mix_all[:, 0], mix_all[:, 1]
    mixes = [
        unpack_mix(relative_parts(part, own))
        for part in (jnp.where(radar, theirs, mine), jnp.where(radar, mine, theirs))
    ]

    return (
        layer_output,
        delta_inputs.reshape(images, SLOTS, D),
        totals[:4].reshape(2, 2, D),
        jnp.stack([mixes[0][0], mixes[1][0]]),
        jnp.stack([mixes[0][1], mixes[1][1]]),
        expands,
        reduces,
        totals[4:7],
        ftriple[:, 0],
        ftriple[:, 1:],
        fout,
        fexpand,
        freduce,
    )


def solution(mesh):
    return jax.shard_map(
        on_device,
        mesh=mesh,
        in_specs=(
            P(("dp", "head"), None, None),
            P(("dp", "head"), None, None),
            P("dp"),
            P("dp", None),
            P(),
            P(None, None, None, "head"),
            P(None, "head", None),
            P(None, None, "head"),
            P(None, "head", None),
            P(),
            P(None, "head"),
            P(None, None, "head"),
            P("head", None),
            P(None, "head"),
            P("head", None),
        ),
        out_specs=(
            P(("dp", "head"), None, None),
            P(("dp", "head"), None, None),
            P(),
            P(None, None, None, "head"),
            P(None, "head", None),
            P(None, None, "head"),
            P(None, "head", None),
            P(),
            P(None, "head"),
            P(None, None, "head"),
            P("head", None),
            P(None, "head"),
            P("head", None),
        ),
        check_vma=False,
    )
```

```python
import functools

import jax
import jax.numpy as jnp
from jax import lax
from jax.experimental import pallas as pl
from jax.experimental.pallas import tpu as pltpu
from jax.sharding import PartitionSpec as P

D = 768
HEADS = 12
HEAD_DIM = 64
GRID = 15
PATCHES = 225
SLOTS = 136
PARTS = 4
PIECE = D // PARTS
CORE, ACROSS = 1, 2
SCALE = HEAD_DIM**-0.5

EPSILON = 1e-06
NEGATIVE = -1e30
F32, BF16 = jnp.float32, jnp.bfloat16
WHOLE = pl.BlockSpec(memory_space=pltpu.VMEM)
ANYWHERE = pl.BlockSpec(memory_space=pl.ANY)
SCALARS = pl.BlockSpec(memory_space=pltpu.SMEM)
ROOM = 56 << 20


def cost(rows, fixed, each):
    return pl.CostEstimate(
        flops=int((fixed + each * rows / 816) * 1e7), bytes_accessed=1, transcendentals=0
    )


def swap(array, dp_mask=0, head_mask=0, senders=None):
    groups, lanes = lax.axis_size("dp"), lax.axis_size("head")
    pairs = [
        (g * lanes + h, (g ^ dp_mask) * lanes + (h ^ head_mask))
        for g in (range(groups) if senders is None else senders)
        for h in range(lanes)
    ]
    return lax.ppermute(array, ("dp", "head"), pairs)


def tie(*arrays):
    return lax.optimization_barrier(arrays)


def rows_nt(left, right):
    return lax.dot_general(left, right, (((1,), (1,)), ((), ())), preferred_element_type=F32)


def rows_nn(left, right):
    return lax.dot_general(left, right, (((1,), (0,)), ((), ())), preferred_element_type=F32)


def rows_tn(left, right):
    return lax.dot_general(left, right, (((0,), (0,)), ((), ())), preferred_element_type=F32)


def normalize(values):
    centered = values - jnp.mean(values, -1, keepdims=True)
    spread = lax.rsqrt(jnp.mean(centered * centered, -1, keepdims=True) + EPSILON)
    return centered * spread, spread


def layer_norm(values, gain):
    return normalize(values)[0] * gain


def norm_back(values, gain, incoming):
    unit, spread = normalize(values)
    scaled = incoming * gain
    delta = spread * (
        scaled
        - jnp.mean(scaled, -1, keepdims=True)
        - unit * jnp.mean(scaled * unit, -1, keepdims=True)
    )
    return delta, jnp.sum(incoming * unit, 0, keepdims=True)


def glue(function, *arrays):
    leaves, tree = jax.tree.flatten(arrays)
    results, result_tree = jax.tree.flatten(jax.eval_shape(function, *arrays))

    def kernel(*refs):
        values = tree.unflatten([ref[...] for ref in refs[: len(leaves)]])
        for ref, value in zip(refs[len(leaves) :], jax.tree.leaves(function(*values))):
            ref[...] = value

    out = pl.pallas_call(
        kernel,
        in_specs=[WHOLE] * len(leaves),
        out_specs=[WHOLE] * len(results),
        out_shape=results,
        compiler_params=pltpu.CompilerParams(vmem_limit_bytes=ROOM),
        cost_estimate=cost(816, 1, 0),
        name="glue",
    )(*leaves)
    return result_tree.unflatten(out)


def chunks_of(rows):
    step = 2 * SLOTS if rows % (2 * SLOTS) == 0 else rows
    return [slice(start, start + step) for start in range(0, rows, step)]


QUARTERS_IN = {1: 4, 2: 2, 8: 2, 10: 4}


def feed_copies(pieces, meta, room, sems):
    if len(pieces) == 1:
        return [
            [pltpu.make_async_copy(pieces[0].at[meta[1] ^ q], room.at[q], sems.at[q])]
            for q in range(4)
        ]
    near = len(pieces) % 8
    copies = [
        [pltpu.make_async_copy(pieces[q], room.at[q], sems.at[q])] for q in range(near)
    ]
    for q in range(near, near + (len(pieces) - near) // PARTS):
        group = []
        for r in range(PARTS):
            at = near + (q - near) * PARTS + r
            rows = pl.ds(pl.multiple_of((meta[0] ^ r) * PIECE, PIECE), PIECE)
            group.append(
                pltpu.make_async_copy(pieces[at], room.at[q, :, rows, :], sems.at[at])
            )
        copies.append(group)
    return copies


def mix_copies(pieces, meta, room, sems):
    near = len(pieces) % 8
    copies = [
        pltpu.make_async_copy(
            pieces[q], room.at[:, pl.ds(q * PIECE, PIECE), :], sems.at[q]
        )
        for q in range(near)
    ]
    for at in range(near, len(pieces)):
        q, r = divmod(at - near, PARTS)
        rows = pl.ds((near + q) * PIECE, PIECE)
        copies.append(
            pltpu.make_async_copy(pieces[at], room.at[meta[0] ^ r, rows, :], sems.at[at])
        )
    return copies


SIZES = (64, 96, 128, SLOTS)


def by_size(count, branch):
    which = sum((count > size).astype(jnp.int32) for size in SIZES[:-1])
    lax.switch(which, [functools.partial(branch, size) for size in SIZES])


def two_heads(block, first):
    zero = jnp.zeros_like(block)
    return jnp.concatenate(
        [jnp.where(first, block, zero), jnp.where(first, zero, block)], 0
    ).astype(BF16)


def pick_heads(stacked, first):
    size = stacked.shape[0] // 2
    return jnp.where(first, stacked[:size], stacked[size:])


def image_setup(size, distance_ref, image, count):
    first = lax.broadcasted_iota(jnp.int32, (size, 2 * HEAD_DIM), 1) < HEAD_DIM
    distance = distance_ref[image, :size, :size]
    distance = jnp.concatenate([distance, distance], 1)
    seen = lax.broadcasted_iota(jnp.int32, (size, 1), 0) < count
    lanes = lax.broadcasted_iota(jnp.int32, (1, 2 * size), 1) < size

    def scores_of(keys, queries, slopes, head):
        slope = jnp.where(lanes, slopes[head], slopes[head + 1])
        return jnp.where(seen, rows_nt(keys, queries) - distance * slope, NEGATIVE)

    return first, scores_of


def mix_forward_kernel(local, cross, images, head, n_pieces, *refs):
    meta, slopes, x_ref = refs[:3]
    refs = refs[3:]
    if cross:
        c_ref, refs = refs[0], refs[1:]
    if local:
        gain_ref, refs = refs[0], refs[1:]
    else:
        a_ref, refs = refs[0], refs[1:]
    pieces, refs = refs[:n_pieces], refs[n_pieces:]
    distance_ref, refs = refs[0], refs[1:]
    if local:
        a_ref, refs = refs[0], refs[1:]
    out_ref, qkv_ref, o_ref, lse_ref, room, wide, sems = refs
    copies = mix_copies(pieces, meta, room, sems)
    for copy in copies:
        copy.start()
    chunks = chunks_of(images * SLOTS)
    if local:
        for rows in chunks:
            a_ref[rows, :] = layer_norm(x_ref[rows, :].astype(F32), gain_ref[...]).astype(BF16)
    for copy in copies:
        copy.wait()
    width = o_ref.shape[1]
    if cross:
        wide[:, :width] = rows_nt(a_ref[...], room[0])
        wide[:, width:] = rows_nt(c_ref[...], room[1:3].reshape(2 * width, D))
    else:
        wide[...] = rows_nt(a_ref[...], room[:3].reshape(3 * width, D))

    def one_image(i, carry):
        image = meta[2] + i
        start = pl.multiple_of(i * SLOTS, 8)
        qkv_ref[i] = wide[pl.ds(start, SLOTS), :].astype(BF16)

        def work(size):
            first, scores_of = image_setup(size, distance_ref, image, meta[3 + image])
            rows = pl.ds(start, size)
            for pair in range(width // (2 * HEAD_DIM)):
                low, high = pair * 2 * HEAD_DIM, (pair + 1) * 2 * HEAD_DIM
                k = wide[rows, width + low : width + high].astype(BF16)
                v = wide[rows, 2 * width + low : 2 * width + high].astype(BF16)
                queries = two_heads(
                    wide[rows, low:high].astype(BF16).astype(F32) * SCALE, first
                )
                scores = scores_of(k, queries, slopes, head + 2 * pair)
                top = jnp.max(scores, 0, keepdims=True)
                exponent = jnp.exp(scores - top)
                total = jnp.sum(exponent, 0, keepdims=True)
                weights = (exponent * (1.0 / total)).astype(BF16)
                wide[rows, low:high] = pick_heads(rows_tn(weights, v), first)
                lse_ref[i, pair : pair + 1, : 2 * size] = top + jnp.log(total)
            if size < SLOTS:
                rest = pl.ds(pl.multiple_of(start + size, 8), SLOTS - size)
                wide[rest, :width] = jnp.zeros((SLOTS - size, width), F32)

        by_size(meta[3 + image], work)
        return carry

    lax.fori_loop(0, images, one_image, 0)
    for rows in chunks:
        o_ref[rows, :] = wide[rows, :width].astype(BF16)
    out_ref[...] = x_ref[...].astype(F32) + rows_nn(o_ref[...], room[3])


def mix_forward(meta, slopes, x, context, gain, normed, pieces, distance, head=0):
    images = x.shape[0] // SLOTS
    rows = images * SLOTS
    cross, local = context is not None, normed is None
    width = PIECE * QUARTERS_IN[len(pieces)]
    operands = [meta, slopes, x] + ([context] if cross else [])
    operands += [gain if local else normed, *pieces, distance]
    specs = [SCALARS] * 2 + [WHOLE] * (3 if cross else 2) + [ANYWHERE] * len(pieces) + [WHOLE]
    narrow = jax.ShapeDtypeStruct((rows, D), BF16)
    return pl.pallas_call(
        functools.partial(mix_forward_kernel, local, cross, images, head, len(pieces)),
        in_specs=specs,
        out_specs=[WHOLE] * (5 if local else 4),
        out_shape=([narrow] if local else [])
        + [
            jax.ShapeDtypeStruct((rows, D), F32),
            jax.ShapeDtypeStruct((images, SLOTS, 3 * width), BF16),
            jax.ShapeDtypeStruct((rows, width), BF16),
            jax.ShapeDtypeStruct((images, width // (2 * HEAD_DIM), 2 * SLOTS), F32),
        ],
        scratch_shapes=[
            pltpu.VMEM((4, width, D), BF16),
            pltpu.VMEM((rows, 3 * width), F32),
            pltpu.SemaphoreType.DMA((16,)),
        ],
        compiler_params=pltpu.CompilerParams(vmem_limit_bytes=ROOM),
        cost_estimate=cost(rows, 4, 8 * width / 384),
        name="mix_forward",
    )(*operands)


def mix_back_kernel(cross, images, spans, *refs):
    meta, slopes, e_ref, x_ref, gain_ref = refs[:5]
    refs = refs[5:]
    qkv_refs, lse_refs, refs = refs[:spans], refs[spans : 2 * spans], refs[2 * spans :]
    pieces, refs = refs[:10], refs[10:]
    distance_ref, dx_ref, dgain_ref, dqkv_ref, eb_ref = refs[:5]
    refs = refs[5:]
    if cross:
        dc_ref, leaving_ref, refs = refs[0], refs[1], refs[2:]
    room, inner_ref, wide, sems = refs
    copies = mix_copies(pieces, meta, room, sems)
    for copy in copies:
        copy.start()
    chunks = chunks_of(images * SLOTS)
    for rows in chunks:
        eb_ref[rows, :] = e_ref[rows, :].astype(BF16)
    for copy in copies:
        copy.wait()
    inner_ref[...] = rows_nt(eb_ref[...], room[3])

    width = D // spans

    def one_image(i, carry):
        image = meta[2] + i
        start = pl.multiple_of(i * SLOTS, 8)

        def work(size):
            first, scores_of = image_setup(size, distance_ref, image, meta[3 + image])
            rows = pl.ds(start, size)
            for pair in range(HEADS // 2):
                low, high = pair * 2 * HEAD_DIM, (pair + 1) * 2 * HEAD_DIM
                half, inside = divmod(pair, HEADS // 2 // spans)
                qkv_ref, lse_ref = qkv_refs[half], lse_refs[half]
                at, to = inside * 2 * HEAD_DIM, (inside + 1) * 2 * HEAD_DIM
                queries = two_heads(qkv_ref[i, :size, at:to].astype(F32) * SCALE, first)
                incoming = two_heads(inner_ref[rows, low:high], first)
                k = qkv_ref[i, :size, width + at : width + to]
                v = qkv_ref[i, :size, 2 * width + at : 2 * width + to]
                scores = scores_of(k, queries, slopes, 2 * pair)
                probable = jnp.exp(scores - lse_ref[i, inside : inside + 1, : 2 * size])
                delta_p = rows_nt(v, incoming)
                shared = jnp.sum(delta_p * probable, 0, keepdims=True)
                delta_s = (probable * (delta_p - shared)).astype(BF16)
                wide[rows, low:high] = pick_heads(rows_tn(delta_s, k), first) * SCALE
                wide[rows, D + low : D + high] = rows_nn(delta_s, queries)
                wide[rows, 2 * D + low : 2 * D + high] = rows_nn(
                    probable.astype(BF16), incoming
                )
            if size < SLOTS:
                rest = pl.ds(pl.multiple_of(start + size, 8), SLOTS - size)
                wide[rest, :] = jnp.zeros((SLOTS - size, 3 * D), F32)

        by_size(meta[3 + image], work)
        return carry

    lax.fori_loop(0, images, one_image, 0)
    for rows in chunks:
        dqkv_ref[rows, :] = wide[rows, :].astype(BF16)
    delta = rows_nn(dqkv_ref[:, :D], room[0])
    side = rows_nn(dqkv_ref[:, D : 2 * D], room[1]) + rows_nn(dqkv_ref[:, 2 * D :], room[2])
    if cross:
        dc_ref[...] = side.astype(BF16)
        inner_ref[...] = delta
    else:
        inner_ref[...] = delta + side
    gain_total = jnp.zeros((1, D), F32)
    for rows in chunks:
        part, gain_part = norm_back(x_ref[rows, :].astype(F32), gain_ref[...], inner_ref[rows, :])
        dx_ref[rows, :] = e_ref[rows, :] + part
        gain_total = gain_total + gain_part
    dgain_ref[...] = gain_total
    if cross:

        @pl.when(meta[2] > 0)
        def _():
            leaving_ref[...] = dc_ref[...]

        @pl.when(meta[2] == 0)
        def _():
            leaving_ref[...] = dx_ref[...].astype(BF16)


def mix_back(meta, slopes, delta, x, gain, qkv, lse, pieces, distance, cross):
    images = qkv[0].shape[0]
    rows = images * SLOTS
    wide_rows = jax.ShapeDtypeStruct((rows, D), BF16)
    return pl.pallas_call(
        functools.partial(mix_back_kernel, cross, images, len(qkv)),
        in_specs=[SCALARS] * 2
        + [WHOLE] * (3 + 2 * len(qkv))
        + [ANYWHERE] * len(pieces)
        + [WHOLE],
        out_specs=[WHOLE] * (6 if cross else 4),
        out_shape=[
            jax.ShapeDtypeStruct((rows, D), F32),
            jax.ShapeDtypeStruct((1, D), F32),
            jax.ShapeDtypeStruct((rows, 3 * D), BF16),
            wide_rows,
        ]
        + ([wide_rows] * 2 if cross else []),
        scratch_shapes=[
            pltpu.VMEM((4, D, D), BF16),
            pltpu.VMEM((rows, D), F32),
            pltpu.VMEM((rows, 3 * D), F32),
            pltpu.SemaphoreType.DMA((16,)),
        ],
        compiler_params=pltpu.CompilerParams(vmem_limit_bytes=ROOM),
        cost_estimate=cost(rows, 5, 23),
        name="mix_back",
    )(meta, slopes, delta, x, gain, *qkv, *lse, *pieces, distance)


def mix_weights_kernel(more, place, dqkv_ref, *refs):
    if more:
        *refs, scratch = refs
        refs, outs = refs[:-2], refs[-2:]
        refs = (*refs, scratch)
    else:
        refs, outs = refs[:-2], refs[-2:]
    if more:
        gain_refs, refs, gains_ref = refs[:5], refs[5:-1], refs[-1]
    o_refs, (a_ref, c_ref, eb_ref) = refs[:-3], refs[-3:]
    kind = pl.program_id(0)

    def put(first, delta):
        for q in range(delta.shape[0] // PIECE):
            part = delta[q * PIECE : (q + 1) * PIECE].astype(BF16)
            outs[(first + q) % 2][(first + q) // 2, 0, :PIECE] = part

    @pl.when(kind == 0)
    def _():
        put(0, rows_tn(dqkv_ref[...], a_ref[...]))

    @pl.when(jnp.logical_or(kind == 1, kind == 2))
    def _():
        put(0, rows_tn(dqkv_ref[...], c_ref[...]))

    @pl.when(kind == 3)
    def _():
        for span, o_ref in enumerate(o_refs):
            put(span * 4 // len(o_refs), rows_tn(o_ref[...], eb_ref[...]))

    if more:
        gains_ref[...] = jnp.zeros_like(gains_ref)
        for i in range(2):
            gains_ref[pl.ds(2 * place[2] + i, 1), :] = gain_refs[i][...]
        for i in range(2, 5):
            gains_ref[2 + i : 3 + i, :] = gain_refs[i][...]
        for out in outs:
            for half in range(2):
                out[half, 0, PIECE:] = gains_ref[...].astype(BF16)


def mix_weights(place, dqkv, o, a, c, eb, gains=None):
    rows = a.shape[0]
    more = gains is not None
    fixed = pl.BlockSpec((rows, D), lambda kind, place: (0, 0))
    narrow = pl.BlockSpec((rows, D // len(o)), lambda kind, place: (0, 0))
    tall = PIECE + (16 if more else 0)
    out = pl.BlockSpec((2, 1, tall, D), lambda kind, place: (0, kind ^ place[0], 0, 0))
    shape = jax.ShapeDtypeStruct((2, PARTS, tall, D), BF16)
    return pl.pallas_call(
        functools.partial(mix_weights_kernel, more),
        grid_spec=pltpu.PrefetchScalarGridSpec(
            num_scalar_prefetch=1,
            grid=(4,),
            in_specs=[pl.BlockSpec((rows, D), lambda kind, place: (0, jnp.minimum(kind, 2)))]
            + [pl.BlockSpec((1, D), lambda kind, place: (0, 0))] * (5 if more else 0)
            + [narrow] * len(o)
            + [fixed] * 3,
            out_specs=[out, out],
            scratch_shapes=[pltpu.VMEM((16, D), F32)] if more else [],
        ),
        out_shape=[shape, shape],
        compiler_params=pltpu.CompilerParams(vmem_limit_bytes=ROOM),
        cost_estimate=cost(rows, 3.5, 7),
        name="mix_weights",
    )(place, dqkv, *(gains if more else []), *o, a, c, eb)


def fetch_quarter(step, copies):
    @pl.when(step == 0)
    def _():
        for group in copies[:2]:
            for copy in group:
                copy.start()

    for q, group in enumerate(copies):

        @pl.when(step == q)
        def _(q=q, group=group):
            for copy in group:
                copy.wait()
            for later in copies[q + 2 : q + 3]:
                for copy in later:
                    copy.start()


def feed_forward_kernel(local, n_pieces, meta, x_ref, norm_ref, *refs):
    pieces, refs = refs[:n_pieces], refs[n_pieces:]
    if local:
        b_ref, refs = refs[0], refs[1:]
    else:
        b_ref = norm_ref
    out_ref, h_ref, g_ref, room, sems, y_ref = refs
    step = pl.program_id(0)
    fetch_quarter(step, feed_copies(pieces, meta, room, sems))

    @pl.when(step == 0)
    def _():
        for rows in chunks_of(x_ref.shape[0]):
            values = x_ref[rows, :]
            y_ref[rows, :] = values
            if local:
                b_ref[rows, :] = layer_norm(values, norm_ref[...]).astype(BF16)

    before = rows_nn(b_ref[...], room[step, 0])
    bell = jnp.exp(-0.5 * before * before) * 0.3989422804014327
    share = 0.5 * (1.0 + lax.erf(before * 0.7071067811865476))
    h_ref[...] = (before * share).astype(BF16)
    g_ref[...] = (share + before * bell).astype(BF16)
    y_ref[...] += rows_nn(h_ref[...], room[step, 1])

    @pl.when(step == pl.num_programs(0) - 1)
    def _():
        out_ref[...] = y_ref[...].astype(BF16)


def feed_forward(meta, x, gain, normed, pieces):
    rows = x.shape[0]
    local = normed is None
    quarters = QUARTERS_IN[len(pieces)]
    fixed = pl.BlockSpec((rows, D), lambda q: (0, 0))
    moving = pl.BlockSpec((rows, D), lambda q: (0, q))
    hidden = jax.ShapeDtypeStruct((rows, quarters * D), BF16)
    return pl.pallas_call(
        functools.partial(feed_forward_kernel, local, len(pieces)),
        grid=(quarters,),
        in_specs=[SCALARS, fixed, pl.BlockSpec((1, D), lambda q: (0, 0)) if local else fixed]
        + [ANYWHERE] * len(pieces),
        out_specs=([fixed] if local else []) + [fixed, moving, moving],
        out_shape=([jax.ShapeDtypeStruct((rows, D), BF16)] if local else [])
        + [jax.ShapeDtypeStruct((rows, D), BF16), hidden, hidden],
        scratch_shapes=[
            pltpu.VMEM((quarters, 2, D, D), BF16),
            pltpu.SemaphoreType.DMA((16,)),
            pltpu.VMEM((rows, D), F32),
        ],
        compiler_params=pltpu.CompilerParams(vmem_limit_bytes=ROOM),
        cost_estimate=cost(rows, 3.6, 4 * quarters),
        name="feed_forward",
    )(meta, x, gain if local else normed, *pieces)


def feed_rows_kernel(leaving, meta, x_ref, gain_ref, next_gain_ref, *refs):
    pieces, refs = refs[:10], refs[10:]
    if not leaving:
        refs = refs[4:]
    y_ref, b_ref, h_ref, g_ref, out_ref, room, sems = refs
    step = pl.program_id(0)
    fetch_quarter(step, feed_copies(pieces, meta, room, sems))

    @pl.when(step == 0)
    def _():
        values = x_ref[...]
        y_ref[...] = values
        b_ref[...] = layer_norm(values, gain_ref[...]).astype(BF16)

    before = rows_nn(b_ref[...], room[step, 0])
    bell = jnp.exp(-0.5 * before * before) * 0.3989422804014327
    share = 0.5 * (1.0 + lax.erf(before * 0.7071067811865476))
    h_ref[...] = (before * share).astype(BF16)
    g_ref[...] = (share + before * bell).astype(BF16)
    y_ref[...] += rows_nn(h_ref[...], room[step, 1])

    @pl.when(jnp.logical_and(step == 3, jnp.logical_or(not leaving, meta[2] == 0)))
    def _():
        out_ref[...] = layer_norm(y_ref[...], next_gain_ref[...]).astype(BF16)

    if leaving:

        @pl.when(jnp.logical_and(step == 3, meta[2] == 1))
        def _():
            out_ref[...] = y_ref[...].astype(BF16)


def feed_rows(place, x, gain, next_gain, pieces, first=None):
    rows = x.shape[0] // 2
    leaving = first is None

    def block(place):
        return 1 - place[2] if leaving else place[2]

    fixed = pl.BlockSpec((rows, D), lambda q, place: (block(place), 0))
    moving = pl.BlockSpec((rows, D), lambda q, place: (block(place), q))
    narrow = pl.BlockSpec((1, D), lambda q, place: (0, 0))
    hidden = jax.ShapeDtypeStruct((2 * rows, 4 * D), BF16)
    return pl.pallas_call(
        functools.partial(feed_rows_kernel, leaving),
        grid_spec=pltpu.PrefetchScalarGridSpec(
            num_scalar_prefetch=1,
            grid=(4,),
            in_specs=[fixed, narrow, narrow] + [ANYWHERE] * (10 if leaving else 14),
            out_specs=[fixed, fixed, moving, moving]
            + [pl.BlockSpec((rows, D), lambda q, place: (0, 0))],
            scratch_shapes=[pltpu.VMEM((4, 2, D, D), BF16), pltpu.SemaphoreType.DMA((16,))],
        ),
        out_shape=[
            jax.ShapeDtypeStruct((2 * rows, D), F32),
            jax.ShapeDtypeStruct((2 * rows, D), BF16),
            hidden,
            hidden,
            jax.ShapeDtypeStruct((rows, D), BF16),
        ],
        input_output_aliases={} if leaving else {14 + i: i for i in range(4)},
        compiler_params=pltpu.CompilerParams(vmem_limit_bytes=ROOM),
        cost_estimate=cost(rows, 3.6, 16),
        name="feed_rows",
    )(place, x, gain, next_gain, *pieces, *([] if leaving else first))


def feed_back_kernel(n_pieces, meta, e_ref, x_ref, gain_ref, slope_ref, b_ref, h_ref, *refs):
    pieces, refs = refs[:n_pieces], refs[n_pieces:]
    dx_ref, dgain_ref, eb_ref, eu_ref, sent_ref, room, sems = refs
    step = pl.program_id(0)
    fetch_quarter(step, feed_copies(pieces, meta, room, sems))
    chunks = chunks_of(x_ref.shape[0])

    @pl.when(step == 0)
    def _():
        for rows in chunks:
            eb_ref[rows, :] = e_ref[rows, :].astype(BF16)
            dx_ref[rows, :] = jnp.zeros_like(dx_ref[rows, :])

    slope = slope_ref[...].astype(F32)
    eu_ref[...] = (rows_nt(eb_ref[...], room[step, 1]) * slope).astype(BF16)
    dx_ref[...] += rows_nt(eu_ref[...], room[step, 0])

    @pl.when(step % 2 == 1)
    def _():
        for kind, (left, right) in enumerate(((b_ref, eu_ref), (h_ref, eb_ref))):
            delta = rows_tn(left[...], right[...])
            for p in range(PARTS):
                rows = pl.ds(pl.multiple_of((meta[0] ^ p) * PIECE, PIECE), PIECE)
                sent_ref[0, kind, rows, :] = delta[p * PIECE : (p + 1) * PIECE].astype(BF16)

    @pl.when(step == 3)
    def _():
        gain_total = jnp.zeros((1, D), F32)
        for rows in chunks:
            part, gain_part = norm_back(x_ref[rows, :], gain_ref[...], dx_ref[rows, :])
            dx_ref[rows, :] = e_ref[rows, :].astype(F32) + part
            gain_total = gain_total + gain_part
        dgain_ref[...] = gain_total


def feed_back(meta, delta, x, gain, slope, pieces, b, h):
    rows = x.shape[0]
    fixed = pl.BlockSpec((rows, D), lambda q: (0, 0))
    moving = pl.BlockSpec((rows, D), lambda q: (0, q))
    narrow = pl.BlockSpec((1, D), lambda q: (0, 0))
    hidden = pl.BlockSpec((rows, D), lambda q: (0, 2 * (q // 2) + 1))
    return pl.pallas_call(
        functools.partial(feed_back_kernel, len(pieces)),
        grid=(4,),
        in_specs=[SCALARS, fixed, fixed, narrow, moving, fixed, hidden]
        + [ANYWHERE] * len(pieces),
        out_specs=[fixed, narrow, fixed, moving]
        + [pl.BlockSpec((1, 2, D, D), lambda q: (q // 2, 0, 0, 0))],
        out_shape=[
            jax.ShapeDtypeStruct((rows, D), F32),
            jax.ShapeDtypeStruct((1, D), F32),
            jax.ShapeDtypeStruct((rows, D), BF16),
            jax.ShapeDtypeStruct((rows, 4 * D), BF16),
            jax.ShapeDtypeStruct((2, 2, D, D), BF16),
        ],
        scratch_shapes=[pltpu.VMEM((4, 2, D, D), BF16), pltpu.SemaphoreType.DMA((16,))],
        compiler_params=pltpu.CompilerParams(vmem_limit_bytes=ROOM),
        cost_estimate=cost(rows, 5, 19),
        name="feed_back",
    )(meta, delta, x, gain, slope, b, h, *pieces)


def feed_weights_kernel(place, eu_ref, *refs):
    h_refs, (b_ref, eb_ref, out_ref) = refs[:-3], refs[-3:]
    j, kind = pl.program_id(0), pl.program_id(1)

    def put(delta):
        for p in range(PARTS):
            rows = pl.ds(pl.multiple_of((place[0] ^ p) * PIECE, PIECE), PIECE)
            out_ref[0, 0, rows, :] = delta[p * PIECE : (p + 1) * PIECE].astype(BF16)

    @pl.when(kind == 0)
    def _():
        put(rows_tn(b_ref[...], eu_ref[...]))

    for span, h_ref in enumerate(h_refs):

        @pl.when(jnp.logical_and(kind == 1, jnp.logical_or(len(h_refs) == 1, j == span)))
        def _(h_ref=h_ref):
            put(rows_tn(h_ref[...], eb_ref[...]))


def feed_weights(place, eu, h, b, eb, first):
    rows = b.shape[0]
    fixed = pl.BlockSpec((rows, D), lambda j, kind, place: (0, 0))
    moving = pl.BlockSpec((rows, D), lambda j, kind, place: (0, 2 * j + first))
    hidden = [moving]
    if len(h) == 2:
        hidden = [pl.BlockSpec((rows, D), lambda j, kind, place: (0, first))] * 2
    return pl.pallas_call(
        feed_weights_kernel,
        grid_spec=pltpu.PrefetchScalarGridSpec(
            num_scalar_prefetch=1,
            grid=(2, 2),
            in_specs=[moving] + hidden + [fixed, fixed],
            out_specs=pl.BlockSpec((1, 1, D, D), lambda j, kind, place: (j, kind, 0, 0)),
        ),
        out_shape=jax.ShapeDtypeStruct((2, 2, D, D), BF16),
        compiler_params=pltpu.CompilerParams(vmem_limit_bytes=ROOM),
        cost_estimate=cost(rows, 4, 6),
        name="feed_weights",
    )(place, eu, *h, b, eb)


def turn_back_kernel(
    meta, side, encoded, gain, context, returned, radar_part, cotangent, out, gain_out
):
    cut = context.shape[0]

    @pl.when(side[0] == 1)
    def _():
        out[:cut] = returned[...].astype(F32)
        out[cut:] = radar_part[...]
        gain_out[...] = jnp.zeros_like(gain_out)

    @pl.when(side[0] == 0)
    def _():
        total = jnp.zeros_like(gain_out)
        for part, incoming in enumerate((context, returned)):
            rows = slice(part * cut, (part + 1) * cut)
            delta, gain_part = norm_back(encoded[rows], gain[...], incoming[...].astype(F32))
            total = total + gain_part
            out[rows] = delta
        gain_out[...] = total

        def one_image(i, carry):
            rows = pl.ds(pl.multiple_of(i * SLOTS, 8), SLOTS)
            seen = lax.broadcasted_iota(jnp.int32, (SLOTS, 1), 0) < meta[3 + i]
            out[rows] += jnp.where(seen, cotangent[i].astype(F32), 0.0)
            return carry

        lax.fori_loop(0, cotangent.shape[0], one_image, 0)


def turn_back(meta, modality, encoded, gain, context, returned, radar_part, cotangent):
    return pl.pallas_call(
        turn_back_kernel,
        in_specs=[SCALARS] * 2 + [WHOLE] * 6,
        out_specs=[WHOLE] * 2,
        out_shape=[
            jax.ShapeDtypeStruct(encoded.shape, F32),
            jax.ShapeDtypeStruct((1, D), F32),
        ],
        compiler_params=pltpu.CompilerParams(vmem_limit_bytes=ROOM),
        cost_estimate=cost(816, 5, 0),
        name="turn_back",
    )(meta, modality[None], encoded, gain, context, returned, radar_part, cotangent)


def relative_parts(parts, own):
    return jnp.stack(
        [lax.dynamic_index_in_dim(parts, r ^ own, 0, keepdims=False) for r in range(PARTS)]
    )


def pack_mix(triple, out_weight):
    return jnp.concatenate([triple.transpose(1, 2, 0), out_weight[None]], 0)


def piece_of(quarter, part):
    if quarter.shape[1] == PIECE:
        return lax.dynamic_index_in_dim(quarter, part, 0, keepdims=False)
    return lax.dynamic_slice_in_dim(quarter, part * PIECE, PIECE, 1)


def unpack_mix(parts):
    return parts[:3].transpose(2, 0, 1).astype(F32), parts[3].astype(F32)


def unpack_feed_kernel(place, *refs):
    refs, (expand_ref, reduce_ref) = refs[:-2], refs[-2:]
    step = PIECE // 2
    for n in range(len(refs) // 5):

        @pl.when(pl.program_id(0) == n)
        def _(n=n):
            part, low, high, low_far, high_far = refs[5 * n : 5 * n + 5]
            for kind, out in enumerate((expand_ref, reduce_ref)):
                lows = [part[kind, :step], low[kind], low_far[0, kind], low_far[1, kind]]
                highs = [part[kind, step:], high_far[0, kind], high[kind], high_far[1, kind]]
                for p in range(PARTS):
                    start = pl.multiple_of((place[0] ^ p) * PIECE, PIECE)
                    out[0, pl.ds(start, step), :] = lows[p].astype(F32)
                    out[0, pl.ds(start + step, step), :] = highs[p].astype(F32)


def unpack_feed(place, *gathered):
    count = len(gathered)
    operands = [piece for pieces in gathered for piece in pieces]
    if count == 1:
        out = pl.BlockSpec((1, D, D), lambda n, place: (n, 0, 0))
    else:
        out = pl.BlockSpec((1, D, D), lambda n, place: (n ^ place[2], 0, 0))
    shape = jax.ShapeDtypeStruct((count, D, D), F32)
    return pl.pallas_call(
        unpack_feed_kernel,
        grid_spec=pltpu.PrefetchScalarGridSpec(
            num_scalar_prefetch=1,
            grid=(count,),
            in_specs=[WHOLE] * len(operands),
            out_specs=[out, out],
        ),
        out_shape=[shape, shape],
        compiler_params=pltpu.CompilerParams(vmem_limit_bytes=ROOM),
        cost_estimate=cost(816, 1, 2 * count),
        name="unpack_feed",
    )(place, *operands)


def fetch_relayed(zero, three):
    return (zero, swap(zero, dp_mask=1), swap(zero, dp_mask=2), three)


def fetch_beside(pieces):
    return pieces + tuple(swap(piece, head_mask=CORE) for piece in pieces)


AXES = {"x": (0, 0, ACROSS), "y": (3, 1, 0), "z": (2, 2, 0)}
THIRDS = ("xyz", "yzx", "zxy")
HALVES = ("xyz", "yxz")
LAST = ("xyz", "yxz")
CROSS = ("yxz", "xzy")


def halves(array, axis):
    return lax.slice_in_dim(array, 0, 1, axis=axis), lax.slice_in_dim(array, 1, 2, axis=axis)


def add_split(keep, beside, orders=THIRDS):
    kinds, rows = keep.shape[1:3]
    kinds, rows = (1, rows) if kinds == PARTS else (kinds, rows // PARTS)
    total = (keep + beside).reshape(2, kinds, 2, 2, rows, D)
    step = PIECE // len(orders)
    cuts = [i * step for i in range(len(orders))] + [rows]
    return [total[:, :, :, :, low:high] for low, high in zip(cuts[:-1], cuts[1:])]


def link_send(shares, stage, orders=THIRDS):
    out = []
    for array, order in zip(shares, orders, strict=True):
        axis, dp_mask, head_mask = AXES[order[stage]]
        keep, sent = halves(array, axis)
        out.append((keep, swap(sent, dp_mask, head_mask)))
    return out


def link_first(keep, beside, orders=THIRDS):
    shape = (2, -1, 2, 2, PIECE, D)
    step = PIECE // len(orders)

    def split(keep, beside):
        out = []
        for i, order in enumerate(orders):
            rows = slice(i * step, (i + 1) * step)
            share = keep[:, :, :, :, rows] + beside[:, :, :, :, rows]
            out.append(halves(share, AXES[order[0]][0]))
        return out

    return glue(split, keep.reshape(shape), beside.reshape(shape))


def link_swap(parts, stage, orders=THIRDS):
    return [
        (keep, swap(sent, *AXES[order[stage]][1:]))
        for (keep, sent), order in zip(parts, orders, strict=True)
    ]


def link_next(pairs, stage, orders=THIRDS):
    def split(pairs):
        return [
            halves(keep + received, AXES[order[stage]][0])
            for (keep, received), order in zip(pairs, orders, strict=True)
        ]

    return link_swap(glue(split, pairs), stage, orders)


def link_add(pairs):
    return [keep + received for keep, received in pairs]


def join(shares):
    return jnp.concatenate([share[0, :, 0, 0] for share in shares], 1)


def rest_send(array, stop):
    mask = PARTS
    while 2 * mask < stop:
        array = array + swap(array, dp_mask=mask)
        mask *= 2
    return array, swap(array, dp_mask=mask)


def rest_add(pair):
    return pair[0] + pair[1]


def over_rest(array, stop):
    mask = PARTS
    while mask < stop:
        array = array + swap(array, dp_mask=mask)
        mask *= 2
    return array


def gather_first(part):
    step = PIECE // 2
    return part, swap(part[:, :step], dp_mask=1), swap(part[:, step:PIECE], dp_mask=2)


def gather_second(first):
    part, low, high = first
    step = PIECE // 2
    return (
        part,
        low,
        high,
        swap(jnp.stack([part[:, :step], low]), dp_mask=2),
        swap(jnp.stack([part[:, step:PIECE], high]), dp_mask=1),
    )


def gather_join(pieces):
    part, low, high, low_far, high_far = pieces
    step = PIECE // 2
    lows = [part[:, :step], low, low_far[0], low_far[1]]
    highs = [part[:, step:PIECE], high_far[0], high, high_far[1]]
    return jnp.stack([jnp.concatenate(pair, 1) for pair in zip(lows, highs, strict=True)])


def on_device(
    tokens,
    cotangent,
    ratios,
    patch_index,
    encoder_gains,
    encoder_attend_in,
    encoder_attend_out,
    encoder_expand,
    encoder_reduce,
    uniting_gains,
    uniting_query,
    uniting_pair,
    uniting_attend_out,
    uniting_expand,
    uniting_reduce,
):
    groups = lax.axis_size("dp")
    side = groups // 2
    group, lane = lax.axis_index("dp"), lax.axis_index("head")
    radar = group >= side
    modality = radar.astype(jnp.int32)
    own = group % PARTS
    images = tokens.shape[0]
    some = images // 2
    cut = some * SLOTS

    def select_slot(stacked):
        return lax.dynamic_index_in_dim(stacked, modality, 0, keepdims=False)

    gains = select_slot(encoder_gains)[:, None]
    uni_gains = uniting_gains[:, None]

    own_ratios = lax.dynamic_slice_in_dim(ratios, lane * images, images, 0)
    patches = lax.dynamic_slice_in_dim(patch_index, lane * images, images, 0)
    counts = PATCHES * (100 - own_ratios) // 100
    first = modality * some
    meta = jnp.concatenate([jnp.stack([own, lane, 0 * first]), counts])
    pair_meta = jnp.concatenate([jnp.stack([own, lane, first]), counts])
    place = jnp.stack([own, lane, modality])
    visible = (jnp.arange(SLOTS)[None, :] < counts[:, None])[:, :, None]
    queries = patches[:, None, :]
    row_gap = (patches // GRID)[:, :, None] - queries // GRID
    col_gap = (patches % GRID)[:, :, None] - queries % GRID
    distance = jnp.sqrt((row_gap * row_gap + col_gap * col_gap).astype(F32))
    per_lane = HEADS // lax.axis_size("head")
    heads = jnp.concatenate(
        [(lane ^ mask) * per_lane + jnp.arange(per_lane) for mask in range(4)]
    )
    slopes = 2.0 ** (-8.0 * (heads.astype(F32) + 1.0) / HEADS)

    mix_quarter = pack_mix(select_slot(encoder_attend_in), select_slot(encoder_attend_out))
    mix_zero = swap(piece_of(mix_quarter, own), head_mask=ACROSS)
    mix_near = (mix_quarter, swap(mix_quarter, head_mask=CORE))
    mix_quarter, encoder_expand, encoder_reduce = tie(
        mix_quarter, encoder_expand, encoder_reduce
    )
    feed_quarter = jnp.stack([select_slot(encoder_expand), select_slot(encoder_reduce)])
    feed_quarter, mix_quarter, mix_zero, flat, uni_feed_quarter, meta, slopes, distance = tie(
        feed_quarter,
        mix_quarter,
        mix_zero,
        tokens.reshape(-1, D),
        jnp.stack([uniting_expand, uniting_reduce]),
        meta,
        slopes,
        distance,
    )
    mix_pieces = fetch_relayed(
        mix_zero, swap(piece_of(mix_quarter, own ^ 3), head_mask=ACROSS)
    )
    feed_zero = swap(piece_of(feed_quarter, own), head_mask=ACROSS)
    feed_near = (feed_quarter, swap(feed_quarter, head_mask=CORE))

    normed_one, middle, *near = mix_forward(
        meta, slopes, flat, None, gains[0], None, mix_near, distance
    )
    middle, mix_pieces, feed_zero, feed_near = tie(middle, mix_pieces, feed_zero, feed_near)
    feed_quarter = feed_near[0]
    mix_far = fetch_beside(mix_pieces)
    feed_pieces = fetch_relayed(
        feed_zero, swap(piece_of(feed_quarter, own ^ 3), head_mask=ACROSS)
    )
    feed_zero, uniting_query, uniting_pair, uniting_attend_out = tie(
        feed_zero, uniting_query, uniting_pair, uniting_attend_out
    )
    uni_quarter = pack_mix(
        jnp.concatenate([uniting_query[:, None], uniting_pair], 1), uniting_attend_out
    )
    middle, mix_far, uni_feed_quarter = tie(middle, mix_far, uni_feed_quarter)
    uni_feed = (lax.all_gather(uni_feed_quarter, "head"),)
    middle, *far = mix_forward(
        meta, slopes, middle, None, None, normed_one, mix_far, distance, HEADS // 2
    )
    qkv, mixed, lse = zip(near, far)
    middle, feed_pieces, uni_quarter = tie(middle, feed_pieces, uni_quarter)
    feed_far = fetch_beside(feed_pieces)
    uni_zero = swap(piece_of(uni_quarter, own), head_mask=ACROSS)
    uni_three = swap(piece_of(uni_quarter, own ^ 3), head_mask=ACROSS)
    enc_mix, enc_feed = mix_near + mix_far, feed_near + feed_far

    *half_fed, leaving = feed_rows(place, middle, gains[1], uni_gains[0], enc_feed)
    leaving, half_fed, uni_zero = tie(leaving, half_fed, uni_zero)
    received = swap(leaving, dp_mask=side)
    uni_mix_pieces = fetch_relayed(uni_zero, uni_three)
    uni_mix_near = (uni_quarter, swap(uni_quarter, head_mask=CORE))
    encoded, normed_two, *stored, context = feed_rows(
        place, middle, gains[1], uni_gains[0], enc_feed, half_fed
    )
    hidden, bend = ([part] for part in stored)
    encoded, received, uni_mix_pieces = tie(encoded, received, uni_mix_pieces)
    uni_mix = uni_mix_near + fetch_beside(uni_mix_pieces)
    received, cotangent = tie(received, cotangent)
    sent_cotangent = swap(cotangent[:some], dp_mask=side)
    radar_rows = jnp.where(radar, encoded[cut:], received.astype(F32))
    context_rows = jnp.where(radar, received, context)

    uni_normed, uni_middle, *stored = mix_forward(
        pair_meta, slopes, radar_rows, context_rows, uni_gains[1], None, uni_mix, distance
    )
    uni_qkv, uni_mixed, uni_lse = ([part] for part in stored)
    uni_normed_two, joined, *stored = feed_forward(
        meta, uni_middle, uni_gains[2], None, uni_feed
    )
    uni_hidden, uni_bend = ([part] for part in stored)

    joined, sent_cotangent = tie(joined, sent_cotangent)
    joined_half = joined.reshape(some, SLOTS, D)
    other_half = [swap(joined_half[i : i + 1], dp_mask=side) for i in range(some)]
    pair_cotangent = jnp.where(radar, cotangent[some:], sent_cotangent)
    pair_visible = lax.dynamic_slice_in_dim(visible, first, some, 0)
    delta_joined = jnp.where(pair_visible, pair_cotangent, 0).reshape(-1, D)
    delta_middle, gain_three, eb, eu, sent = feed_back(
        meta,
        delta_joined,
        uni_middle,
        uni_gains[2],
        uni_bend[0],
        uni_feed,
        uni_normed_two,
        uni_hidden[0],
    )
    sent, eu, other_half[:2] = tie(sent, eu, other_half[:2])
    beside = swap(sent, head_mask=CORE)
    keep = feed_weights(place, eu, uni_hidden, uni_normed_two, eb, 0)
    keep, beside, other_half[2:] = tie(keep, beside, other_half[2:])
    uni_feed_parts, delta_middle = tie(link_first(keep, beside), delta_middle)
    uni_feed_pairs = link_swap(uni_feed_parts, 0)
    delta_radar, gain_two, dqkv, mix_eb, delta_context, leaving = mix_back(
        pair_meta,
        slopes,
        delta_middle,
        radar_rows,
        uni_gains[1],
        uni_qkv,
        uni_lse,
        uni_mix,
        distance,
        True,
    )
    leaving, dqkv, uni_feed_pairs = tie(leaving, dqkv, uni_feed_pairs)
    other_half = jnp.concatenate(other_half, 0)
    returned = swap(leaving, dp_mask=side)
    uni_feed_pairs = link_next(uni_feed_pairs, 1)
    keep, sent = mix_weights(place, dqkv, uni_mixed, uni_normed, context_rows, mix_eb)
    layer_output = jnp.where(
        visible,
        jnp.where(
            radar,
            jnp.concatenate([other_half, joined_half], 0),
            encoded.astype(BF16).reshape(images, SLOTS, D),
        ),
        0,
    )
    sent, returned, uni_feed_pairs, layer_output = tie(
        sent, returned, uni_feed_pairs, layer_output
    )
    beside = swap(sent, head_mask=CORE)
    uni_feed_pairs = link_send(link_add(uni_feed_pairs), 2)
    delta_encoded, gain_one = turn_back(
        meta, modality, encoded, uni_gains[0], delta_context, returned, delta_radar, cotangent
    )
    delta_encoded, beside, uni_feed_pairs = tie(delta_encoded, beside, uni_feed_pairs)
    uni_mix_sum, uni_feed_part = add_split(keep, beside, CROSS), join(link_add(uni_feed_pairs))
    delta_encoded, uni_mix_sum, uni_feed_part = tie(delta_encoded, uni_mix_sum, uni_feed_part)
    uni_feed_rest = rest_send(uni_feed_part, groups)
    uni_mix_pairs = link_send(uni_mix_sum, 0, CROSS)

    delta_middle, gain_b, eb, eu, sent = feed_back(
        meta, delta_encoded, middle, gains[1], bend[0], enc_feed, normed_two, hidden[0]
    )
    sent, eu, uni_feed_rest, uni_mix_pairs = tie(sent, eu, uni_feed_rest, uni_mix_pairs)
    uni_feed_part, uni_mix_sum = rest_add(uni_feed_rest), link_add(uni_mix_pairs)
    eu, uni_feed_part, uni_mix_sum = tie(eu, uni_feed_part, uni_mix_sum)
    beside = swap(sent, head_mask=CORE)
    uni_feed_near = swap(uni_feed_part, dp_mask=1)
    uni_mix_pairs = link_send(uni_mix_sum, 1, CROSS)
    keep = feed_weights(place, eu, hidden, normed_two, eb, 0)
    keep, beside, uni_feed_near, uni_mix_pairs = tie(keep, beside, uni_feed_near, uni_mix_pairs)
    uni_feed_near = jnp.stack([uni_feed_part, uni_feed_near])
    enc_feed_sum, uni_mix_sum = add_split(keep, beside, HALVES), link_add(uni_mix_pairs)
    delta_middle, enc_feed_sum, uni_mix_sum, uni_feed_near = tie(
        delta_middle, enc_feed_sum, uni_mix_sum, uni_feed_near
    )
    enc_feed_pairs = link_send(enc_feed_sum, 0, HALVES)
    uni_mix_pairs = link_send(uni_mix_sum, 2, CROSS)
    uni_feed_far = swap(uni_feed_near, dp_mask=2)
    delta_inputs, gain_a, dqkv, eb = mix_back(
        meta, slopes, delta_middle, flat, gains[0], qkv, lse, enc_mix, distance, False
    )
    dqkv, enc_feed_pairs, uni_mix_pairs, uni_feed_far = tie(
        dqkv, enc_feed_pairs, uni_mix_pairs, uni_feed_far
    )
    enc_feed_sum, uni_mix_part = link_add(enc_feed_pairs), join(link_add(uni_mix_pairs))
    dqkv, enc_feed_sum, uni_mix_part = tie(dqkv, enc_feed_sum, uni_mix_part)
    enc_feed_pairs = link_send(enc_feed_sum, 1, HALVES)
    uni_mix_rest = rest_send(uni_mix_part, groups)

    totals = (gain_a, gain_b, gain_one, gain_two, gain_three)
    keep, sent = mix_weights(place, dqkv, mixed, normed_one, normed_one, eb, totals)
    sent, enc_feed_pairs, uni_mix_rest = tie(sent, enc_feed_pairs, uni_mix_rest)
    uni_mix_gather = gather_first(rest_add(uni_mix_rest))
    beside = swap(sent, head_mask=CORE)
    enc_feed_pairs = link_send(link_add(enc_feed_pairs), 2, HALVES)
    enc_mix_pairs = link_send(add_split(keep, beside, LAST), 0, LAST)
    feed_part = over_rest(join(link_add(enc_feed_pairs)), side)
    feed_other = swap(feed_part, dp_mask=side)
    enc_mix_pairs, feed_part, uni_mix_gather = tie(enc_mix_pairs, feed_part, uni_mix_gather)
    enc_mix_pairs = link_send(link_add(enc_mix_pairs), 1, LAST)
    feed_gather = gather_first(feed_part)
    enc_mix_pairs = link_send(link_add(enc_mix_pairs), 2, LAST)
    enc_mix_pairs, feed_gather = tie(enc_mix_pairs, feed_gather)
    feed_gather = gather_second(feed_gather)
    enc_mix_pairs, feed_other = tie(enc_mix_pairs, feed_other)
    mix_part = over_rest(join(link_add(enc_mix_pairs)), side)
    mix_part, feed_other = tie(mix_part, feed_other)
    mix_other = swap(mix_part, dp_mask=side)
    feed_other_gather = gather_first(feed_other)
    feed_gather, uni_feed_near = tie(feed_gather, uni_feed_near)
    uni_feed_all = relative_parts(jnp.concatenate([uni_feed_near, uni_feed_far], 0), own)
    fexpand, freduce = (uni_feed_all[:, i].reshape(D, D).astype(F32) for i in range(2))
    mix_other, feed_other_gather, feed_gather, uni_mix_gather, fexpand, freduce = tie(
        mix_other, feed_other_gather, feed_gather, uni_mix_gather, fexpand, freduce
    )
    mix_gather = gather_first(jnp.concatenate([mix_part, mix_other], 0))
    feed_other_gather = gather_second(feed_other_gather)
    mix_gather, uni_mix_gather = tie(mix_gather, uni_mix_gather)
    mix_gather, uni_mix_gather = gather_second(mix_gather), gather_second(uni_mix_gather)
    totals = (mix_part + mix_other)[0, PIECE:].astype(F32)

    ftriple, fout = unpack_mix(relative_parts(gather_join(uni_mix_gather)[:, 0], own))
    expands, reduces = unpack_feed(place, feed_gather, feed_other_gather)
    mix_all = gather_join(mix_gather)
    mine, theirs = mix_all[:, 0], mix_all[:, 1]
    mixes = [
        unpack_mix(relative_parts(part, own))
        for part in (jnp.where(radar, theirs, mine), jnp.where(radar, mine, theirs))
    ]

    return (
        layer_output,
        delta_inputs.reshape(images, SLOTS, D),
        totals[:4].reshape(2, 2, D),
        jnp.stack([mixes[0][0], mixes[1][0]]),
        jnp.stack([mixes[0][1], mixes[1][1]]),
        expands,
        reduces,
        totals[4:7],
        ftriple[:, 0],
        ftriple[:, 1:],
        fout,
        fexpand,
        freduce,
    )


def solution(mesh):
    return jax.shard_map(
        on_device,
        mesh=mesh,
        in_specs=(
            P(("dp", "head"), None, None),
            P(("dp", "head"), None, None),
            P("dp"),
            P("dp", None),
            P(),
            P(None, None, None, "head"),
            P(None, "head", None),
            P(None, None, "head"),
            P(None, "head", None),
            P(),
            P(None, "head"),
            P(None, None, "head"),
            P("head", None),
            P(None, "head"),
            P("head", None),
        ),
        out_specs=(
            P(("dp", "head"), None, None),
            P(("dp", "head"), None, None),
            P(),
            P(None, None, None, "head"),
            P(None, "head", None),
            P(None, None, "head"),
            P(None, "head", None),
            P(),
            P(None, "head"),
            P(None, None, "head"),
            P("head", None),
            P(None, "head"),
            P("head", None),
        ),
        check_vma=False,
    )
```
